128 devices in a mesh: ctx: 16 (over x, y), exp: 8 (over z, core).
Axes of the slice: x: 4, y: 4, z: 4, core: 2. Of those that a mesh axis runs over, the one named last changes fastest.
Arguments:
- mixer_in: bfloat16 [2048, 16384], P('ctx', 'exp'), may hold values from -6 to 6
- gate_in: bfloat16 [2048, 16384], P('ctx', 'exp'), may hold values from -6 to 6
- delta_in: bfloat16 [2048, 16384], P('ctx', 'exp'), may hold values from -3 to 3
- b_proj: float32 [16, 2048], P(None, 'ctx'), may hold values from -0.6 to 0.6
- c_proj: float32 [16, 2048], P(None, 'ctx'), may hold values from -1.8 to 1.8
- conv_kernel: float32 [4, 16384], P(None, 'exp'), may hold values from -3 to 3
- conv_bias: float32 [16384], P('exp'), may hold values from -0.5 to 0.5
- delta_bias: float32 [16384], P('exp'), may hold values from -1 to 0
- decay_log: float32 [16, 16384], P(None, 'exp'), may hold values from -12 to -2
- skip_gain: float32 [16384], P('exp'), may hold values from 0.5 to 1.5
- prefix_state: float32 [16, 16384], P(None, 'exp'), may hold values from -6 to 6
- prefix_tail: bfloat16 [3, 16384], P(None, 'exp'), may hold values from -6 to 6
- out_proj: bfloat16 [16384, 8192], P('exp', 'ctx'), may hold values from -0.046875 to 0.046875
- residual: bfloat16 [2048, 8192], P('exp', 'ctx'), may hold values from -40 to 40
- norm_gain: float32 [8192], P('ctx'), may hold values from 0.1 to 1.9
- expert_gate: bfloat16 [8, 8192, 6144], P('exp', None, 'ctx'), may hold values from -0.0625 to 0.0625
- expert_up: bfloat16 [8, 8192, 6144], P('exp', None, 'ctx'), may hold values from -0.0625 to 0.0625
- expert_down: bfloat16 [8, 6144, 8192], P('exp', 'ctx'), may hold values from -0.109375 to 0.109375
- expert_ids: int32 [2048, 2], P('exp'), may hold values from 0 to 7, all different within a row; in each aligned block of 256 rows (0 to 255, 256 to 511, ...) at most 96 rows name the same one
- route_gates: float32 [2048, 2], P('exp'), may hold values from 0.2 to 1
Outputs:
- mixer_out: bfloat16 [2048, 8192], P('exp', 'ctx')
- block_out: bfloat16 [2048, 8192], P('exp', 'ctx')
The draws below stay inside these ranges and needn't reach their ends.
Inputs may be any that keep to these rules, and one draw needn't show every extreme that they name: `expert_ids`: each row names 2 different experts. Within each aligned block of 256 rows (the rows of one index of exp) no expert is named more than 96 times, and in every draw some expert is named exactly 96 times in some block.
All inputs are finite; a program needn't handle non-finite values.
Results may differ from the reference program's by a relative error of at most 0.015.
Values may be sent and summed in bfloat16 or wider, within the bound.
A program may use at most 128 MiB of HBM per device.

```python
import math
import jax
import jax.numpy as jnp
import numpy as np
from jax import lax

D = 8192
DI = 16384
NS = 16
KC = 4
TOP = 2
FF_DEV = 384
SEQ_LEN = 2048
BLOCK = 256
EXPERTS = 8
CAP = 96
FF_WIN = 6144
N_CTX = 16
N_EXP = 8


def draw_decay_log(key, part):
    key = jax.random.fold_in(key, 11)
    subkeys = jax.random.split(key, 3)
    slow_share = 0.5
    slow_mask = jax.random.uniform(subkeys[0], (NS, DI), jnp.float32) < slow_share
    slow_log = jnp.log(jax.random.uniform(subkeys[1], (NS, DI), jnp.float32, 0.3, 1.5) / SEQ_LEN)
    fast_log = jnp.log(jax.random.uniform(subkeys[2], (NS, DI), jnp.float32, 0.025, 0.05))
    return jnp.where(slow_mask, slow_log, fast_log).astype(jnp.float32)


def draw_residual(key, part):
    key = jax.random.fold_in(key, 12)
    subkeys = jax.random.split(key, 2)
    row_scale = jnp.exp(jax.random.uniform(subkeys[0], (SEQ_LEN, 1), jnp.float32, jnp.log(0.3), jnp.log(3.0)))
    column_scale = 0.3 * jnp.power(10.0, jnp.arange(D, dtype=jnp.float32) / D)[None, :]
    base_value = jnp.clip(jax.random.normal(subkeys[1], (SEQ_LEN, D), jnp.float32), -4.0, 4.0)
    return (base_value * row_scale * column_scale).astype(jnp.bfloat16)


def strengthened(drawn, key, source, target, parts, factor):
    owner, partner = [(jnp.arange(drawn.shape[position]) // (drawn.shape[position] // parts)).reshape([-1 if axis == position else 1 for axis in range(drawn.ndim)]) for position in (source, target)]
    chosen = jax.random.permutation(key, parts)[partner]
    strong = (owner == chosen) | (owner == (partner + parts // 2) % parts)
    return jnp.where(strong, factor * drawn, drawn)


def shard_levels(own_key, dims, cuts, low, high):
    factor_of = 1.0
    for dim, parts in cuts:
        draws = jax.random.uniform(jax.random.fold_in(jax.random.fold_in(own_key, 6), dim), (parts,), jnp.float32, low / len(cuts), high / len(cuts))
        factor_of = factor_of * jnp.repeat(jnp.exp(draws), dims[dim] // parts).reshape((-1,) + (1,) * (len(dims) - 1 - dim))
    return factor_of


def assign_block(key, own, number, rows, count, top, reach, lean):
    sequence = jax.random.permutation(key, count)
    heavy_load, usual = load_shares(count, rows * top, reach, lean, True), load_shares(count, rows * top, reach, lean, False)
    places = jnp.arange(count)

    def named(tallies, turn):
        used = int((tallies > 0).sum())
        fixed = max(1, used // 4)
        passed = fixed + (places - fixed + turn * (used - fixed)) % max(1, count - fixed)
        return jnp.zeros((count,), jnp.int32).at[sequence[jnp.where(places < fixed, places, passed)]].set(jnp.asarray(tallies, jnp.int32))

    tallies = jnp.where(number % 4 == 0, named(heavy_load, number // 4), named(usual, number - number // 4 - 1))
    mixed = jax.random.permutation(jax.random.fold_in(own, 3), count)
    source_of, sink = mixed[0:count // 2 * 2:2], mixed[1:count // 2 * 2:2]
    slack = jnp.minimum(tallies[source_of] - 1, reach - tallies[sink]) // 2
    slack = jnp.where((source_of == sequence[0]) | (sink == sequence[0]) | (tallies[sink] == 0), 0, jnp.maximum(slack, 0))
    passed = jax.random.randint(jax.random.fold_in(own, 4), (count // 2,), 0, 1 << 20) % (slack + 1)
    tallies = tallies.at[source_of].add(-passed).at[sink].add(passed)
    members = jnp.searchsorted(jnp.cumsum(tallies), jnp.arange(rows * top), side="right").astype(jnp.int32)
    table = members.reshape(top, rows).T
    table = table[jax.random.permutation(jax.random.fold_in(own, 1), rows)]
    turn = jax.random.randint(jax.random.fold_in(own, 2), (rows, 1), 0, top)
    return jnp.take_along_axis(table, (jnp.arange(top)[None, :] + turn) % top, axis=1)


def load_shares(amount, total, bound, slope, full):
    loads = [(1 << 20) // math.isqrt(grade ** slope) + 1 for grade in range(1, amount + 1)]
    largest = bound if full else min(bound, max(-(-total // amount), total * loads[0] // sum(loads)))
    least = 1 if total - largest >= amount - 1 else 0
    holding, rest = [largest] + [least] * (amount - 1), total - largest - least * (amount - 1)
    while rest > 0:
        candidates = [i for i in range(1, amount) if holding[i] < largest] or [i for i in range(1, amount) if holding[i] < bound]
        pool, left = sum([loads[i] for i in candidates]), rest
        for i in candidates:
            extra = min(bound - holding[i], max(1, left * loads[i] // pool), rest)
            holding[i] = holding[i] + extra
            rest = rest - extra
    return np.array(holding)


def gaussian(key, shape, scale, reach, shards=(), held_as=jnp.bfloat16):
    loudness = shard_levels(key, shape, shards, -0.22, 0.18) if shards else 1.0
    drawn = jax.random.normal(key, shape, jnp.float32) * scale * loudness
    return jnp.minimum(jnp.maximum(drawn, -reach), reach).astype(held_as)


def bell_draw_with(own_key, extent, width, reach, cuts, heavy, kind=jnp.bfloat16):
    values = width * jax.random.normal(own_key, extent, jnp.float32)
    if cuts:
        values = values * shard_levels(own_key, extent, cuts, -0.22, 0.18)
    return jnp.clip(strengthened(values, jax.random.fold_in(own_key, 3), *heavy), -reach, reach).astype(kind)


def setup_inputs(seed: int = 0) -> dict:
    key_list = jax.random.split(jax.random.key(seed), 21)
    mixer_in = gaussian(key_list[0], (SEQ_LEN, DI), 1.0, 6.0, ((0, 16), (1, 8)))
    gate_in = gaussian(key_list[1], (SEQ_LEN, DI), 1.0, 6.0, ((0, 16), (1, 8)))
    delta_in = gaussian(key_list[2], (SEQ_LEN, DI), 0.5, 3.0, ((0, 16), (1, 8)))
    b_proj = gaussian(key_list[3], (NS, SEQ_LEN), 0.1, 0.6, ((1, 16),), jnp.float32)
    c_proj = gaussian(key_list[4], (NS, SEQ_LEN), 0.3, 1.8, ((1, 16),), jnp.float32)
    conv_kernel = gaussian(key_list[5], (KC, DI), KC ** -0.5, 3.0, ((1, 8),), jnp.float32)
    conv_bias = jnp.clip(jax.random.uniform(key_list[6], (DI,), jnp.float32, -0.5, 0.5) * shard_levels(key_list[6], (DI,), ((0, 8),), -0.4, 0.0), -0.5, 0.5)
    delta_bias = jnp.clip(-1.0 + 1.0 * jax.random.uniform(key_list[7], (DI,), jnp.float32) ** shard_levels(key_list[7], (DI,), ((0, 8),), -0.2, 0.2), -1.0, 0.0)
    decay_log = draw_decay_log(jax.random.fold_in(key_list[20], 71), 0)
    skip_gain = jnp.clip(0.5 + 1.0 * jax.random.uniform(key_list[9], (DI,), jnp.float32) ** shard_levels(key_list[9], (DI,), ((0, 8),), -0.2, 0.2), 0.5, 1.5)
    prefix_state = gaussian(key_list[10], (NS, DI), 1.0, 6.0, ((1, 8),), jnp.float32)
    prefix_tail = gaussian(key_list[11], (KC - 1, DI), 1.0, 6.0, ((1, 8),))
    out_proj = gaussian(key_list[12], (DI, D), DI ** -0.5, 0.046875, ((0, 8), (1, 16)))
    residual = draw_residual(jax.random.fold_in(key_list[20], 71), 0)
    norm_gain = jnp.clip(1.0 + 0.18 * jax.random.normal(key_list[14], (D,), jnp.float32), 0.1, 1.9)
    expert_gate = gaussian(key_list[15], (EXPERTS, D, FF_WIN), D ** -0.5, 0.0625, ((0, 8), (2, 16)))
    expert_up = gaussian(key_list[16], (EXPERTS, D, FF_WIN), D ** -0.5, 0.0625, ((0, 8), (2, 16)))
    expert_down = bell_draw_with(key_list[17], (EXPERTS, FF_WIN, D), FF_WIN ** -0.5, 0.109375, ((0, 8), (1, 16)), (1, 2, 16, 2.0))
    expert_ids_keys = jax.random.split(jax.random.fold_in(key_list[18], 1), SEQ_LEN // BLOCK)
    expert_ids_turns = jax.random.permutation(jax.random.fold_in(key_list[18], 3), SEQ_LEN // BLOCK)
    expert_ids = jax.vmap(lambda own, number: assign_block(jax.random.fold_in(key_list[18], 2), own, number, BLOCK, EXPERTS, TOP, CAP, 2))(expert_ids_keys, expert_ids_turns).reshape((SEQ_LEN, TOP))
    route_gates = jnp.clip(0.2 + 0.8 * jax.random.uniform(key_list[19], (SEQ_LEN, TOP), jnp.float32) ** shard_levels(key_list[19], (SEQ_LEN, TOP), ((0, 8),), -0.2, 0.2), 0.2, 1.0)
    return {"mixer_in": mixer_in, "gate_in": gate_in, "delta_in": delta_in, "b_proj": b_proj, "c_proj": c_proj, "conv_kernel": conv_kernel, "conv_bias": conv_bias, "delta_bias": delta_bias, "decay_log": decay_log, "skip_gain": skip_gain, "prefix_state": prefix_state, "prefix_tail": prefix_tail, "out_proj": out_proj, "residual": residual, "norm_gain": norm_gain, "expert_gate": expert_gate, "expert_up": expert_up, "expert_down": expert_down, "expert_ids": expert_ids, "route_gates": route_gates}


def mixer_layer(mixer_in, gate_in, delta_in, b_proj, c_proj, conv_kernel, conv_bias, delta_bias, decay_log, skip_gain, prefix_state, prefix_tail, out_proj, residual):
    padded = jnp.concatenate([prefix_tail, mixer_in], axis=0).astype(jnp.float32)
    convolved = conv_bias[None, :] + sum((conv_kernel[tap_index][None, :] * padded[tap_index:tap_index + SEQ_LEN] for tap_index in range(KC)))
    conv_act = jax.nn.silu(convolved)
    step_size = jax.nn.softplus(delta_in.astype(jnp.float32) + delta_bias[None, :])
    decay_rate = -jnp.exp(decay_log)
    driving = step_size * conv_act

    def advance(carry_state, inputs):
        step_row, drive_row, b_column, c_column = inputs
        carry_state = jnp.exp(step_row[None, :] * decay_rate) * carry_state + b_column[:, None] * drive_row[None, :]
        return (carry_state, lax.optimization_barrier(jnp.sum(c_column[:, None] * carry_state, axis=0)))
    final_state, scan_out = lax.scan(advance, prefix_state, (step_size, driving, b_proj.T, c_proj.T))
    mixed_out = scan_out + skip_gain[None, :] * conv_act
    gated_rows = (mixed_out * jax.nn.silu(gate_in.astype(jnp.float32))).astype(jnp.bfloat16)
    projected = jnp.dot(gated_rows, out_proj, preferred_element_type=jnp.float32)
    return (residual.astype(jnp.float32) + projected).astype(jnp.bfloat16)

def reference(mixer_in, gate_in, delta_in, b_proj, c_proj, conv_kernel, conv_bias, delta_bias, decay_log, skip_gain, prefix_state, prefix_tail, out_proj, residual, norm_gain, expert_gate, expert_up, expert_down, expert_ids, route_gates):
    mixer_out = mixer_layer(mixer_in, gate_in, delta_in, b_proj, c_proj, conv_kernel, conv_bias, delta_bias, decay_log, skip_gain, prefix_state, prefix_tail, out_proj, residual)
    mixer_wide = mixer_out.astype(jnp.float32)
    norm_scale = lax.rsqrt(lax.optimization_barrier(jnp.mean(mixer_wide * mixer_wide, axis=1, keepdims=True)) + 1e-05)
    normed = (mixer_wide * norm_scale * norm_gain[None, :]).astype(jnp.bfloat16)
    slot_total = N_EXP * CAP
    flat_choice = expert_ids.reshape(N_EXP, BLOCK * TOP)
    flat_gates = route_gates.reshape(-1)
    token_of = (jnp.arange(SEQ_LEN * TOP) // TOP).astype(jnp.int32)
    block_base = (jnp.arange(N_EXP) * CAP).astype(jnp.int32)[:, None]

    def one_expert(expert_num, totals):
        expert_index = jnp.asarray(expert_num).astype(jnp.int32)
        chosen = (flat_choice == expert_index).astype(jnp.int32)
        earlier_count = jnp.cumsum(chosen, axis=1).astype(jnp.int32) - 1
        places = jnp.where(chosen > 0, block_base + earlier_count, slot_total).astype(jnp.int32).reshape(-1)
        picks = jnp.zeros((slot_total,), jnp.int32).at[places].set(token_of, mode='drop')
        weights = jnp.zeros((slot_total,), jnp.float32).at[places].set(flat_gates, mode='drop')
        arrived = normed[picks]
        w_gate = lax.dynamic_index_in_dim(expert_gate, expert_index, 0, keepdims=False)
        w_up = lax.dynamic_index_in_dim(expert_up, expert_index, 0, keepdims=False)
        w_down = lax.dynamic_index_in_dim(expert_down, expert_index, 0, keepdims=False)
        gate_act = jnp.dot(arrived, w_gate, preferred_element_type=jnp.float32)
        up_act = jnp.dot(arrived, w_up, preferred_element_type=jnp.float32)
        hidden = (jax.nn.silu(gate_act) * up_act).astype(jnp.bfloat16)

        def add_share(share, accum):
            begin = (jnp.asarray(share) * FF_DEV).astype(jnp.int32)
            part_sum = jnp.dot(lax.dynamic_slice_in_dim(hidden, begin, FF_DEV, 1), lax.dynamic_slice_in_dim(w_down, begin, FF_DEV, 0), preferred_element_type=jnp.float32)
            return accum + lax.optimization_barrier(part_sum.astype(jnp.bfloat16)).astype(jnp.float32)
        expert_sum = lax.fori_loop(0, N_CTX, add_share, jnp.zeros((slot_total, D), jnp.float32))
        expert_out = lax.optimization_barrier(expert_sum.astype(jnp.bfloat16)).astype(jnp.float32)
        return totals.at[picks].add(weights[:, None] * expert_out)
    expert_mix = lax.fori_loop(0, EXPERTS, one_expert, jnp.zeros((SEQ_LEN, D), jnp.float32))
    block_out = (mixer_wide + expert_mix).astype(jnp.bfloat16)
    return (mixer_out, block_out)
```

```python
import functools
import math

import jax
import jax.numpy as jnp
from jax import lax
from jax.experimental import pallas as pl
from jax.experimental.pallas import tpu as pltpu
from jax.sharding import PartitionSpec as P

D = 8192
SIDE = 4
STATES = 16
LANES = 128
STRIP = 512
LOG2E = math.log2(math.e)
MESH = pl.DeviceIdType.MESH


def strip_spec(rows):
    return pl.BlockSpec((rows, STRIP), lambda i: (0, i))


def whole_spec(shape):
    return pl.BlockSpec(shape, lambda i: (0,) * len(shape))


def lane_parts(value):
    return tuple(value[:, k * LANES : (k + 1) * LANES] for k in range(STRIP // LANES))


def prepare_kernel(
    rim_ref, mixer_ref, delta_ref, taps_ref, bias_ref, delta_bias_ref, decay_ref, b_ref,
    act_out, step_out, total_out, end_out, padded, drive,
):
    tokens = mixer_ref.shape[0]
    padded[0:8] = rim_ref[...]
    padded[8 : 8 + tokens] = mixer_ref[...].astype(jnp.float32)
    convolved = bias_ref[...]
    for k in range(4):
        convolved = convolved + taps_ref[k : k + 1] * padded[5 + k : 5 + k + tokens]
    act = convolved / (1.0 + jnp.exp(-convolved))
    step = jnp.log(1.0 + jnp.exp(delta_ref[...].astype(jnp.float32) + delta_bias_ref[...]))
    act_out[...] = act
    step_out[...] = step
    drive[...] = act * step
    total_out[...] = jnp.sum(step, axis=0, keepdims=True)
    rate = lane_parts(-jnp.exp(decay_ref[...]) * LOG2E)

    def group(index, state):
        base = pl.multiple_of(index * 8, 8)
        steps = step_out[pl.ds(base, 8), :]
        drives = drive[pl.ds(base, 8), :]
        for i in range(8):
            b_column = b_ref[base + i]
            step_row, drive_row = lane_parts(steps[i : i + 1]), lane_parts(drives[i : i + 1])
            state = tuple(
                jnp.exp2(r * s) * h + b_column * d
                for r, s, h, d in zip(rate, step_row, state, drive_row)
            )
        return state

    zero = jnp.zeros((STATES, LANES), jnp.float32)
    state = lax.fori_loop(0, tokens // 8, group, (zero,) * (STRIP // LANES))
    end_out[...] = jnp.concatenate(state, axis=1).astype(end_out.dtype)


def scan_kernel(
    place_ref, act_ref, step_ref, gate_ref, decay_ref, prefix_ref, gain_ref, b_ref, c_ref,
    totals_ref, ends_ref, out_ref, summed, drive,
):
    tokens = act_ref.shape[0]
    rate_whole = -jnp.exp(decay_ref[...]) * LOG2E
    rate = lane_parts(rate_whole)

    def enter(source, state):
        return (
            jnp.exp2(rate_whole * totals_ref[source]) * state
            + ends_ref[source].astype(jnp.float32)
        )

    drive[...] = act_ref[...] * step_ref[...]
    entry = lane_parts(lax.fori_loop(0, place_ref[0], enter, prefix_ref[...]))

    def group(index, state):
        base = pl.multiple_of(index * 8, 8)
        steps = step_ref[pl.ds(base, 8), :]
        drives = drive[pl.ds(base, 8), :]
        rows = []
        for i in range(8):
            b_column, c_column = b_ref[base + i], c_ref[base + i]
            step_row, drive_row = lane_parts(steps[i : i + 1]), lane_parts(drives[i : i + 1])
            state = tuple(
                jnp.exp2(r * s) * h + b_column * d
                for r, s, h, d in zip(rate, step_row, state, drive_row)
            )
            rows.append(
                jnp.concatenate(
                    [jnp.sum(c_column * h, axis=0, keepdims=True) for h in state], axis=1
                )
            )
        summed[pl.ds(base, 8), :] = jnp.concatenate(rows, axis=0)
        return state

    lax.fori_loop(0, tokens // 8, group, entry)
    gate = gate_ref[...].astype(jnp.float32)
    mixed = summed[...] + gain_ref[...] * act_ref[...]
    out_ref[...] = (mixed * (gate / (1.0 + jnp.exp(-gate)))).astype(out_ref.dtype)


def exchange_kernel(count, ends_ref, total_ref, all_ends, all_totals, send_sems, recv_sems):
    me = lax.axis_index("ctx")
    barrier = pltpu.get_barrier_semaphore()
    for k in range(1, count):

        @pl.when(me >= k)
        def _():
            pl.semaphore_signal(barrier, inc=1, device_id={"ctx": me - k}, device_id_type=MESH)

    @pl.when(me < count - 1)
    def _():
        pl.semaphore_wait(barrier, count - 1 - me)

    def copies(k, source, target):
        return [
            pltpu.make_async_remote_copy(
                src_ref=mine,
                dst_ref=whole.at[source],
                send_sem=send_sems.at[k - 1, part],
                recv_sem=recv_sems.at[k - 1, part],
                device_id={"ctx": target},
                device_id_type=MESH,
            )
            for part, (mine, whole) in enumerate(((ends_ref, all_ends), (total_ref, all_totals)))
        ]

    for k in range(1, count):

        @pl.when(me + k < count)
        def _():
            for copy in copies(k, me, me + k):
                copy.start()

    for k in range(1, count):

        @pl.when(me >= k)
        def _():
            for copy in copies(k, me - k, me):
                copy.wait_recv()

        @pl.when(me + k < count)
        def _():
            for copy in copies(k, me, me + k):
                copy.wait_send()


def exchange(count, ends, total):
    return pl.pallas_call(
        functools.partial(exchange_kernel, count),
        out_shape=(
            jax.ShapeDtypeStruct((count,) + ends.shape, ends.dtype),
            jax.ShapeDtypeStruct((count,) + total.shape, total.dtype),
        ),
        in_specs=[pl.BlockSpec(memory_space=pltpu.VMEM)] * 2,
        out_specs=(pl.BlockSpec(memory_space=pltpu.VMEM),) * 2,
        scratch_shapes=[
            pltpu.SemaphoreType.DMA((count - 1, 2)),
            pltpu.SemaphoreType.DMA((count - 1, 2)),
        ],
        compiler_params=pltpu.CompilerParams(collective_id=1, has_side_effects=True),
        name="state_exchange",
    )(ends, total)


PIECES = 20


def gather_kernel(by_columns, block_ref, out_ref, send_sems, recv_sems, own_sem):
    me = lax.axis_index("ctx")
    place = (me // SIDE, me % SIDE)
    rows, columns = block_ref.shape
    half, quarter = rows // 2, rows // 4

    def index(half_number, first, second):
        a = lax.rem(place[half_number] + first + 2 * SIDE, SIDE)
        b = lax.rem(place[1 - half_number] + second + 2 * SIDE, SIDE)
        return a * SIDE + b if half_number == 0 else b * SIDE + a

    def window(owner, start, size):
        if by_columns:
            return out_ref.at[pl.ds(start, size), pl.ds(pl.multiple_of(owner * columns, columns), columns)]
        return out_ref.at[pl.ds(pl.multiple_of(owner * rows + start, 16), size), :]

    def copy(number, sem, owner, start, size, target, own=False):
        return pltpu.make_async_remote_copy(
            src_ref=block_ref.at[pl.ds(start, size), :] if own else window(owner, start, size),
            dst_ref=window(owner, start, size),
            send_sem=send_sems.at[number, sem],
            recv_sem=recv_sems.at[number, sem],
            device_id={"ctx": target},
            device_id_type=MESH,
        )

    barrier = pltpu.get_barrier_semaphore()
    for first, second in ((1, 0), (-1, 0), (0, 1), (0, -1)):
        pl.semaphore_signal(
            barrier, inc=1, device_id={"ctx": index(0, first, second)}, device_id_type=MESH
        )
    pl.semaphore_wait(barrier, 4)
    own_copy = pltpu.make_async_copy(block_ref, window(me, 0, rows), own_sem)
    own_copy.start()

    RING = {(-1, None): 0, (1, None): 1, (2, 0): 2, (2, 1): 3}
    LINE = {0: 4, -1: 8, 1: 12, 2: 16}
    sent = []

    def span(number, part):
        start = number * half
        return (start, half) if part is None else (start + part * quarter, quarter)

    def send(number, sem, first, second, part, towards, own=False):
        one = copy(
            number, sem, index(number, first, second), *span(number, part),
            index(number, *towards), own,
        )
        one.start()
        sent.append(one)

    def arrived(number, sem, first, second, part):
        copy(number, sem, index(number, first, second), *span(number, part), me).wait_recv()

    def send_line(number, first, own=False):
        send(number, LINE[first] + RING[-1, None], first, 0, None, (0, 1), own)
        send(number, LINE[first] + RING[1, None], first, 0, None, (0, -1), own)

    def pass_on(number, first):
        arrived(number, LINE[first] + 0, first, -1, None)
        send(number, LINE[first] + 2, first, -1, 0, (0, 1))
        arrived(number, LINE[first] + 1, first, 1, None)
        send(number, LINE[first] + 3, first, 1, 1, (0, -1))

    for number in (0, 1):
        send(number, RING[-1, None], 0, 0, None, (1, 0), True)
        send(number, RING[1, None], 0, 0, None, (-1, 0), True)
    for number in (0, 1):
        send_line(number, 0, True)
    for number in (0, 1):
        arrived(number, 0, -1, 0, None)
        send(number, RING[2, 0], -1, 0, 0, (1, 0))
        arrived(number, 1, 1, 0, None)
        send(number, RING[2, 1], 1, 0, 1, (-1, 0))
    for number in (0, 1):
        send_line(number, -1)
        send_line(number, 1)
    for number in (0, 1):
        pass_on(number, 0)
    for number in (0, 1):
        arrived(number, 2, 2, 0, 0)
        arrived(number, 3, 2, 0, 1)
        send_line(number, 2)
    for first in (-1, 1, 2):
        for number in (0, 1):
            pass_on(number, first)
    for first in (0, -1, 1, 2):
        for number in (0, 1):
            arrived(number, LINE[first] + 2, first, 2, 0)
            arrived(number, LINE[first] + 3, first, 2, 1)
    for one in sent:
        one.wait_send()
    own_copy.wait()


def gather(block, by_columns, collective_id):
    rows, columns = block.shape
    count = SIDE * SIDE
    shape = (rows, count * columns) if by_columns else (count * rows, columns)
    return pl.pallas_call(
        functools.partial(gather_kernel, by_columns),
        out_shape=jax.ShapeDtypeStruct(shape, block.dtype),
        in_specs=[pl.BlockSpec(memory_space=pl.ANY)],
        out_specs=pl.BlockSpec(memory_space=pl.ANY),
        scratch_shapes=[
            pltpu.SemaphoreType.DMA((2, PIECES)),
            pltpu.SemaphoreType.DMA((2, PIECES)),
            pltpu.SemaphoreType.DMA,
        ],
        compiler_params=pltpu.CompilerParams(
            collective_id=collective_id, has_side_effects=True
        ),
        name="gather_columns" if by_columns else "gather_rows",
    )(block)


def from_behind(array, axis, by):
    length = lax.axis_size(axis)
    pairs = [(i, i + by) for i in range(length) if 0 <= i + by < length]
    return lax.ppermute(array, axis, pairs)


def shards(
    mixer_in,
    gate_in,
    delta_in,
    b_proj,
    c_proj,
    conv_kernel,
    conv_bias,
    delta_bias,
    decay_log,
    skip_gain,
    prefix_state,
    prefix_tail,
    out_proj,
    residual,
    norm_gain,
    expert_gate,
    expert_up,
    expert_down,
    expert_ids,
    route_gates,
):
    tokens = mixer_in.shape[0]
    width = prefix_tail.shape[0]
    leading = lax.axis_index("ctx") == 0
    rim_rows = from_behind(mixer_in[tokens - width :], "ctx", 1)
    rim_rows = jnp.where(leading, prefix_tail, rim_rows)
    rim = jnp.concatenate(
        [jnp.zeros((8 - width, rim_rows.shape[1]), jnp.float32), rim_rows.astype(jnp.float32)]
    )
    channels = mixer_in.shape[1]
    b_wide = jnp.broadcast_to(b_proj.T[:, :, None], (tokens, STATES, LANES))
    c_wide = jnp.broadcast_to(c_proj.T[:, :, None], (tokens, STATES, LANES))
    f32 = functools.partial(jax.ShapeDtypeStruct, dtype=jnp.float32)
    strips = (channels // STRIP,)
    limit = pltpu.CompilerParams(vmem_limit_bytes=32 * 1024 * 1024)
    conv_act, step_size, total, local_end = pl.pallas_call(
        prepare_kernel,
        grid=strips,
        out_shape=(
            f32((tokens, channels)),
            f32((tokens, channels)),
            f32((1, channels)),
            jax.ShapeDtypeStruct((STATES, channels), jnp.bfloat16),
        ),
        in_specs=[
            strip_spec(8),
            strip_spec(tokens),
            strip_spec(tokens),
            strip_spec(4),
            strip_spec(1),
            strip_spec(1),
            strip_spec(STATES),
            whole_spec((tokens, STATES, LANES)),
        ],
        out_specs=(
            strip_spec(tokens),
            strip_spec(tokens),
            strip_spec(1),
            strip_spec(STATES),
        ),
        scratch_shapes=[
            pltpu.VMEM((8 + tokens, STRIP), jnp.float32),
            pltpu.VMEM((tokens, STRIP), jnp.float32),
        ],
        compiler_params=limit,
        name="prepare",
    )(
        rim, mixer_in, delta_in, conv_kernel, conv_bias[None], delta_bias[None], decay_log, b_wide
    )
    count = lax.axis_size("ctx")
    all_ends, all_totals = exchange(count, local_end, total.reshape(channels // LANES, LANES))
    gated_rows = pl.pallas_call(
        scan_kernel,
        grid=strips,
        out_shape=jax.ShapeDtypeStruct((tokens, channels), jnp.bfloat16),
        in_specs=[
            pl.BlockSpec(memory_space=pltpu.SMEM),
            strip_spec(tokens),
            strip_spec(tokens),
            strip_spec(tokens),
            strip_spec(STATES),
            strip_spec(STATES),
            strip_spec(1),
            whole_spec((tokens, STATES, LANES)),
            whole_spec((tokens, STATES, LANES)),
            pl.BlockSpec((count, 1, STRIP), lambda i: (0, 0, i)),
            pl.BlockSpec((count, STATES, STRIP), lambda i: (0, 0, i)),
        ],
        out_specs=strip_spec(tokens),
        scratch_shapes=[
            pltpu.VMEM((tokens, STRIP), jnp.float32),
            pltpu.VMEM((tokens, STRIP), jnp.float32),
        ],
        compiler_params=limit,
        name="scan",
    )(
        lax.axis_index("ctx").reshape(1),
        conv_act,
        step_size,
        gate_in,
        decay_log,
        prefix_state,
        skip_gain[None],
        b_wide,
        c_wide,
        all_totals.reshape(count, 1, channels),
        all_ends,
    )
    gathered = gather(gated_rows, False, 2)
    block_rows = residual.shape[0]
    projected = lax.psum_scatter(
        jnp.dot(
            lax.slice_in_dim(gathered, 0, lax.axis_size("exp") * block_rows, axis=0),
            out_proj,
            preferred_element_type=jnp.float32,
        ).astype(jnp.bfloat16),
        "exp",
        scatter_dimension=0,
        tiled=True,
    ).astype(jnp.float32)
    mixer_out = (residual.astype(jnp.float32) + projected).astype(jnp.bfloat16)
    mixer_wide = mixer_out.astype(jnp.float32)
    squares = jnp.sum(
        lax.all_gather(jnp.sum(mixer_wide * mixer_wide, axis=1), "ctx", axis=0), axis=0
    )
    norm_scale = lax.rsqrt(squares / D + 1e-05)
    normed = (mixer_wide * norm_scale[:, None] * norm_gain[None, :]).astype(jnp.bfloat16)
    experts = expert_gate.shape[0] * lax.axis_size("exp")
    top_count = expert_ids.shape[1]
    capacity = 3 * block_rows * top_count // (2 * experts)
    flat_choice = expert_ids.reshape(-1)
    owner_hot = (flat_choice[:, None] == jnp.arange(experts, dtype=jnp.int32)[None, :]).astype(
        jnp.int32
    )
    earlier_count = jnp.cumsum(owner_hot, axis=0) - owner_hot
    slot_index = jnp.sum(earlier_count * owner_hot, axis=1)
    matches = (
        flat_choice[:, None, None] == jnp.arange(experts, dtype=jnp.int32)[None, :, None]
    ) & (slot_index[:, None, None] == jnp.arange(capacity, dtype=jnp.int32)[None, None, :])
    picks = matches.reshape(block_rows, top_count, experts, capacity)
    selector = jnp.any(picks, axis=1).astype(jnp.bfloat16)
    weights = jnp.sum(picks.astype(jnp.float32) * route_gates[:, :, None, None], axis=1)
    slot_total = experts * capacity
    outgoing = jnp.einsum(
        "tec,td->ecd", selector, normed, preferred_element_type=jnp.float32
    ).astype(jnp.bfloat16)
    received = lax.all_to_all(outgoing, "exp", split_axis=0, concat_axis=0, tiled=True)
    arrived = received.reshape(slot_total, -1)
    piece_rows = gather(arrived, True, 3)
    feature_count = piece_rows.shape[1]
    gate_rows = lax.slice_in_dim(expert_gate[0], 0, feature_count, axis=0)
    up_rows = lax.slice_in_dim(expert_up[0], 0, feature_count, axis=0)
    gate_act = jnp.dot(piece_rows, gate_rows, preferred_element_type=jnp.float32)
    up_act = jnp.dot(piece_rows, up_rows, preferred_element_type=jnp.float32)
    hidden = (jax.nn.silu(gate_act) * up_act).astype(jnp.bfloat16)
    partial_value = jnp.dot(hidden, expert_down[0], preferred_element_type=jnp.float32)
    summed = lax.psum_scatter(
        partial_value.astype(jnp.bfloat16), "ctx", scatter_dimension=1, tiled=True
    )
    answer = summed.reshape(experts, capacity, -1)
    returned = lax.all_to_all(answer, "exp", split_axis=0, concat_axis=0, tiled=True)
    expert_mix = jnp.einsum(
        "tec,ecd->td", weights, returned.astype(jnp.float32), preferred_element_type=jnp.float32
    )
    block_out = (mixer_wide + expert_mix).astype(jnp.bfloat16)
    return (mixer_out, block_out)


def solution(mesh):
    placed = (
        P("ctx", "exp"),
        P("ctx", "exp"),
        P("ctx", "exp"),
        P(None, "ctx"),
        P(None, "ctx"),
        P(None, "exp"),
        P("exp"),
        P("exp"),
        P(None, "exp"),
        P("exp"),
        P(None, "exp"),
        P(None, "exp"),
        P("exp", "ctx"),
        P("exp", "ctx"),
        P("ctx"),
        P("exp", None, "ctx"),
        P("exp", None, "ctx"),
        P("exp", "ctx", None),
        P("exp", None),
        P("exp", None),
    )
    return jax.shard_map(
        shards,
        mesh=mesh,
        in_specs=placed,
        out_specs=(P("exp", "ctx"), P("exp", "ctx")),
        check_vma=False,
    )
```

```python
import functools
import math

import jax
import jax.numpy as jnp
from jax import lax
from jax.experimental import pallas as pl
from jax.experimental.pallas import tpu as pltpu
from jax.sharding import PartitionSpec as P

D = 8192
SIDE = 4
STATES = 16
LANES = 128
STRIP = 512
LOG2E = math.log2(math.e)
MESH = pl.DeviceIdType.MESH


def strip_spec(rows):
    return pl.BlockSpec((rows, STRIP), lambda i: (0, i))


def whole_spec(shape):
    return pl.BlockSpec(shape, lambda i: (0,) * len(shape))


def lane_parts(value):
    return tuple(value[:, k * LANES : (k + 1) * LANES] for k in range(STRIP // LANES))


def prepare_kernel(
    rim_ref, mixer_ref, delta_ref, taps_ref, bias_ref, delta_bias_ref, decay_ref, b_ref,
    act_out, step_out, total_out, end_out, padded, drive,
):
    tokens = mixer_ref.shape[0]
    padded[0:8] = rim_ref[...]
    padded[8 : 8 + tokens] = mixer_ref[...].astype(jnp.float32)
    convolved = bias_ref[...]
    for k in range(4):
        convolved = convolved + taps_ref[k : k + 1] * padded[5 + k : 5 + k + tokens]
    act = convolved / (1.0 + jnp.exp(-convolved))
    step = jnp.log(1.0 + jnp.exp(delta_ref[...].astype(jnp.float32) + delta_bias_ref[...]))
    act_out[...] = act
    step_out[...] = step
    drive[...] = act * step
    total_out[...] = jnp.sum(step, axis=0, keepdims=True)
    rate = lane_parts(-jnp.exp(decay_ref[...]) * LOG2E)

    def group(index, state):
        base = pl.multiple_of(index * 8, 8)
        steps = step_out[pl.ds(base, 8), :]
        drives = drive[pl.ds(base, 8), :]
        for i in range(8):
            b_column = b_ref[base + i]
            step_row, drive_row = lane_parts(steps[i : i + 1]), lane_parts(drives[i : i + 1])
            state = tuple(
                jnp.exp2(r * s) * h + b_column * d
                for r, s, h, d in zip(rate, step_row, state, drive_row)
            )
        return state

    zero = jnp.zeros((STATES, LANES), jnp.float32)
    state = lax.fori_loop(0, tokens // 8, group, (zero,) * (STRIP // LANES))
    end_out[...] = jnp.concatenate(state, axis=1).astype(end_out.dtype)


def scan_kernel(
    place_ref, act_ref, step_ref, gate_ref, decay_ref, prefix_ref, gain_ref, b_ref, c_ref,
    totals_ref, ends_ref, out_ref, summed, drive,
):
    tokens = act_ref.shape[0]
    rate_whole = -jnp.exp(decay_ref[...]) * LOG2E
    rate = lane_parts(rate_whole)

    def enter(source, state):
        return (
            jnp.exp2(rate_whole * totals_ref[source]) * state
            + ends_ref[source].astype(jnp.float32)
        )

    drive[...] = act_ref[...] * step_ref[...]
    entry = lane_parts(lax.fori_loop(0, place_ref[0], enter, prefix_ref[...]))

    def group(index, state):
        base = pl.multiple_of(index * 8, 8)
        steps = step_ref[pl.ds(base, 8), :]
        drives = drive[pl.ds(base, 8), :]
        rows = []
        for i in range(8):
            b_column, c_column = b_ref[base + i], c_ref[base + i]
            step_row, drive_row = lane_parts(steps[i : i + 1]), lane_parts(drives[i : i + 1])
            state = tuple(
                jnp.exp2(r * s) * h + b_column * d
                for r, s, h, d in zip(rate, step_row, state, drive_row)
            )
            rows.append(
                jnp.concatenate(
                    [jnp.sum(c_column * h, axis=0, keepdims=True) for h in state], axis=1
                )
            )
        summed[pl.ds(base, 8), :] = jnp.concatenate(rows, axis=0)
        return state

    lax.fori_loop(0, tokens // 8, group, entry)
    gate = gate_ref[...].astype(jnp.float32)
    mixed = summed[...] + gain_ref[...] * act_ref[...]
    out_ref[...] = (mixed * (gate / (1.0 + jnp.exp(-gate)))).astype(out_ref.dtype)


def exchange_kernel(count, ends_ref, total_ref, all_ends, all_totals, send_sems, recv_sems):
    me = lax.axis_index("ctx")
    barrier = pltpu.get_barrier_semaphore()
    for k in range(1, count):

        @pl.when(me >= k)
        def _():
            pl.semaphore_signal(barrier, inc=1, device_id={"ctx": me - k}, device_id_type=MESH)

    @pl.when(me < count - 1)
    def _():
        pl.semaphore_wait(barrier, count - 1 - me)

    def copies(k, source, target):
        return [
            pltpu.make_async_remote_copy(
                src_ref=mine,
                dst_ref=whole.at[source],
                send_sem=send_sems.at[k - 1, part],
                recv_sem=recv_sems.at[k - 1, part],
                device_id={"ctx": target},
                device_id_type=MESH,
            )
            for part, (mine, whole) in enumerate(((ends_ref, all_ends), (total_ref, all_totals)))
        ]

    for k in range(1, count):

        @pl.when(me + k < count)
        def _():
            for copy in copies(k, me, me + k):
                copy.start()

    for k in range(1, count):

        @pl.when(me >= k)
        def _():
            for copy in copies(k, me - k, me):
                copy.wait_recv()

        @pl.when(me + k < count)
        def _():
            for copy in copies(k, me, me + k):
                copy.wait_send()


def exchange(count, ends, total):
    return pl.pallas_call(
        functools.partial(exchange_kernel, count),
        out_shape=(
            jax.ShapeDtypeStruct((count,) + ends.shape, ends.dtype),
            jax.ShapeDtypeStruct((count,) + total.shape, total.dtype),
        ),
        in_specs=[pl.BlockSpec(memory_space=pltpu.VMEM)] * 2,
        out_specs=(pl.BlockSpec(memory_space=pltpu.VMEM),) * 2,
        scratch_shapes=[
            pltpu.SemaphoreType.DMA((count - 1, 2)),
            pltpu.SemaphoreType.DMA((count - 1, 2)),
        ],
        compiler_params=pltpu.CompilerParams(collective_id=1, has_side_effects=True),
        name="state_exchange",
    )(ends, total)


PIECES = 20


def gather_kernel(by_columns, block_ref, out_ref, send_sems, recv_sems, own_sem):
    me = lax.axis_index("ctx")
    place = (me // SIDE, me % SIDE)
    rows, columns = block_ref.shape
    half, quarter = rows // 2, rows // 4

    def index(half_number, first, second):
        a = lax.rem(place[half_number] + first + 2 * SIDE, SIDE)
        b = lax.rem(place[1 - half_number] + second + 2 * SIDE, SIDE)
        return a * SIDE + b if half_number == 0 else b * SIDE + a

    def window(owner, start, size):
        if by_columns:
            return out_ref.at[pl.ds(start, size), pl.ds(pl.multiple_of(owner * columns, columns), columns)]
        return out_ref.at[pl.ds(pl.multiple_of(owner * rows + start, 16), size), :]

    def copy(number, sem, owner, start, size, target, own=False):
        return pltpu.make_async_remote_copy(
            src_ref=block_ref.at[pl.ds(start, size), :] if own else window(owner, start, size),
            dst_ref=window(owner, start, size),
            send_sem=send_sems.at[number, sem],
            recv_sem=recv_sems.at[number, sem],
            device_id={"ctx": target},
            device_id_type=MESH,
        )

    barrier = pltpu.get_barrier_semaphore()
    for first, second in ((1, 0), (-1, 0), (0, 1), (0, -1)):
        pl.semaphore_signal(
            barrier, inc=1, device_id={"ctx": index(0, first, second)}, device_id_type=MESH
        )
    pl.semaphore_wait(barrier, 4)
    own_copy = pltpu.make_async_copy(block_ref, window(me, 0, rows), own_sem)
    own_copy.start()

    RING = {(-1, None): 0, (1, None): 1, (2, 0): 2, (2, 1): 3}
    LINE = {0: 4, -1: 8, 1: 12, 2: 16}
    sent = []

    def span(number, part):
        start = number * half
        return (start, half) if part is None else (start + part * quarter, quarter)

    def send(number, sem, first, second, part, towards, own=False):
        one = copy(
            number, sem, index(number, first, second), *span(number, part),
            index(number, *towards), own,
        )
        one.start()
        sent.append(one)

    def arrived(number, sem, first, second, part):
        copy(number, sem, index(number, first, second), *span(number, part), me).wait_recv()

    def send_line(number, first, own=False):
        send(number, LINE[first] + RING[-1, None], first, 0, None, (0, 1), own)
        send(number, LINE[first] + RING[1, None], first, 0, None, (0, -1), own)

    def pass_on(number, first):
        arrived(number, LINE[first] + 0, first, -1, None)
        send(number, LINE[first] + 2, first, -1, 0, (0, 1))
        arrived(number, LINE[first] + 1, first, 1, None)
        send(number, LINE[first] + 3, first, 1, 1, (0, -1))

    for number in (0, 1):
        send(number, RING[-1, None], 0, 0, None, (1, 0), True)
        send(number, RING[1, None], 0, 0, None, (-1, 0), True)
    for number in (0, 1):
        send_line(number, 0, True)
    for number in (0, 1):
        arrived(number, 0, -1, 0, None)
        send(number, RING[2, 0], -1, 0, 0, (1, 0))
        arrived(number, 1, 1, 0, None)
        send(number, RING[2, 1], 1, 0, 1, (-1, 0))
    for number in (0, 1):
        send_line(number, -1)
        send_line(number, 1)
    for number in (0, 1):
        pass_on(number, 0)
    for number in (0, 1):
        arrived(number, 2, 2, 0, 0)
        arrived(number, 3, 2, 0, 1)
        send_line(number, 2)
    for first in (-1, 1, 2):
        for number in (0, 1):
            pass_on(number, first)
    for first in (0, -1, 1, 2):
        for number in (0, 1):
            arrived(number, LINE[first] + 2, first, 2, 0)
            arrived(number, LINE[first] + 3, first, 2, 1)
    for one in sent:
        one.wait_send()
    own_copy.wait()


def gather(block, by_columns, collective_id):
    rows, columns = block.shape
    count = SIDE * SIDE
    shape = (rows, count * columns) if by_columns else (count * rows, columns)
    return pl.pallas_call(
        functools.partial(gather_kernel, by_columns),
        out_shape=jax.ShapeDtypeStruct(shape, block.dtype),
        in_specs=[pl.BlockSpec(memory_space=pl.ANY)],
        out_specs=pl.BlockSpec(memory_space=pl.ANY),
        scratch_shapes=[
            pltpu.SemaphoreType.DMA((2, PIECES)),
            pltpu.SemaphoreType.DMA((2, PIECES)),
            pltpu.SemaphoreType.DMA,
        ],
        compiler_params=pltpu.CompilerParams(
            collective_id=collective_id, has_side_effects=True
        ),
        name="gather_columns" if by_columns else "gather_rows",
    )(block)


EXPERTS = 8
FORWARD = ((-1, None), (1, None), (2, 0), (2, 1))
LINES = {0: 0, -1: 1, 1: 2, 2: 3}
RING = 4


class Torus:
    def __init__(self):
        me = lax.axis_index("ctx")
        self.me = me
        self.place = (me // SIDE, me % SIDE)

    def index(self, half, first, second):
        a = lax.rem(self.place[half] + first + 2 * SIDE, SIDE)
        b = lax.rem(self.place[1 - half] + second + 2 * SIDE, SIDE)
        return a * SIDE + b if half == 0 else b * SIDE + a


def span(rows, half, part=None):
    start = half * (rows // 2)
    return (start, rows // 2) if part is None else (start + part * (rows // 4), rows // 4)


def expert_kernel(
    capacity, features,
    mixer_ref, squares_ref, pick_ref, place_ref, route_ref, gain_ref, gate_ref, up_ref, down_ref,
    out_ref,
    blocks, landed, wide, down, total, hidden, outgoing, answer, returned, all_squares,
    square_sems, dispatch_sems, return_sems, gather_sems, sum_sems, weight_sems,
):
    torus = Torus()
    me, index = torus.me, torus.index
    own_expert = lax.axis_index("exp")
    slots, width = answer.shape
    units = down.shape[0]
    count = SIDE * SIDE

    weights = [
        pltpu.make_async_copy(gate_ref.at[0], wide.at[:, pl.ds(0, units)], weight_sems.at[0]),
        pltpu.make_async_copy(up_ref.at[0], wide.at[:, pl.ds(units, units)], weight_sems.at[1]),
        pltpu.make_async_copy(down_ref.at[0], down, weight_sems.at[2]),
    ]
    for one in weights:
        one.start()

    barrier = pltpu.get_barrier_semaphore()
    for k in range(1, count):
        pl.semaphore_signal(
            barrier, inc=1, device_id={"ctx": lax.rem(me + k, count)}, device_id_type=MESH
        )
    for k in range(1, EXPERTS):
        pl.semaphore_signal(
            barrier, inc=1, device_id={"exp": lax.rem(own_expert + k, EXPERTS)}, device_id_type=MESH
        )
    pl.semaphore_wait(barrier, count - 1 + EXPERTS - 1)

    square_copies = []
    for k in range(1, count):
        square_copies.append(
            pltpu.make_async_remote_copy(
                src_ref=squares_ref,
                dst_ref=all_squares.at[me],
                send_sem=square_sems.at[0, k - 1],
                recv_sem=square_sems.at[1, k - 1],
                device_id={"ctx": lax.rem(me + k, count)},
                device_id_type=MESH,
            )
        )
        square_copies[-1].start()
    all_squares[me] = squares_ref[...]
    for k in range(1, count):
        source = lax.rem(me + count - k, count)
        pltpu.make_async_remote_copy(
            src_ref=squares_ref,
            dst_ref=all_squares.at[source],
            send_sem=square_sems.at[0, k - 1],
            recv_sem=square_sems.at[1, k - 1],
            device_id={"ctx": me},
            device_id_type=MESH,
        ).wait_recv()
    scale = lax.rsqrt(jnp.sum(all_squares[...], axis=0) / features + 1e-05)

    def pick(chunk, carry):
        rows = pl.ds(pl.multiple_of(chunk * capacity, 16), capacity)
        chosen = pick_ref[rows, :]
        picked = jnp.dot(chosen, mixer_ref[...], preferred_element_type=jnp.float32)
        chosen = chosen.astype(jnp.float32)
        row_scale = sum(
            jnp.sum(
                chosen[:, k * LANES : (k + 1) * LANES] * scale[k : k + 1], axis=1, keepdims=True
            )
            for k in range(chosen.shape[1] // LANES)
        )
        outgoing[rows, :] = (picked * row_scale * gain_ref[...]).astype(outgoing.dtype)
        return carry

    lax.fori_loop(0, EXPERTS, pick, 0)

    def expert_rows(expert):
        return pl.ds(pl.multiple_of(expert * capacity, 16), capacity)

    def across(sems, source, target_ref):
        started = []
        for k in range(1, EXPERTS):
            peer = lax.rem(own_expert + k, EXPERTS)
            started.append(
                pltpu.make_async_remote_copy(
                    src_ref=source.at[expert_rows(peer), :],
                    dst_ref=target_ref.at[expert_rows(own_expert), :],
                    send_sem=sems.at[0, k - 1],
                    recv_sem=sems.at[1, k - 1],
                    device_id={"exp": peer},
                    device_id_type=MESH,
                )
            )
            started[-1].start()
        target_ref[expert_rows(own_expert), :] = source[expert_rows(own_expert), :]
        for k in range(1, EXPERTS):
            origin = lax.rem(own_expert + EXPERTS - k, EXPERTS)
            pltpu.make_async_remote_copy(
                src_ref=source.at[expert_rows(origin), :],
                dst_ref=target_ref.at[expert_rows(origin), :],
                send_sem=sems.at[0, k - 1],
                recv_sem=sems.at[1, k - 1],
                device_id={"exp": own_expert},
                device_id_type=MESH,
            ).wait_recv()
        return started

    crossing = across(dispatch_sems, outgoing, blocks.at[me])

    in_flight = {}

    def moved(half, line, kind, first, second, part, target):
        start, size = span(slots, half, part)
        ref = blocks.at[index(half, first, second), pl.ds(start, size), :]
        return pltpu.make_async_remote_copy(
            src_ref=ref,
            dst_ref=ref,
            send_sem=gather_sems.at[0, half, line, kind],
            recv_sem=gather_sems.at[1, half, line, kind],
            device_id={"ctx": target},
            device_id_type=MESH,
        )

    def send(half, line, kind, first, second, part, towards):
        one = moved(half, line, kind, first, second, part, index(half, *towards))
        one.start()
        where = (first, second) if half == 0 else (second, first)
        in_flight.setdefault(where, []).append(one)

    def arrived(half, line, kind, first, second, part):
        moved(half, line, kind, first, second, part, me).wait_recv()

    def send_line(half, first):
        send(half, LINES[first], 0, first, 0, None, (0, 1))
        send(half, LINES[first], 1, first, 0, None, (0, -1))

    def pass_on(half, first):
        arrived(half, LINES[first], 0, first, -1, None)
        send(half, LINES[first], 2, first, -1, 0, (0, 1))
        arrived(half, LINES[first], 1, first, 1, None)
        send(half, LINES[first], 3, first, 1, 1, (0, -1))

    def last_of(half, first):
        arrived(half, LINES[first], 2, first, 2, 0)
        arrived(half, LINES[first], 3, first, 2, 1)

    row_tile = slots // 2

    def over_blocks(where, number, body):
        def one(step, carry):
            block, tile = step // 2, step % 2
            dx, dy = where(block)
            owner = index(0, dx, dy)
            body(owner, pl.ds(pl.multiple_of(tile * row_tile, 16), row_tile))
            return carry

        lax.fori_loop(0, number * 2, one, 0)

    def grow(owner, rows):
        part = wide[pl.ds(pl.multiple_of(owner * width, 16), width), :]
        total[rows, :] += jnp.dot(blocks[owner, rows, :], part, preferred_element_type=jnp.float32)

    def sign(i):
        return 1 - 2 * (i % 2)

    def beside(i):
        return sign(i) * (1 - i // 2), sign(i) * (i // 2)

    def corner(i):
        return sign(i), 1 - 2 * (i // 2)

    def knight(i):
        along = i // 2
        return sign(i) * (1 - along) + 2 * along, 2 * (1 - along) + sign(i) * along

    def across_ring(i):
        return 2 * (1 - i), 2 * i

    def single(dx, dy):
        return lambda i: (dx, dy)

    for half in (0, 1):
        send(half, RING, 0, 0, 0, None, (1, 0))
        send(half, RING, 1, 0, 0, None, (-1, 0))
    for half in (0, 1):
        send_line(half, 0)
    total[...] = jnp.zeros_like(total)
    for one in weights:
        one.wait()
    over_blocks(single(0, 0), 1, grow)
    for half in (0, 1):
        arrived(half, RING, 0, -1, 0, None)
        send(half, RING, 2, -1, 0, 0, (1, 0))
        arrived(half, RING, 1, 1, 0, None)
        send(half, RING, 3, 1, 0, 1, (-1, 0))
    for half in (0, 1):
        send_line(half, -1)
        send_line(half, 1)
    for half in (0, 1):
        pass_on(half, 0)
    over_blocks(beside, 4, grow)
    for half in (0, 1):
        arrived(half, RING, 2, 2, 0, 0)
        arrived(half, RING, 3, 2, 0, 1)
        send_line(half, 2)
    for half in (0, 1):
        last_of(half, 0)
    over_blocks(across_ring, 2, grow)
    for first in (-1, 1):
        for half in (0, 1):
            pass_on(half, first)
    over_blocks(corner, 4, grow)
    for half in (0, 1):
        pass_on(half, 2)
    for first in (-1, 1):
        for half in (0, 1):
            last_of(half, first)
    over_blocks(knight, 4, grow)
    for half in (0, 1):
        last_of(half, 2)
    over_blocks(single(2, 2), 1, grow)

    def activate(step, carry):
        rows = pl.ds(pl.multiple_of(step * capacity, 16), capacity)
        gate = total[rows, 0:units]
        hidden[rows, :] = (gate / (1.0 + jnp.exp(-gate)) * total[rows, units : 2 * units]).astype(
            hidden.dtype
        )
        return carry

    lax.fori_loop(0, EXPERTS, activate, 0)

    def project(owner, rows):
        part = down[:, pl.ds(pl.multiple_of(owner * width, LANES), width)]
        blocks[owner, rows, :] = jnp.dot(
            hidden[rows, :], part, preferred_element_type=jnp.float32
        ).astype(blocks.dtype)

    def fill(places, where):
        for place in places:
            for one in in_flight.pop(place, ()):
                one.wait_send()
        over_blocks(where, len(places), project)

    summing = []

    def part_rows(half, part):
        start, size = span(slots, half, part)
        return pl.ds(start, size)

    def landing(half, line, kind):
        if kind < 2:
            return landed.at[half, line, kind]
        size = slots // 4
        return landed.at[half, line, 2, pl.ds((kind - 2) * size, size), :]

    def sum_copy(half, line, kind, first, second, part, target):
        return pltpu.make_async_remote_copy(
            src_ref=blocks.at[index(half, first, second), part_rows(half, part), :],
            dst_ref=landing(half, line, kind),
            send_sem=sum_sems.at[0, half, line, kind],
            recv_sem=sum_sems.at[1, half, line, kind],
            device_id={"ctx": target},
            device_id_type=MESH,
        )

    def give(half, line, kind, first, second, part):
        step = 1 if kind % 2 == 0 else -1
        target = index(half, step, 0) if line == RING else index(half, 0, step)
        one = sum_copy(half, line, kind, first, second, part, target)
        one.start()
        summing.append(one)

    def taken(half, line, kind):
        part = None if kind < 2 else kind - 2
        sum_copy(half, line, kind, 0, 0, part, me).wait_recv()

    def add(half, first, second, part, line, kinds, target=None):
        for kind in kinds:
            taken(half, line, kind)
        start, size = span(slots, half, part)
        owner = index(half, first, second)
        tile = 96

        def one(step, carry):
            offset = pl.multiple_of(step * tile, 16)
            rows = pl.ds(pl.multiple_of(start + offset, 16), tile)
            value = blocks[owner, rows, :].astype(jnp.float32)
            for kind in kinds:
                value = value + landing(half, line, kind)[pl.ds(offset, tile), :].astype(jnp.float32)
            value = value.astype(blocks.dtype)
            if target is None:
                blocks[owner, rows, :] = value
            else:
                target[rows, :] = value
            return carry

        lax.fori_loop(0, size // tile, one, 0)

    def at(line, offset):
        return (offset, 0) if line == RING else ({v: k for k, v in LINES.items()}[line], offset)

    def begin(half, line):
        give(half, line, 2, *at(line, 2), 0)
        give(half, line, 3, *at(line, 2), 1)

    def middle(half, line):
        add(half, *at(line, 1), 0, line, (2,))
        give(half, line, 0, *at(line, 1), None)
        add(half, *at(line, -1), 1, line, (3,))
        give(half, line, 1, *at(line, -1), None)

    def finish(half, line, target=None):
        add(half, *at(line, 0), None, line, (0, 1), target)

    halves = (0, 1)
    fill([(2, 2)], single(2, 2))
    for half in halves:
        begin(half, LINES[2])
    fill([(1, 2), (-1, 2), (2, 1), (2, -1)], knight)
    for first in (1, -1):
        for half in halves:
            begin(half, LINES[first])
    fill([(2, 0), (0, 2)], across_ring)
    for half in halves:
        begin(half, LINES[0])
    for half in halves:
        middle(half, LINES[2])
    fill([(1, 1), (-1, 1), (1, -1), (-1, -1)], corner)
    for first in (1, -1):
        for half in halves:
            middle(half, LINES[first])
    fill([(1, 0), (-1, 0), (0, 1), (0, -1)], beside)
    for half in halves:
        middle(half, LINES[0])
    for one in crossing:
        one.wait_send()
    fill([(0, 0)], single(0, 0))
    for half in halves:
        finish(half, LINES[2])
        begin(half, RING)
    for first in (1, -1):
        for half in halves:
            finish(half, LINES[first])
    for half in halves:
        middle(half, RING)
    for half in halves:
        finish(half, LINES[0])
    for half in halves:
        finish(half, RING, answer)

    back = across(return_sems, answer, returned)
    rows = mixer_ref.shape[0]
    value = mixer_ref[...].astype(jnp.float32)
    for k in range(route_ref.shape[1]):
        value = value + route_ref[:, k : k + 1] * jnp.dot(
            place_ref[k], returned[...], preferred_element_type=jnp.float32
        )
    out_ref[...] = value.astype(out_ref.dtype)
    for one in summing + back + square_copies:
        one.wait_send()


def expert_layer(
    mixer_out, squares, pick, place, route_gates, gain, expert_gate, expert_up, expert_down, capacity
):
    rows, width = mixer_out.shape
    features, units = expert_gate.shape[1:]
    slots = EXPERTS * capacity
    count = SIDE * SIDE
    here = pl.BlockSpec(memory_space=pltpu.VMEM)
    away = pl.BlockSpec(memory_space=pl.ANY)
    bf16, f32 = jnp.bfloat16, jnp.float32
    return pl.pallas_call(
        functools.partial(expert_kernel, capacity, features),
        out_shape=jax.ShapeDtypeStruct((rows, width), bf16),
        in_specs=[here] * 6 + [away] * 3,
        out_specs=here,
        scratch_shapes=[
            pltpu.VMEM((count, slots, width), bf16),
            pltpu.VMEM((2, 5, 3, slots // 2, width), bf16),
            pltpu.VMEM((features, 2 * units), bf16),
            pltpu.VMEM((units, features), bf16),
            pltpu.VMEM((slots, 2 * units), f32),
            pltpu.VMEM((slots, units), bf16),
            pltpu.VMEM((slots, width), bf16),
            pltpu.VMEM((slots, width), bf16),
            pltpu.VMEM((slots, width), bf16),
            pltpu.VMEM((count,) + squares.shape, f32),
            pltpu.SemaphoreType.DMA((2, count - 1)),
            pltpu.SemaphoreType.DMA((2, EXPERTS - 1)),
            pltpu.SemaphoreType.DMA((2, EXPERTS - 1)),
            pltpu.SemaphoreType.DMA((2, 2, 5, 4)),
            pltpu.SemaphoreType.DMA((2, 2, 5, 4)),
            pltpu.SemaphoreType.DMA((3,)),
        ],
        compiler_params=pltpu.CompilerParams(
            collective_id=3, has_side_effects=True, vmem_limit_bytes=56 * 1024 * 1024
        ),
        name="expert_layer",
    )(mixer_out, squares, pick, place, route_gates, gain, expert_gate, expert_up, expert_down)


def from_behind(array, axis, by):
    length = lax.axis_size(axis)
    pairs = [(i, i + by) for i in range(length) if 0 <= i + by < length]
    return lax.ppermute(array, axis, pairs)


def shards(
    mixer_in,
    gate_in,
    delta_in,
    b_proj,
    c_proj,
    conv_kernel,
    conv_bias,
    delta_bias,
    decay_log,
    skip_gain,
    prefix_state,
    prefix_tail,
    out_proj,
    residual,
    norm_gain,
    expert_gate,
    expert_up,
    expert_down,
    expert_ids,
    route_gates,
):
    tokens = mixer_in.shape[0]
    width = prefix_tail.shape[0]
    leading = lax.axis_index("ctx") == 0
    rim_rows = from_behind(mixer_in[tokens - width :], "ctx", 1)
    rim_rows = jnp.where(leading, prefix_tail, rim_rows)
    rim = jnp.concatenate(
        [jnp.zeros((8 - width, rim_rows.shape[1]), jnp.float32), rim_rows.astype(jnp.float32)]
    )
    channels = mixer_in.shape[1]
    b_wide = jnp.broadcast_to(b_proj.T[:, :, None], (tokens, STATES, LANES))
    c_wide = jnp.broadcast_to(c_proj.T[:, :, None], (tokens, STATES, LANES))
    f32 = functools.partial(jax.ShapeDtypeStruct, dtype=jnp.float32)
    strips = (channels // STRIP,)
    limit = pltpu.CompilerParams(vmem_limit_bytes=32 * 1024 * 1024)
    conv_act, step_size, total, local_end = pl.pallas_call(
        prepare_kernel,
        grid=strips,
        out_shape=(
            f32((tokens, channels)),
            f32((tokens, channels)),
            f32((1, channels)),
            jax.ShapeDtypeStruct((STATES, channels), jnp.bfloat16),
        ),
        in_specs=[
            strip_spec(8),
            strip_spec(tokens),
            strip_spec(tokens),
            strip_spec(4),
            strip_spec(1),
            strip_spec(1),
            strip_spec(STATES),
            whole_spec((tokens, STATES, LANES)),
        ],
        out_specs=(
            strip_spec(tokens),
            strip_spec(tokens),
            strip_spec(1),
            strip_spec(STATES),
        ),
        scratch_shapes=[
            pltpu.VMEM((8 + tokens, STRIP), jnp.float32),
            pltpu.VMEM((tokens, STRIP), jnp.float32),
        ],
        compiler_params=limit,
        name="prepare",
    )(
        rim, mixer_in, delta_in, conv_kernel, conv_bias[None], delta_bias[None], decay_log, b_wide
    )
    count = lax.axis_size("ctx")
    all_ends, all_totals = exchange(count, local_end, total.reshape(channels // LANES, LANES))
    gated_rows = pl.pallas_call(
        scan_kernel,
        grid=strips,
        out_shape=jax.ShapeDtypeStruct((tokens, channels), jnp.bfloat16),
        in_specs=[
            pl.BlockSpec(memory_space=pltpu.SMEM),
            strip_spec(tokens),
            strip_spec(tokens),
            strip_spec(tokens),
            strip_spec(STATES),
            strip_spec(STATES),
            strip_spec(1),
            whole_spec((tokens, STATES, LANES)),
            whole_spec((tokens, STATES, LANES)),
            pl.BlockSpec((count, 1, STRIP), lambda i: (0, 0, i)),
            pl.BlockSpec((count, STATES, STRIP), lambda i: (0, 0, i)),
        ],
        out_specs=strip_spec(tokens),
        scratch_shapes=[
            pltpu.VMEM((tokens, STRIP), jnp.float32),
            pltpu.VMEM((tokens, STRIP), jnp.float32),
        ],
        compiler_params=limit,
        name="scan",
    )(
        lax.axis_index("ctx").reshape(1),
        conv_act,
        step_size,
        gate_in,
        decay_log,
        prefix_state,
        skip_gain[None],
        b_wide,
        c_wide,
        all_totals.reshape(count, 1, channels),
        all_ends,
    )
    gathered = gather(gated_rows, False, 2)
    block_rows = residual.shape[0]
    projected = lax.psum_scatter(
        jnp.dot(
            lax.slice_in_dim(gathered, 0, lax.axis_size("exp") * block_rows, axis=0),
            out_proj,
            preferred_element_type=jnp.float32,
        ).astype(jnp.bfloat16),
        "exp",
        scatter_dimension=0,
        tiled=True,
    ).astype(jnp.float32)
    mixer_out = (residual.astype(jnp.float32) + projected).astype(jnp.bfloat16)
    mixer_wide = mixer_out.astype(jnp.float32)
    squares = jnp.sum(mixer_wide * mixer_wide, axis=1).reshape(-1, LANES)
    experts = expert_gate.shape[0] * lax.axis_size("exp")
    top_count = expert_ids.shape[1]
    capacity = 3 * block_rows * top_count // (2 * experts)
    flat_choice = expert_ids.reshape(-1)
    owner_hot = (flat_choice[:, None] == jnp.arange(experts, dtype=jnp.int32)[None, :]).astype(
        jnp.int32
    )
    earlier_count = jnp.cumsum(owner_hot, axis=0) - owner_hot
    slot_index = jnp.sum(earlier_count * owner_hot, axis=1)
    target = (flat_choice * capacity + slot_index).reshape(block_rows, top_count)
    every_slot = jnp.arange(experts * capacity, dtype=jnp.int32)
    place = (target.T[:, :, None] == every_slot[None, None, :]).astype(jnp.bfloat16)
    pick = jnp.any(target[None, :, :] == every_slot[:, None, None], axis=2).astype(jnp.bfloat16)
    block_out = expert_layer(
        mixer_out, squares, pick, place, route_gates, norm_gain[None],
        expert_gate, expert_up, expert_down, capacity,
    )
    return (mixer_out, block_out)


def solution(mesh):
    placed = (
        P("ctx", "exp"),
        P("ctx", "exp"),
        P("ctx", "exp"),
        P(None, "ctx"),
        P(None, "ctx"),
        P(None, "exp"),
        P("exp"),
        P("exp"),
        P(None, "exp"),
        P("exp"),
        P(None, "exp"),
        P(None, "exp"),
        P("exp", "ctx"),
        P("exp", "ctx"),
        P("ctx"),
        P("exp", None, "ctx"),
        P("exp", None, "ctx"),
        P("exp", "ctx", None),
        P("exp", None),
        P("exp", None),
    )
    return jax.shard_map(
        shards,
        mesh=mesh,
        in_specs=placed,
        out_specs=(P("exp", "ctx"), P("exp", "ctx")),
        check_vma=False,
    )
```

```python
import functools
import math

import jax
import jax.numpy as jnp
from jax import lax
from jax.experimental import pallas as pl
from jax.experimental.pallas import tpu as pltpu
from jax.sharding import PartitionSpec as P

SIDE = 4
STATES = 16
LANES = 128
STRIP = 512
LOG2E = math.log2(math.e)
MESH = pl.DeviceIdType.MESH


EXPERTS = 8
LINES = {0: 0, -1: 1, 1: 2, 2: 3}
RING = 4


class Torus:
    def __init__(self):
        me = lax.axis_index("ctx")
        self.me = me
        self.place = (me // SIDE, me % SIDE)

    def index(self, half, first, second):
        a = lax.rem(self.place[half] + first + 2 * SIDE, SIDE)
        b = lax.rem(self.place[1 - half] + second + 2 * SIDE, SIDE)
        return a * SIDE + b if half == 0 else b * SIDE + a


def span(rows, half, part=None):
    start = half * (rows // 2)
    return (start, rows // 2) if part is None else (start + part * (rows // 4), rows // 4)


SLOTS = (
    (0, 0),
    (1, 0), (-1, 0), (0, 1), (0, -1),
    (2, 0), (0, 2),
    (1, 1), (-1, 1), (1, -1), (-1, -1),
    (1, 2), (-1, 2), (2, 1), (2, -1),
    (2, 2),
)


def lane_parts(value):
    return tuple(value[:, k * LANES : (k + 1) * LANES] for k in range(value.shape[1] // LANES))


def sign(i):
    return 1 - 2 * (i % 2)


def beside(i):
    return sign(i) * (1 - i // 2), sign(i) * (i // 2)


def across_ring(i):
    return 2 * (1 - i), 2 * i


def corner(i):
    return sign(i), 1 - 2 * (i // 2)


def knight(i):
    along = i // 2
    return sign(i) * (1 - along) + 2 * along, 2 * (1 - along) + sign(i) * along


def single(dx, dy):
    return lambda i: (dx, dy)


def mixer_kernel(
    mixer_ref, gate_ref, delta_ref, b_ref, c_ref, taps_ref, bias_ref, delta_bias_ref, decay_ref,
    gain_ref, prefix_ref, tail_ref, weight_ref, residual_ref,
    out_ref, squares_ref,
    rim, padded, act, step, drive, summed, b_wide, c_wide, ends, spans, line_ends, line_spans,
    rows_all, weight, parts, got, landed,
    rim_sems, end_sems, gather_sems, pair_sems, sum_sems, weight_sem,
):
    torus = Torus()
    me, index = torus.me, torus.index
    x, y = torus.place
    own = lax.axis_index("exp")
    z, core = own // 2, own % 2
    count = SIDE * SIDE
    tokens, channels = mixer_ref.shape
    strips = channels // STRIP
    f32 = jnp.float32

    def strip_lanes(strip):
        return pl.ds(pl.multiple_of(strip * STRIP, STRIP), STRIP)

    load = pltpu.make_async_copy(weight_ref, weight, weight_sem)
    load.start()
    barrier = pltpu.get_barrier_semaphore()
    for k in range(1, count):
        pl.semaphore_signal(
            barrier, inc=1, device_id={"ctx": lax.rem(me + k, count)}, device_id_type=MESH
        )
    for k in range(1, EXPERTS):
        pl.semaphore_signal(
            barrier, inc=1, device_id={"exp": lax.rem(own + k, EXPERTS)}, device_id_type=MESH
        )
    pl.semaphore_wait(barrier, count - 1 + EXPERTS - 1)

    def rim_copy(target):
        return pltpu.make_async_remote_copy(
            src_ref=mixer_ref.at[pl.ds(tokens - 16, 16), :],
            dst_ref=rim,
            send_sem=rim_sems.at[0],
            recv_sem=rim_sems.at[1],
            device_id={"ctx": target},
            device_id_type=MESH,
        )

    @pl.when(me < count - 1)
    def _():
        rim_copy(me + 1).start()

    for t in range(tokens):
        b_wide[t] = jnp.broadcast_to(b_ref[:, t : t + 1], (STATES, LANES))
        c_wide[t] = jnp.broadcast_to(c_ref[:, t : t + 1], (STATES, LANES))

    def find_step(strip, carry):
        lanes = strip_lanes(strip)
        value = jnp.log(1.0 + jnp.exp(delta_ref[:, lanes].astype(f32) + delta_bias_ref[:, lanes]))
        step[:, lanes] = value
        spans[:, lanes] = jnp.sum(value, axis=0, keepdims=True)
        return carry

    lax.fori_loop(0, strips, find_step, 0)

    @pl.when(me > 0)
    def _():
        rim_copy(me).wait_recv()

    @pl.when(me == 0)
    def _():
        rim[...] = tail_ref[...]

    def rates(lanes):
        return -jnp.exp(decay_ref[:, lanes]) * LOG2E

    def advance(rate, state, steps, drives, i, b_column):
        return tuple(
            jnp.exp2(r * s) * h + b_column * d
            for r, s, h, d in zip(
                rate, lane_parts(steps[i : i + 1]), state, lane_parts(drives[i : i + 1])
            )
        )

    def prepare(strip, carry):
        lanes = strip_lanes(strip)
        padded[0:8] = rim[:, lanes].astype(f32)[8:16]
        padded[8 : 8 + tokens] = mixer_ref[:, lanes].astype(f32)
        convolved = bias_ref[:, lanes]
        for k in range(4):
            convolved = convolved + taps_ref[k : k + 1, lanes] * padded[5 + k : 5 + k + tokens]
        value = convolved / (1.0 + jnp.exp(-convolved))
        act[:, lanes] = value
        drive[:, lanes] = value * step[:, lanes]
        rate = lane_parts(rates(lanes))

        def group(number, state):
            base = pl.multiple_of(number * 8, 8)
            steps, drives = step[pl.ds(base, 8), lanes], drive[pl.ds(base, 8), lanes]
            for i in range(8):
                state = advance(rate, state, steps, drives, i, b_wide[base + i])
            return state

        zero = jnp.zeros((STATES, LANES), f32)
        state = lax.fori_loop(0, tokens // 8, group, (zero,) * (STRIP // LANES))
        ends[:, lanes] = jnp.concatenate(state, axis=1).astype(ends.dtype)
        return carry

    lax.fori_loop(0, strips, prepare, 0)

    def end_copies(stage, k, place, target):
        pairs = ((ends, line_ends), (spans, line_spans))
        return [
            pltpu.make_async_remote_copy(
                src_ref=mine,
                dst_ref=whole.at[stage, place],
                send_sem=end_sems.at[0, stage, k - 1, part],
                recv_sem=end_sems.at[1, stage, k - 1, part],
                device_id={"ctx": target},
                device_id_type=MESH,
            )
            for part, (mine, whole) in enumerate(pairs)
        ]

    leaving = []
    for k in range(1, SIDE):
        leaving += end_copies(0, k, y, index(0, 0, k))
    for one in leaving:
        one.start()
    line_ends[0, y] = ends[...]
    line_spans[0, y] = spans[...]
    for k in range(1, SIDE):
        for one in end_copies(0, k, lax.rem(y + SIDE - k, SIDE), me):
            one.wait_recv()
    for one in leaving:
        one.wait_send()

    def follow(stage):
        def one(strip, source, state):
            lanes = strip_lanes(strip)
            return (
                jnp.exp2(rates(lanes) * line_spans[stage, source, :, lanes]) * state
                + line_ends[stage, source, :, lanes].astype(f32)
            )

        return one

    def line_end(strip, carry):
        lanes = strip_lanes(strip)
        state = lax.fori_loop(
            0, SIDE, functools.partial(follow(0), strip), jnp.zeros((STATES, STRIP), f32)
        )
        ends[:, lanes] = state.astype(ends.dtype)
        spans[:, lanes] = sum(line_spans[0, source, :, lanes] for source in range(SIDE))
        return carry

    lax.fori_loop(0, strips, line_end, 0)
    for k in range(1, SIDE):

        @pl.when(x + k < SIDE)
        def _():
            for one in end_copies(1, k, x, (x + k) * SIDE + y):
                one.start()

    for k in range(1, SIDE):

        @pl.when(x >= k)
        def _():
            for one in end_copies(1, k, x - k, me):
                one.wait_recv()

    in_flight = []

    def moved(half, line, kind, first, second, part, towards, target):
        def rows(a, b):
            where = (a, b) if half == 0 else (b, a)
            where = tuple((v + 1) % SIDE - 1 for v in where)
            start, size = (0, tokens) if part is None else (part * (tokens // 2), tokens // 2)
            return rows_all.at[half, pl.ds(SLOTS.index(where) * tokens + start, size), :]

        return pltpu.make_async_remote_copy(
            src_ref=rows(first, second),
            dst_ref=rows(first - towards[0], second - towards[1]),
            send_sem=gather_sems.at[0, half, line, kind],
            recv_sem=gather_sems.at[1, half, line, kind],
            device_id={"ctx": target},
            device_id_type=MESH,
        )

    def send(half, line, kind, first, second, part, towards):
        one = moved(half, line, kind, first, second, part, towards, index(half, *towards))
        one.start()
        in_flight.append(one)

    def arrived(half, line, kind, first, second, part):
        moved(half, line, kind, first, second, part, (0, 0), me).wait_recv()

    def send_line(half, first):
        send(half, LINES[first], 0, first, 0, None, (0, 1))
        send(half, LINES[first], 1, first, 0, None, (0, -1))

    def pass_on(half, first):
        arrived(half, LINES[first], 0, first, -1, None)
        send(half, LINES[first], 2, first, -1, 0, (0, 1))
        arrived(half, LINES[first], 1, first, 1, None)
        send(half, LINES[first], 3, first, 1, 1, (0, -1))

    def last_of(half, first):
        arrived(half, LINES[first], 2, first, 2, 0)
        arrived(half, LINES[first], 3, first, 2, 1)

    per_half = strips // 2

    def scan(half, strip, carry):
        lanes = strip_lanes(half * per_half + strip)
        rate = lane_parts(rates(lanes))
        state = prefix_ref[:, lanes]
        state = lax.fori_loop(
            0, x, functools.partial(follow(1), half * per_half + strip), state
        )
        state = lax.fori_loop(
            0, y, functools.partial(follow(0), half * per_half + strip), state
        )

        def group(number, state):
            base = pl.multiple_of(number * 8, 8)
            steps, drives = step[pl.ds(base, 8), lanes], drive[pl.ds(base, 8), lanes]
            found = []
            for i in range(8):
                state = advance(rate, state, steps, drives, i, b_wide[base + i])
                c_column = c_wide[base + i]
                found.append(
                    jnp.concatenate(
                        [jnp.sum(c_column * h, axis=0, keepdims=True) for h in state], axis=1
                    )
                )
            summed[pl.ds(base, 8), :] = jnp.concatenate(found, axis=0)
            return state

        lax.fori_loop(0, tokens // 8, group, lane_parts(state))
        gate = gate_ref[:, lanes].astype(f32)
        mixed = summed[...] + gain_ref[:, lanes] * act[:, lanes]
        rows_all[half, 0:tokens, strip_lanes(strip)] = (
            mixed * (gate / (1.0 + jnp.exp(-gate)))
        ).astype(rows_all.dtype)
        return carry

    for half in (0, 1):
        lax.fori_loop(0, per_half, functools.partial(scan, half), 0)
        send(half, RING, 0, 0, 0, None, (1, 0))
        send(half, RING, 1, 0, 0, None, (-1, 0))
        send_line(half, 0)

    width = weight.shape[1]
    half_channels = channels // 2

    def pair_copy(column, part, target):
        rows = pl.ds(pl.multiple_of(part * tokens, tokens), tokens)
        return pltpu.make_async_remote_copy(
            src_ref=parts.at[1 - core, column, rows, :],
            dst_ref=got.at[column, rows, :],
            send_sem=pair_sems.at[0, column, part],
            recv_sem=pair_sems.at[1, column, part],
            device_id={"exp": target},
            device_id_type=MESH,
        )

    sibling = own + 1 - 2 * core

    def project(where, number, first_slot):
        together = min(number, 2)

        def one(pair, carry):
            rows = pl.ds(pl.multiple_of((first_slot + pair * together) * tokens, tokens), together * tokens)
            value = jnp.dot(
                rows_all[0, rows, :], weight[0:half_channels], preferred_element_type=f32
            ) + jnp.dot(
                rows_all[1, rows, :], weight[half_channels:], preferred_element_type=f32
            )
            for k in range(together):
                dx, dy = where(pair * together + k)
                column = lax.rem(x + dx + SIDE, SIDE)
                line = lax.rem(y + dy + SIDE, SIDE)
                owner, part = line // 2, line % 2
                parts[owner, column, pl.ds(pl.multiple_of(part * tokens, tokens), tokens), :] = value[
                    k * tokens : (k + 1) * tokens
                ].astype(parts.dtype)

                @pl.when(owner != core)
                def _():
                    pair_copy(column, part, sibling).start()

            return carry

        lax.fori_loop(0, number // together, one, 0)

    load.wait()
    project(single(0, 0), 1, 0)
    for half in (0, 1):
        arrived(half, RING, 0, -1, 0, None)
        send(half, RING, 2, -1, 0, 0, (1, 0))
        arrived(half, RING, 1, 1, 0, None)
        send(half, RING, 3, 1, 0, 1, (-1, 0))
        send_line(half, -1)
        send_line(half, 1)
    for half in (0, 1):
        pass_on(half, 0)
    project(beside, 4, 1)
    for half in (0, 1):
        arrived(half, RING, 2, 2, 0, 0)
        arrived(half, RING, 3, 2, 0, 1)
        send_line(half, 2)
    for half in (0, 1):
        last_of(half, 0)
    project(across_ring, 2, 5)
    for first in (-1, 1):
        for half in (0, 1):
            pass_on(half, first)
    project(corner, 4, 7)
    for half in (0, 1):
        pass_on(half, 2)
    for first in (-1, 1):
        for half in (0, 1):
            last_of(half, first)
    project(knight, 4, 11)
    for half in (0, 1):
        last_of(half, 2)
    project(single(2, 2), 1, 15)

    def column_at(offset):
        return lax.rem(z + offset + SIDE, SIDE)

    def pair_sum(offset):
        column = column_at(offset)
        for part in (0, 1):
            pair_copy(column, part, own).wait_recv()
        value = parts[core, column].astype(f32) + got[column].astype(f32)
        return value

    def settle(offset):
        parts[core, column_at(offset)] = pair_sum(offset).astype(parts.dtype)

    summing = []

    def sum_copy(kind, offset, target):
        size = tokens
        rows = pl.ds(0, 2 * size) if kind < 2 else pl.ds((kind - 2) * size, size)
        return pltpu.make_async_remote_copy(
            src_ref=parts.at[core, column_at(offset), rows, :],
            dst_ref=landed.at[min(kind, 2), rows, :],
            send_sem=sum_sems.at[0, kind],
            recv_sem=sum_sems.at[1, kind],
            device_id={"exp": target},
            device_id_type=MESH,
        )

    def give(kind, offset):
        step_z = 1 if kind % 2 == 0 else -1
        one = sum_copy(kind, offset, column_at(step_z) * 2 + core)
        one.start()
        summing.append(one)

    settle(2)
    give(2, 2)
    give(3, 2)
    settle(1)
    settle(-1)
    for kind, offset in ((2, 1), (3, -1)):
        sum_copy(kind, 0, own).wait_recv()
        rows = pl.ds((kind - 2) * tokens, tokens)
        column = column_at(offset)
        parts[core, column, rows, :] = (
            parts[core, column, rows, :].astype(f32) + landed[2, rows, :].astype(f32)
        ).astype(parts.dtype)
        give(kind - 2, offset)
    value = pair_sum(0) + residual_ref[...].astype(f32)
    for kind in (0, 1):
        sum_copy(kind, 0, own).wait_recv()
    value = value + landed[0].astype(f32) + landed[1].astype(f32)
    value = value.astype(out_ref.dtype)
    out_ref[...] = value
    value = value.astype(f32)
    value = value * value
    ones = jnp.ones((16, width), jnp.bfloat16)
    found = jnp.zeros((16, value.shape[0]), f32)
    for _ in range(3):
        term = value.astype(jnp.bfloat16)
        value = value - term.astype(f32)
        found = found + lax.dot_general(
            ones, term, (((1,), (1,)), ((), ())), preferred_element_type=f32
        )
    squares_ref[...] = found[0:8]

    @pl.when(me < count - 1)
    def _():
        rim_copy(me + 1).wait_send()

    for k in range(1, SIDE):

        @pl.when(x + k < SIDE)
        def _():
            for one in end_copies(1, k, x, (x + k) * SIDE + y):
                one.wait_send()

    for column in range(SIDE):
        for part in (0, 1):
            pair_copy(column, part, sibling).wait_send()
    for one in in_flight + summing:
        one.wait_send()


def mixer(
    mixer_in, gate_in, delta_in, b_proj, c_proj, conv_kernel, conv_bias, delta_bias, decay_log,
    skip_gain, prefix_state, prefix_tail, out_proj, residual,
):
    tokens, channels = mixer_in.shape
    rows, width = residual.shape
    count = SIDE * SIDE
    tail = jnp.concatenate(
        [jnp.zeros((16 - prefix_tail.shape[0], channels), prefix_tail.dtype), prefix_tail]
    )
    here = pl.BlockSpec(memory_space=pltpu.VMEM)
    away = pl.BlockSpec(memory_space=pl.ANY)
    bf16, f32 = jnp.bfloat16, jnp.float32
    return pl.pallas_call(
        mixer_kernel,
        out_shape=(
            jax.ShapeDtypeStruct((rows, width), bf16),
            jax.ShapeDtypeStruct((8, rows), f32),
        ),
        in_specs=[here] * 12 + [away, here],
        out_specs=(here, here),
        scratch_shapes=[
            pltpu.VMEM((16, channels), bf16),
            pltpu.VMEM((8 + tokens, STRIP), f32),
            pltpu.VMEM((tokens, channels), f32),
            pltpu.VMEM((tokens, channels), f32),
            pltpu.VMEM((tokens, channels), f32),
            pltpu.VMEM((tokens, STRIP), f32),
            pltpu.VMEM((tokens, STATES, LANES), f32),
            pltpu.VMEM((tokens, STATES, LANES), f32),
            pltpu.VMEM((STATES, channels), bf16),
            pltpu.VMEM((1, channels), f32),
            pltpu.VMEM((2, SIDE, STATES, channels), bf16),
            pltpu.VMEM((2, SIDE, 1, channels), f32),
            pltpu.VMEM((2, count * tokens, channels // 2), bf16),
            pltpu.VMEM((channels, width), bf16),
            pltpu.VMEM((2, SIDE, rows, width), bf16),
            pltpu.VMEM((SIDE, rows, width), bf16),
            pltpu.VMEM((3, rows, width), bf16),
            pltpu.SemaphoreType.DMA((2,)),
            pltpu.SemaphoreType.DMA((2, 2, SIDE - 1, 2)),
            pltpu.SemaphoreType.DMA((2, 2, 5, 4)),
            pltpu.SemaphoreType.DMA((2, SIDE, 2)),
            pltpu.SemaphoreType.DMA((2, 4)),
            pltpu.SemaphoreType.DMA,
        ],
        compiler_params=pltpu.CompilerParams(
            collective_id=1, has_side_effects=True, vmem_limit_bytes=56 * 1024 * 1024
        ),
        name="mixer",
    )(
        mixer_in, gate_in, delta_in, b_proj, c_proj, conv_kernel, conv_bias[None], delta_bias[None],
        decay_log, skip_gain[None], prefix_state, tail, out_proj, residual,
    )


def expert_kernel(
    capacity, features,
    mixer_ref, squares_ref, pick_ref, place_ref, route_ref, gain_ref, gate_ref, up_ref, down_ref,
    out_ref,
    blocks, landed, wide, down, total, hidden, outgoing, answer, returned, all_squares,
    square_sems, dispatch_sems, return_sems, gather_sems, sum_sems, weight_sems,
):
    torus = Torus()
    me, index = torus.me, torus.index
    own_expert = lax.axis_index("exp")
    slots, width = answer.shape
    units = down.shape[0]
    count = SIDE * SIDE

    weights = [
        pltpu.make_async_copy(gate_ref.at[0], wide.at[:, pl.ds(0, units)], weight_sems.at[0]),
        pltpu.make_async_copy(up_ref.at[0], wide.at[:, pl.ds(units, units)], weight_sems.at[1]),
        pltpu.make_async_copy(down_ref.at[0], down, weight_sems.at[2]),
    ]
    for one in weights:
        one.start()

    barrier = pltpu.get_barrier_semaphore()
    for k in range(1, count):
        pl.semaphore_signal(
            barrier, inc=1, device_id={"ctx": lax.rem(me + k, count)}, device_id_type=MESH
        )
    for k in range(1, EXPERTS):
        pl.semaphore_signal(
            barrier, inc=1, device_id={"exp": lax.rem(own_expert + k, EXPERTS)}, device_id_type=MESH
        )
    pl.semaphore_wait(barrier, count - 1 + EXPERTS - 1)

    square_copies = []
    for k in range(1, count):
        square_copies.append(
            pltpu.make_async_remote_copy(
                src_ref=squares_ref,
                dst_ref=all_squares.at[me],
                send_sem=square_sems.at[0, k - 1],
                recv_sem=square_sems.at[1, k - 1],
                device_id={"ctx": lax.rem(me + k, count)},
                device_id_type=MESH,
            )
        )
        square_copies[-1].start()
    all_squares[me] = squares_ref[...]
    for k in range(1, count):
        source = lax.rem(me + count - k, count)
        pltpu.make_async_remote_copy(
            src_ref=squares_ref,
            dst_ref=all_squares.at[source],
            send_sem=square_sems.at[0, k - 1],
            recv_sem=square_sems.at[1, k - 1],
            device_id={"ctx": me},
            device_id_type=MESH,
        ).wait_recv()
    scale = lax.rsqrt(jnp.sum(all_squares[...], axis=0)[0:1] / features + 1e-05)

    def pick(chunk, carry):
        rows = pl.ds(pl.multiple_of(chunk * capacity, 16), capacity)
        chosen = pick_ref[rows, :]
        picked = jnp.dot(chosen, mixer_ref[...], preferred_element_type=jnp.float32)
        chosen = chosen.astype(jnp.float32)
        row_scale = jnp.sum(chosen * scale, axis=1, keepdims=True)
        outgoing[rows, :] = (picked * row_scale * gain_ref[...]).astype(outgoing.dtype)
        return carry

    lax.fori_loop(0, EXPERTS, pick, 0)

    def expert_rows(expert):
        return pl.ds(pl.multiple_of(expert * capacity, 16), capacity)

    def across(sems, source, target_ref):
        started = []
        for k in range(1, EXPERTS):
            peer = lax.rem(own_expert + k, EXPERTS)
            started.append(
                pltpu.make_async_remote_copy(
                    src_ref=source.at[expert_rows(peer), :],
                    dst_ref=target_ref.at[expert_rows(own_expert), :],
                    send_sem=sems.at[0, k - 1],
                    recv_sem=sems.at[1, k - 1],
                    device_id={"exp": peer},
                    device_id_type=MESH,
                )
            )
            started[-1].start()
        target_ref[expert_rows(own_expert), :] = source[expert_rows(own_expert), :]
        for k in range(1, EXPERTS):
            origin = lax.rem(own_expert + EXPERTS - k, EXPERTS)
            pltpu.make_async_remote_copy(
                src_ref=source.at[expert_rows(origin), :],
                dst_ref=target_ref.at[expert_rows(origin), :],
                send_sem=sems.at[0, k - 1],
                recv_sem=sems.at[1, k - 1],
                device_id={"exp": own_expert},
                device_id_type=MESH,
            ).wait_recv()
        return started

    crossing = across(dispatch_sems, outgoing, blocks.at[me])

    in_flight = {}

    def moved(half, line, kind, first, second, part, target):
        start, size = span(slots, half, part)
        ref = blocks.at[index(half, first, second), pl.ds(start, size), :]
        return pltpu.make_async_remote_copy(
            src_ref=ref,
            dst_ref=ref,
            send_sem=gather_sems.at[0, half, line, kind],
            recv_sem=gather_sems.at[1, half, line, kind],
            device_id={"ctx": target},
            device_id_type=MESH,
        )

    def send(half, line, kind, first, second, part, towards):
        one = moved(half, line, kind, first, second, part, index(half, *towards))
        one.start()
        where = (first, second) if half == 0 else (second, first)
        in_flight.setdefault(where, []).append(one)

    def arrived(half, line, kind, first, second, part):
        moved(half, line, kind, first, second, part, me).wait_recv()

    def send_line(half, first):
        send(half, LINES[first], 0, first, 0, None, (0, 1))
        send(half, LINES[first], 1, first, 0, None, (0, -1))

    def pass_on(half, first):
        arrived(half, LINES[first], 0, first, -1, None)
        send(half, LINES[first], 2, first, -1, 0, (0, 1))
        arrived(half, LINES[first], 1, first, 1, None)
        send(half, LINES[first], 3, first, 1, 1, (0, -1))

    def last_of(half, first):
        arrived(half, LINES[first], 2, first, 2, 0)
        arrived(half, LINES[first], 3, first, 2, 1)

    row_tile = slots // 2

    def over_blocks(where, number, body):
        def one(step, carry):
            block, tile = step // 2, step % 2
            dx, dy = where(block)
            owner = index(0, dx, dy)
            body(owner, pl.ds(pl.multiple_of(tile * row_tile, 16), row_tile))
            return carry

        lax.fori_loop(0, number * 2, one, 0)

    def grow(owner, rows):
        part = wide[pl.ds(pl.multiple_of(owner * width, 16), width), :]
        total[rows, :] += jnp.dot(blocks[owner, rows, :], part, preferred_element_type=jnp.float32)

    for half in (0, 1):
        send(half, RING, 0, 0, 0, None, (1, 0))
        send(half, RING, 1, 0, 0, None, (-1, 0))
    for half in (0, 1):
        send_line(half, 0)
    total[...] = jnp.zeros_like(total)
    for one in weights:
        one.wait()
    over_blocks(single(0, 0), 1, grow)
    for half in (0, 1):
        arrived(half, RING, 0, -1, 0, None)
        send(half, RING, 2, -1, 0, 0, (1, 0))
        arrived(half, RING, 1, 1, 0, None)
        send(half, RING, 3, 1, 0, 1, (-1, 0))
    for half in (0, 1):
        send_line(half, -1)
        send_line(half, 1)
    for half in (0, 1):
        pass_on(half, 0)
    over_blocks(beside, 4, grow)
    for half in (0, 1):
        arrived(half, RING, 2, 2, 0, 0)
        arrived(half, RING, 3, 2, 0, 1)
        send_line(half, 2)
    for half in (0, 1):
        last_of(half, 0)
    over_blocks(across_ring, 2, grow)
    for first in (-1, 1):
        for half in (0, 1):
            pass_on(half, first)
    over_blocks(corner, 4, grow)
    for half in (0, 1):
        pass_on(half, 2)
    for first in (-1, 1):
        for half in (0, 1):
            last_of(half, first)
    over_blocks(knight, 4, grow)
    for half in (0, 1):
        last_of(half, 2)
    over_blocks(single(2, 2), 1, grow)

    def activate(step, carry):
        rows = pl.ds(pl.multiple_of(step * capacity, 16), capacity)
        gate = total[rows, 0:units]
        hidden[rows, :] = (gate / (1.0 + jnp.exp(-gate)) * total[rows, units : 2 * units]).astype(
            hidden.dtype
        )
        return carry

    lax.fori_loop(0, EXPERTS, activate, 0)

    def project(owner, rows):
        part = down[:, pl.ds(pl.multiple_of(owner * width, LANES), width)]
        blocks[owner, rows, :] = jnp.dot(
            hidden[rows, :], part, preferred_element_type=jnp.float32
        ).astype(blocks.dtype)

    def fill(places, where):
        for place in places:
            for one in in_flight.pop(place, ()):
                one.wait_send()
        over_blocks(where, len(places), project)

    summing = []

    def part_rows(half, part):
        start, size = span(slots, half, part)
        return pl.ds(start, size)

    def landing(half, line, kind):
        if kind < 2:
            return landed.at[half, line, kind]
        size = slots // 4
        return landed.at[half, line, 2, pl.ds((kind - 2) * size, size), :]

    def sum_copy(half, line, kind, first, second, part, target):
        return pltpu.make_async_remote_copy(
            src_ref=blocks.at[index(half, first, second), part_rows(half, part), :],
            dst_ref=landing(half, line, kind),
            send_sem=sum_sems.at[0, half, line, kind],
            recv_sem=sum_sems.at[1, half, line, kind],
            device_id={"ctx": target},
            device_id_type=MESH,
        )

    def give(half, line, kind, first, second, part):
        step = 1 if kind % 2 == 0 else -1
        target = index(half, step, 0) if line == RING else index(half, 0, step)
        one = sum_copy(half, line, kind, first, second, part, target)
        one.start()
        summing.append(one)

    def taken(half, line, kind):
        part = None if kind < 2 else kind - 2
        sum_copy(half, line, kind, 0, 0, part, me).wait_recv()

    def add(half, first, second, part, line, kinds, target=None):
        for kind in kinds:
            taken(half, line, kind)
        start, size = span(slots, half, part)
        owner = index(half, first, second)
        tile = 96

        def one(step, carry):
            offset = pl.multiple_of(step * tile, 16)
            rows = pl.ds(pl.multiple_of(start + offset, 16), tile)
            value = blocks[owner, rows, :].astype(jnp.float32)
            for kind in kinds:
                value = value + landing(half, line, kind)[pl.ds(offset, tile), :].astype(jnp.float32)
            value = value.astype(blocks.dtype)
            if target is None:
                blocks[owner, rows, :] = value
            else:
                target[rows, :] = value
            return carry

        lax.fori_loop(0, size // tile, one, 0)

    def at(line, offset):
        return (offset, 0) if line == RING else ({v: k for k, v in LINES.items()}[line], offset)

    def begin(half, line):
        give(half, line, 2, *at(line, 2), 0)
        give(half, line, 3, *at(line, 2), 1)

    def middle(half, line):
        add(half, *at(line, 1), 0, line, (2,))
        give(half, line, 0, *at(line, 1), None)
        add(half, *at(line, -1), 1, line, (3,))
        give(half, line, 1, *at(line, -1), None)

    def finish(half, line, target=None):
        add(half, *at(line, 0), None, line, (0, 1), target)

    halves = (0, 1)
    fill([(2, 2)], single(2, 2))
    for half in halves:
        begin(half, LINES[2])
    fill([(1, 2), (-1, 2), (2, 1), (2, -1)], knight)
    for first in (1, -1):
        for half in halves:
            begin(half, LINES[first])
    fill([(2, 0), (0, 2)], across_ring)
    for half in halves:
        begin(half, LINES[0])
    for half in halves:
        middle(half, LINES[2])
    fill([(1, 1), (-1, 1), (1, -1), (-1, -1)], corner)
    for first in (1, -1):
        for half in halves:
            middle(half, LINES[first])
    fill([(1, 0), (-1, 0), (0, 1), (0, -1)], beside)
    for half in halves:
        middle(half, LINES[0])
    for one in crossing:
        one.wait_send()
    fill([(0, 0)], single(0, 0))
    for half in halves:
        finish(half, LINES[2])
        begin(half, RING)
    for first in (1, -1):
        for half in halves:
            finish(half, LINES[first])
    for half in halves:
        middle(half, RING)
    for half in halves:
        finish(half, LINES[0])
    for half in halves:
        finish(half, RING, answer)

    back = across(return_sems, answer, returned)
    rows = mixer_ref.shape[0]
    value = mixer_ref[...].astype(jnp.float32)
    for k in range(route_ref.shape[1]):
        value = value + route_ref[:, k : k + 1] * jnp.dot(
            place_ref[k], returned[...], preferred_element_type=jnp.float32
        )
    out_ref[...] = value.astype(out_ref.dtype)
    for one in summing + back + square_copies:
        one.wait_send()


def expert_layer(
    mixer_out, squares, pick, place, route_gates, gain, expert_gate, expert_up, expert_down, capacity
):
    rows, width = mixer_out.shape
    features, units = expert_gate.shape[1:]
    slots = EXPERTS * capacity
    count = SIDE * SIDE
    here = pl.BlockSpec(memory_space=pltpu.VMEM)
    away = pl.BlockSpec(memory_space=pl.ANY)
    bf16, f32 = jnp.bfloat16, jnp.float32
    return pl.pallas_call(
        functools.partial(expert_kernel, capacity, features),
        out_shape=jax.ShapeDtypeStruct((rows, width), bf16),
        in_specs=[here] * 6 + [away] * 3,
        out_specs=here,
        scratch_shapes=[
            pltpu.VMEM((count, slots, width), bf16),
            pltpu.VMEM((2, 5, 3, slots // 2, width), bf16),
            pltpu.VMEM((features, 2 * units), bf16),
            pltpu.VMEM((units, features), bf16),
            pltpu.VMEM((slots, 2 * units), f32),
            pltpu.VMEM((slots, units), bf16),
            pltpu.VMEM((slots, width), bf16),
            pltpu.VMEM((slots, width), bf16),
            pltpu.VMEM((slots, width), bf16),
            pltpu.VMEM((count,) + squares.shape, f32),
            pltpu.SemaphoreType.DMA((2, count - 1)),
            pltpu.SemaphoreType.DMA((2, EXPERTS - 1)),
            pltpu.SemaphoreType.DMA((2, EXPERTS - 1)),
            pltpu.SemaphoreType.DMA((2, 2, 5, 4)),
            pltpu.SemaphoreType.DMA((2, 2, 5, 4)),
            pltpu.SemaphoreType.DMA((3,)),
        ],
        compiler_params=pltpu.CompilerParams(
            collective_id=3, has_side_effects=True, vmem_limit_bytes=56 * 1024 * 1024
        ),
        name="expert_layer",
    )(mixer_out, squares, pick, place, route_gates, gain, expert_gate, expert_up, expert_down)


def shards(
    mixer_in,
    gate_in,
    delta_in,
    b_proj,
    c_proj,
    conv_kernel,
    conv_bias,
    delta_bias,
    decay_log,
    skip_gain,
    prefix_state,
    prefix_tail,
    out_proj,
    residual,
    norm_gain,
    expert_gate,
    expert_up,
    expert_down,
    expert_ids,
    route_gates,
):
    mixer_out, squares = mixer(
        mixer_in, gate_in, delta_in, b_proj, c_proj, conv_kernel, conv_bias, delta_bias, decay_log,
        skip_gain, prefix_state, prefix_tail, out_proj, residual,
    )
    block_rows = residual.shape[0]
    experts = expert_gate.shape[0] * lax.axis_size("exp")
    top_count = expert_ids.shape[1]
    capacity = 3 * block_rows * top_count // (2 * experts)
    flat_choice = expert_ids.reshape(-1)
    owner_hot = (flat_choice[:, None] == jnp.arange(experts, dtype=jnp.int32)[None, :]).astype(
        jnp.int32
    )
    earlier_count = jnp.cumsum(owner_hot, axis=0) - owner_hot
    slot_index = jnp.sum(earlier_count * owner_hot, axis=1)
    target = (flat_choice * capacity + slot_index).reshape(block_rows, top_count)
    every_slot = jnp.arange(experts * capacity, dtype=jnp.int32)
    place = (target.T[:, :, None] == every_slot[None, None, :]).astype(jnp.bfloat16)
    pick = jnp.any(target[None, :, :] == every_slot[:, None, None], axis=2).astype(jnp.bfloat16)
    block_out = expert_layer(
        mixer_out, squares, pick, place, route_gates, norm_gain[None],
        expert_gate, expert_up, expert_down, capacity,
    )
    return (mixer_out, block_out)


def solution(mesh):
    placed = (
        P("ctx", "exp"),
        P("ctx", "exp"),
        P("ctx", "exp"),
        P(None, "ctx"),
        P(None, "ctx"),
        P(None, "exp"),
        P("exp"),
        P("exp"),
        P(None, "exp"),
        P("exp"),
        P(None, "exp"),
        P(None, "exp"),
        P("exp", "ctx"),
        P("exp", "ctx"),
        P("ctx"),
        P("exp", None, "ctx"),
        P("exp", None, "ctx"),
        P("exp", "ctx", None),
        P("exp", None),
        P("exp", None),
    )
    return jax.shard_map(
        shards,
        mesh=mesh,
        in_specs=placed,
        out_specs=(P("exp", "ctx"), P("exp", "ctx")),
        check_vma=False,
    )
```

```python
import functools
import math

import jax
import jax.numpy as jnp
from jax import lax
from jax.experimental import pallas as pl
from jax.experimental.pallas import tpu as pltpu
from jax.sharding import PartitionSpec as P

SIDE = 4
STATES = 16
LANES = 128
STRIP = 512
LOG2E = math.log2(math.e)
MESH = pl.DeviceIdType.MESH


EXPERTS = 8
LINES = {0: 0, -1: 1, 1: 2, 2: 3}
RING = 4


class Torus:
    def __init__(self):
        me = lax.axis_index("ctx")
        self.me = me
        self.place = (me // SIDE, me % SIDE)

    def index(self, half, first, second):
        a = lax.rem(self.place[half] + first + 2 * SIDE, SIDE)
        b = lax.rem(self.place[1 - half] + second + 2 * SIDE, SIDE)
        return a * SIDE + b if half == 0 else b * SIDE + a


PEERS = ((1, 0), (1, 1), (2, 0), (2, 1), (0, 0), (0, 1), (-1, 0), (-1, 1))
OWN = 4
UNITS = (0, 1, 2, 3)


def span(rows, unit, part=None):
    size = rows // len(UNITS)
    return (unit * size, size) if part is None else (unit * size + part * (size // 2), size // 2)


SLOTS = (
    (0, 0),
    (1, 0), (-1, 0), (0, 1), (0, -1),
    (2, 0), (0, 2),
    (1, 1), (-1, 1), (1, -1), (-1, -1),
    (1, 2), (-1, 2), (2, 1), (2, -1),
    (2, 2),
)


def lane_parts(value):
    return tuple(value[:, k * LANES : (k + 1) * LANES] for k in range(value.shape[1] // LANES))


def sign(i):
    return 1 - 2 * (i % 2)


def beside(i):
    return sign(i) * (1 - i // 2), sign(i) * (i // 2)


def across_ring(i):
    return 2 * (1 - i), 2 * i


def corner(i):
    return sign(i), 1 - 2 * (i // 2)


def knight(i):
    along = i // 2
    return sign(i) * (1 - along) + 2 * along, 2 * (1 - along) + sign(i) * along


def single(dx, dy):
    return lambda i: (dx, dy)


def mixer_kernel(
    mixer_ref, gate_ref, delta_ref, b_ref, c_ref, taps_ref, bias_ref, delta_bias_ref, decay_ref,
    gain_ref, prefix_ref, tail_ref, weight_ref, residual_ref,
    out_ref, squares_ref,
    rim, padded, act, step, drive, summed, b_wide, c_wide, ends, spans, line_ends, line_spans,
    rows_all, weight, parts, got, landed, home,
    rim_sems, end_sems, gather_sems, pair_sems, sum_send_sems, sum_sems, weight_sem,
):
    torus = Torus()
    me, index = torus.me, torus.index
    x, y = torus.place
    own = lax.axis_index("exp")
    z, core = own // 2, own % 2
    count = SIDE * SIDE
    tokens, channels = mixer_ref.shape
    strips = channels // STRIP
    f32 = jnp.float32

    def strip_lanes(strip):
        return pl.ds(pl.multiple_of(strip * STRIP, STRIP), STRIP)

    load = pltpu.make_async_copy(weight_ref, weight, weight_sem)
    load.start()
    barrier = pltpu.get_barrier_semaphore()
    for k in range(1, count):
        pl.semaphore_signal(
            barrier, inc=1, device_id={"ctx": lax.rem(me + k, count)}, device_id_type=MESH
        )
    for k in range(1, EXPERTS):
        pl.semaphore_signal(
            barrier, inc=1, device_id={"exp": lax.rem(own + k, EXPERTS)}, device_id_type=MESH
        )
    pl.semaphore_wait(barrier, count - 1 + EXPERTS - 1)

    def rim_copy(target):
        return pltpu.make_async_remote_copy(
            src_ref=mixer_ref.at[pl.ds(tokens - 16, 16), :],
            dst_ref=rim,
            send_sem=rim_sems.at[0],
            recv_sem=rim_sems.at[1],
            device_id={"ctx": target},
            device_id_type=MESH,
        )

    @pl.when(me < count - 1)
    def _():
        rim_copy(me + 1).start()

    for t in range(tokens):
        b_wide[t] = jnp.broadcast_to(b_ref[:, t : t + 1], (STATES, LANES))
        c_wide[t] = jnp.broadcast_to(c_ref[:, t : t + 1], (STATES, LANES))

    def find_step(strip, carry):
        lanes = strip_lanes(strip)
        value = jnp.log(1.0 + jnp.exp(delta_ref[:, lanes].astype(f32) + delta_bias_ref[:, lanes]))
        step[:, lanes] = value
        spans[0, :, lanes] = jnp.sum(value, axis=0, keepdims=True)
        return carry

    lax.fori_loop(0, strips, find_step, 0)

    @pl.when(me > 0)
    def _():
        rim_copy(me).wait_recv()

    @pl.when(me == 0)
    def _():
        rim[...] = jnp.zeros_like(rim)

    def rates(lanes):
        return -jnp.exp(decay_ref[:, lanes]) * LOG2E

    def advance(rate, state, steps, drives, i, b_column):
        return tuple(
            jnp.exp2(r * s) * h + b_column * d
            for r, s, h, d in zip(
                rate, lane_parts(steps[i : i + 1]), state, lane_parts(drives[i : i + 1])
            )
        )

    def prepare(strip, carry):
        lanes = strip_lanes(strip)
        padded[0:8] = rim[:, lanes].astype(f32)[8:16]
        padded[8 : 8 + tokens] = mixer_ref[:, lanes].astype(f32)

        @pl.when(me == 0)
        def _():
            padded[5:8] = tail_ref[:, lanes].astype(f32)

        convolved = bias_ref[:, lanes]
        for k in range(4):
            convolved = convolved + taps_ref[k : k + 1, lanes] * padded[5 + k : 5 + k + tokens]
        value = convolved / (1.0 + jnp.exp(-convolved))
        act[:, lanes] = value
        drive[:, lanes] = value * step[:, lanes]
        rate = lane_parts(rates(lanes))

        def group(number, state):
            base = pl.multiple_of(number * 8, 8)
            steps, drives = step[pl.ds(base, 8), lanes], drive[pl.ds(base, 8), lanes]
            for i in range(8):
                state = advance(rate, state, steps, drives, i, b_wide[base + i])
            return state

        zero = jnp.zeros((STATES, LANES), f32)
        state = lax.fori_loop(0, tokens // 8, group, (zero,) * (STRIP // LANES))
        ends[0, :, lanes] = jnp.concatenate(state, axis=1).astype(ends.dtype)
        return carry

    half_channels = channels // 2
    per_half = strips // 2

    def end_copies(stage, half, k, place, target):
        lanes = pl.ds(half * half_channels, half_channels)
        pairs = ((ends, line_ends), (spans, line_spans))
        return [
            pltpu.make_async_remote_copy(
                src_ref=mine.at[stage, :, lanes],
                dst_ref=whole.at[stage, place, :, lanes],
                send_sem=end_sems.at[0, stage, half, k - 1, part],
                recv_sem=end_sems.at[1, stage, half, k - 1, part],
                device_id={"ctx": target},
                device_id_type=MESH,
            )
            for part, (mine, whole) in enumerate(pairs)
        ]

    def follow(stage, strip):
        lanes = strip_lanes(strip)

        def one(source, state):
            return (
                jnp.exp2(rates(lanes) * line_spans[stage, source, :, lanes]) * state
                + line_ends[stage, source, :, lanes].astype(f32)
            )

        return one

    def line_end(half, number, carry):
        strip = half * per_half + number
        lanes = strip_lanes(strip)
        state = lax.fori_loop(0, SIDE, follow(0, strip), jnp.zeros((STATES, STRIP), f32))
        ends[1, :, lanes] = state.astype(ends.dtype)
        spans[1, :, lanes] = sum(line_spans[0, source, :, lanes] for source in range(SIDE))
        return carry

    leaving = []
    for half in (0, 1):
        lax.fori_loop(half * per_half, (half + 1) * per_half, prepare, 0)
        lanes = pl.ds(half * half_channels, half_channels)
        for k in range(1, SIDE):
            leaving += end_copies(0, half, k, y, index(0, 0, k))
            for one in leaving[-2:]:
                one.start()
        line_ends[0, y, :, lanes] = ends[0, :, lanes]
        line_spans[0, y, :, lanes] = spans[0, :, lanes]
    for half in (0, 1):
        for k in range(1, SIDE):
            for one in end_copies(0, half, k, lax.rem(y + SIDE - k, SIDE), me):
                one.wait_recv()
        lax.fori_loop(0, per_half, functools.partial(line_end, half), 0)
        for k in range(1, SIDE):

            @pl.when(x + k < SIDE)
            def _():
                for one in end_copies(1, half, k, x, (x + k) * SIDE + y):
                    one.start()

    in_flight = []

    def moved(half, line, kind, first, second, part, towards, target):
        def rows(a, b):
            where = (a, b) if half == 0 else (b, a)
            where = tuple((v + 1) % SIDE - 1 for v in where)
            start, size = (0, tokens) if part is None else (part * (tokens // 2), tokens // 2)
            return rows_all.at[half, pl.ds(SLOTS.index(where) * tokens + start, size), :]

        return pltpu.make_async_remote_copy(
            src_ref=rows(first, second),
            dst_ref=rows(first - towards[0], second - towards[1]),
            send_sem=gather_sems.at[0, half, line, kind],
            recv_sem=gather_sems.at[1, half, line, kind],
            device_id={"ctx": target},
            device_id_type=MESH,
        )

    def send(half, line, kind, first, second, part, towards):
        one = moved(half, line, kind, first, second, part, towards, index(half, *towards))
        one.start()
        in_flight.append(one)

    def arrived(half, line, kind, first, second, part):
        moved(half, line, kind, first, second, part, (0, 0), me).wait_recv()

    def send_line(half, first):
        send(half, LINES[first], 0, first, 0, None, (0, 1))
        send(half, LINES[first], 1, first, 0, None, (0, -1))

    def pass_on(half, first):
        arrived(half, LINES[first], 0, first, -1, None)
        send(half, LINES[first], 2, first, -1, 0, (0, 1))
        arrived(half, LINES[first], 1, first, 1, None)
        send(half, LINES[first], 3, first, 1, 1, (0, -1))

    def last_of(half, first):
        arrived(half, LINES[first], 2, first, 2, 0)
        arrived(half, LINES[first], 3, first, 2, 1)

    def scan(half, strip, carry):
        lanes = strip_lanes(half * per_half + strip)
        rate = lane_parts(rates(lanes))
        state = prefix_ref[:, lanes]
        state = lax.fori_loop(0, x, follow(1, half * per_half + strip), state)
        state = lax.fori_loop(0, y, follow(0, half * per_half + strip), state)

        def group(number, state):
            base = pl.multiple_of(number * 8, 8)
            steps, drives = step[pl.ds(base, 8), lanes], drive[pl.ds(base, 8), lanes]
            found = []
            for i in range(8):
                state = advance(rate, state, steps, drives, i, b_wide[base + i])
                c_column = c_wide[base + i]
                found.append(
                    jnp.concatenate(
                        [jnp.sum(c_column * h, axis=0, keepdims=True) for h in state], axis=1
                    )
                )
            summed[pl.ds(base, 8), :] = jnp.concatenate(found, axis=0)
            return state

        lax.fori_loop(0, tokens // 8, group, lane_parts(state))
        gate = gate_ref[:, lanes].astype(f32)
        mixed = summed[...] + gain_ref[:, lanes] * act[:, lanes]
        rows_all[half, 0:tokens, strip_lanes(strip)] = (
            mixed * (gate / (1.0 + jnp.exp(-gate)))
        ).astype(rows_all.dtype)
        return carry

    for half in (0, 1):
        for k in range(1, SIDE):

            @pl.when(x >= k)
            def _():
                for one in end_copies(1, half, k, x - k, me):
                    one.wait_recv()

        lax.fori_loop(0, per_half, functools.partial(scan, half), 0)
        send(half, RING, 0, 0, 0, None, (1, 0))
        send(half, RING, 1, 0, 0, None, (-1, 0))
        send_line(half, 0)

    width = weight.shape[1]
    sibling = own + 1 - 2 * core

    def of_slot(where, number):
        dx, dy = where(number)
        line = lax.rem(y + dy + SIDE, SIDE)
        return lax.rem(x + dx + SIDE, SIDE), line // 2, line % 2

    def pair_copy(slot, target):
        return pltpu.make_async_remote_copy(
            src_ref=parts.at[slot],
            dst_ref=got.at[slot],
            send_sem=pair_sems.at[0, slot],
            recv_sem=pair_sems.at[1, slot],
            device_id={"exp": target},
            device_id_type=MESH,
        )

    def part_rows(part):
        return pl.ds(pl.multiple_of(part * tokens, tokens), tokens)

    def sum_copy(slot, column, part):
        behind = lax.rem(column - z + SIDE, SIDE) - 1
        return pltpu.make_async_remote_copy(
            src_ref=parts.at[slot],
            dst_ref=landed.at[behind, part_rows(part), :],
            send_sem=sum_send_sems.at[slot],
            recv_sem=sum_sems.at[behind, part],
            device_id={"exp": column * 2 + core},
            device_id_type=MESH,
        )

    def project(where, number, first_slot):
        together = min(number, 2)

        def one(pair, carry):
            first = first_slot + pair * together
            rows = pl.ds(pl.multiple_of(first * tokens, tokens), together * tokens)
            value = jnp.dot(
                rows_all[0, rows, :], weight[0:half_channels], preferred_element_type=f32
            ) + jnp.dot(
                rows_all[1, rows, :], weight[half_channels:], preferred_element_type=f32
            )
            for k in range(together):
                column, owner, part = of_slot(where, pair * together + k)
                parts[first + k] = value[k * tokens : (k + 1) * tokens].astype(parts.dtype)

                @pl.when(owner != core)
                def _():
                    pair_copy(first + k, sibling).start()

            return carry

        lax.fori_loop(0, number // together, one, 0)

    def settle(where, number, first_slot):
        def one(k, carry):
            slot = first_slot + k
            column, owner, part = of_slot(where, k)

            @pl.when(owner == core)
            def _():
                pair_copy(slot, own).wait_recv()
                value = parts[slot].astype(f32) + got[slot].astype(f32)

                @pl.when(column == z)
                def _():
                    home[part_rows(part), :] = value

                @pl.when(column != z)
                def _():
                    parts[slot] = value.astype(parts.dtype)
                    sum_copy(slot, column, part).start()

            return carry

        lax.fori_loop(0, number, one, 0)

    def clear(where, number, first_slot):
        def one(k, carry):
            slot = first_slot + k
            column, owner, part = of_slot(where, k)

            @pl.when(owner != core)
            def _():
                pair_copy(slot, sibling).wait_send()

            @pl.when((owner == core) & (column != z))
            def _():
                sum_copy(slot, column, part).wait_send()

            return carry

        lax.fori_loop(0, number, one, 0)

    load.wait()
    project(single(0, 0), 1, 0)
    for half in (0, 1):
        arrived(half, RING, 0, -1, 0, None)
        send(half, RING, 2, -1, 0, 0, (1, 0))
        arrived(half, RING, 1, 1, 0, None)
        send(half, RING, 3, 1, 0, 1, (-1, 0))
        send_line(half, -1)
        send_line(half, 1)
    for half in (0, 1):
        pass_on(half, 0)
    project(beside, 4, 1)
    settle(single(0, 0), 1, 0)
    for half in (0, 1):
        arrived(half, RING, 2, 2, 0, 0)
        arrived(half, RING, 3, 2, 0, 1)
        send_line(half, 2)
    for half in (0, 1):
        last_of(half, 0)
    project(across_ring, 2, 5)
    settle(beside, 4, 1)
    for first in (-1, 1):
        for half in (0, 1):
            pass_on(half, first)
    project(corner, 4, 7)
    settle(across_ring, 2, 5)
    for half in (0, 1):
        pass_on(half, 2)
    for first in (-1, 1):
        for half in (0, 1):
            last_of(half, first)
    project(knight, 4, 11)
    settle(corner, 4, 7)
    for half in (0, 1):
        last_of(half, 2)
    project(single(2, 2), 1, 15)
    settle(knight, 4, 11)

    settle(single(2, 2), 1, 15)
    value = home[...] + residual_ref[...].astype(f32)
    for behind in range(SIDE - 1):
        for part in (0, 1):
            rows = pl.ds(part * tokens, tokens)
            pltpu.make_async_remote_copy(
                src_ref=landed.at[behind, rows, :],
                dst_ref=landed.at[behind, rows, :],
                send_sem=sum_send_sems.at[0],
                recv_sem=sum_sems.at[behind, part],
                device_id={"exp": own},
                device_id_type=MESH,
            ).wait_recv()
        value = value + landed[behind].astype(f32)
    value = value.astype(out_ref.dtype)
    out_ref[...] = value
    value = value.astype(f32)
    value = value * value
    ones = jnp.ones((16, width), jnp.bfloat16)
    found = jnp.zeros((16, value.shape[0]), f32)
    for _ in range(3):
        term = value.astype(jnp.bfloat16)
        value = value - term.astype(f32)
        found = found + lax.dot_general(
            ones, term, (((1,), (1,)), ((), ())), preferred_element_type=f32
        )
    squares_ref[...] = found[0:8]

    @pl.when(me < count - 1)
    def _():
        rim_copy(me + 1).wait_send()

    for half in (0, 1):
        for k in range(1, SIDE):

            @pl.when(x + k < SIDE)
            def _():
                for one in end_copies(1, half, k, x, (x + k) * SIDE + y):
                    one.wait_send()

    clear(single(0, 0), 1, 0)
    clear(beside, 4, 1)
    clear(across_ring, 2, 5)
    clear(corner, 4, 7)
    clear(knight, 4, 11)
    clear(single(2, 2), 1, 15)
    for one in in_flight + leaving:
        one.wait_send()


def mixer(
    mixer_in, gate_in, delta_in, b_proj, c_proj, conv_kernel, conv_bias, delta_bias, decay_log,
    skip_gain, prefix_state, prefix_tail, out_proj, residual,
):
    tokens, channels = mixer_in.shape
    rows, width = residual.shape
    count = SIDE * SIDE
    here = pl.BlockSpec(memory_space=pltpu.VMEM)
    away = pl.BlockSpec(memory_space=pl.ANY)
    bf16, f32 = jnp.bfloat16, jnp.float32
    return pl.pallas_call(
        mixer_kernel,
        out_shape=(
            jax.ShapeDtypeStruct((rows, width), bf16),
            jax.ShapeDtypeStruct((8, rows), f32),
        ),
        in_specs=[here] * 12 + [away, here],
        out_specs=(here, here),
        scratch_shapes=[
            pltpu.VMEM((16, channels), bf16),
            pltpu.VMEM((8 + tokens, STRIP), f32),
            pltpu.VMEM((tokens, channels), f32),
            pltpu.VMEM((tokens, channels), f32),
            pltpu.VMEM((tokens, channels), f32),
            pltpu.VMEM((tokens, STRIP), f32),
            pltpu.VMEM((tokens, STATES, LANES), f32),
            pltpu.VMEM((tokens, STATES, LANES), f32),
            pltpu.VMEM((2, STATES, channels), bf16),
            pltpu.VMEM((2, 1, channels), f32),
            pltpu.VMEM((2, SIDE, STATES, channels), bf16),
            pltpu.VMEM((2, SIDE, 1, channels), f32),
            pltpu.VMEM((2, count * tokens, channels // 2), bf16),
            pltpu.VMEM((channels, width), bf16),
            pltpu.VMEM((count, tokens, width), bf16),
            pltpu.VMEM((count, tokens, width), bf16),
            pltpu.VMEM((SIDE - 1, rows, width), bf16),
            pltpu.VMEM((rows, width), f32),
            pltpu.SemaphoreType.DMA((2,)),
            pltpu.SemaphoreType.DMA((2, 2, 2, SIDE - 1, 2)),
            pltpu.SemaphoreType.DMA((2, 2, 5, 4)),
            pltpu.SemaphoreType.DMA((2, count)),
            pltpu.SemaphoreType.DMA((count,)),
            pltpu.SemaphoreType.DMA((SIDE - 1, 2)),
            pltpu.SemaphoreType.DMA,
        ],
        compiler_params=pltpu.CompilerParams(
            collective_id=1, has_side_effects=True, vmem_limit_bytes=56 * 1024 * 1024
        ),
        name="mixer",
    )(
        mixer_in, gate_in, delta_in, b_proj, c_proj, conv_kernel, conv_bias[None], delta_bias[None],
        decay_log, skip_gain[None], prefix_state, prefix_tail, out_proj, residual,
    )


def expert_kernel(
    capacity, features,
    mixer_ref, squares_ref, ids_ref, route_ref, gain_ref, gate_ref, up_ref, down_ref,
    out_ref,
    blocks, landed, wide, down, total, hidden, outgoing, answer, returned, all_squares, pick_all, routing,
    square_sems, dispatch_sems, return_sems, gather_sems, sum_sems, weight_sems,
):
    torus = Torus()
    me, index = torus.me, torus.index
    own_expert = lax.axis_index("exp")
    slots, width = answer.shape
    units = down.shape[0]
    count = SIDE * SIDE

    weights = [
        pltpu.make_async_copy(gate_ref.at[0], wide.at[:, pl.ds(0, units)], weight_sems.at[0]),
        pltpu.make_async_copy(up_ref.at[0], wide.at[:, pl.ds(units, units)], weight_sems.at[1]),
        pltpu.make_async_copy(down_ref.at[0], down, weight_sems.at[2]),
    ]
    for one in weights:
        one.start()

    barrier = pltpu.get_barrier_semaphore()
    for k in range(1, count):
        pl.semaphore_signal(
            barrier, inc=1, device_id={"ctx": lax.rem(me + k, count)}, device_id_type=MESH
        )
    for k in range(1, EXPERTS):
        pl.semaphore_signal(
            barrier, inc=1, device_id={"exp": lax.rem(own_expert + k, EXPERTS)}, device_id_type=MESH
        )

    tokens = mixer_ref.shape[0]
    z, core = own_expert // 2, own_expert % 2

    def at_peer(number, way):
        dz, dc = PEERS[number]
        other = core + dc - 2 * core * dc
        return lax.rem(z + way * dz + 2 * SIDE, SIDE) * 2 + other

    experts_wide = lax.broadcasted_iota(jnp.int32, (16, tokens), 0)
    named, gates_wide = jnp.zeros((16, tokens), jnp.float32), jnp.zeros((16, tokens), jnp.float32)
    for k in range(ids_ref.shape[0]):
        here = ids_ref[k : k + 1, :] == experts_wide
        named = jnp.where(here, 1.0, named)
        gates_wide = jnp.where(here, route_ref[k : k + 1, :], gates_wide)
    before = lax.broadcasted_iota(jnp.int32, (tokens, tokens), 0)
    after = lax.broadcasted_iota(jnp.int32, (tokens, tokens), 1)
    routing[0] = named[0:EXPERTS]
    routing[1] = jnp.dot(
        named.astype(jnp.bfloat16),
        (before < after).astype(jnp.float32).astype(jnp.bfloat16),
        preferred_element_type=jnp.float32,
    )[0:EXPERTS]
    first = lax.broadcasted_iota(jnp.int32, (16, LANES), 0)
    second = lax.broadcasted_iota(jnp.int32, (16, LANES), 1)
    turn = (first == second).astype(jnp.float32).astype(jnp.bfloat16)
    gates = jnp.zeros((tokens, LANES), jnp.float32)
    for _ in range(3):
        term = gates_wide.astype(jnp.bfloat16)
        gates_wide = gates_wide - term.astype(jnp.float32)
        gates = gates + lax.dot_general(
            term, turn, (((0,), (0,)), ((), ())), preferred_element_type=jnp.float32
        )

    for number in range(len(PEERS)):
        expert = pl.ds(at_peer(number, 1), 1)
        slot = lax.broadcasted_iota(jnp.int32, (capacity, tokens), 0).astype(jnp.float32)
        chosen = (routing[1, expert, :] == slot) & (routing[0, expert, :] > 0.5)
        pick_all[number * capacity : (number + 1) * capacity, :] = chosen.astype(
            jnp.float32
        ).astype(jnp.bfloat16)
    pl.semaphore_wait(barrier, count - 1 + EXPERTS - 1)

    square_copies = []
    for k in range(1, count):
        square_copies.append(
            pltpu.make_async_remote_copy(
                src_ref=squares_ref,
                dst_ref=all_squares.at[me],
                send_sem=square_sems.at[0, k - 1],
                recv_sem=square_sems.at[1, k - 1],
                device_id={"ctx": lax.rem(me + k, count)},
                device_id_type=MESH,
            )
        )
        square_copies[-1].start()
    all_squares[me] = squares_ref[...]
    for k in range(1, count):
        source = lax.rem(me + count - k, count)
        pltpu.make_async_remote_copy(
            src_ref=squares_ref,
            dst_ref=all_squares.at[source],
            send_sem=square_sems.at[0, k - 1],
            recv_sem=square_sems.at[1, k - 1],
            device_id={"ctx": me},
            device_id_type=MESH,
        ).wait_recv()
    scale = lax.rsqrt(jnp.sum(all_squares[...], axis=0)[0:1] / features + 1e-05)

    def pick(chunk, carry):
        rows = pl.ds(pl.multiple_of(chunk * capacity, 16), capacity)
        chosen = pick_all[rows, :]
        picked = jnp.dot(chosen, mixer_ref[...], preferred_element_type=jnp.float32)
        chosen = chosen.astype(jnp.float32)
        row_scale = jnp.sum(chosen * scale, axis=1, keepdims=True)
        outgoing[rows, :] = (picked * row_scale * gain_ref[...]).astype(outgoing.dtype)
        return carry

    lax.fori_loop(0, EXPERTS, pick, 0)

    def rows_of(number):
        return pl.ds(number * capacity, capacity)

    def dispatch(number, target):
        return pltpu.make_async_remote_copy(
            src_ref=outgoing.at[rows_of(number), :],
            dst_ref=blocks.at[me, rows_of(number), :],
            send_sem=dispatch_sems.at[0, number],
            recv_sem=dispatch_sems.at[1, number],
            device_id={"exp": target},
            device_id_type=MESH,
        )

    crossing = [dispatch(n, at_peer(n, 1)) for n in (5, 6, 7, 0, 1, 2, 3)]
    for one in crossing:
        one.start()
    blocks[me, rows_of(OWN), :] = outgoing[rows_of(OWN), :]

    in_flight = {}

    def moved(unit, line, kind, first, second, part, target):
        half = unit % 2
        start, size = span(slots, unit, part)
        ref = blocks.at[index(half, first, second), pl.ds(start, size), :]
        return pltpu.make_async_remote_copy(
            src_ref=ref,
            dst_ref=ref,
            send_sem=gather_sems.at[0, unit, line, kind],
            recv_sem=gather_sems.at[1, unit, line, kind],
            device_id={"ctx": target},
            device_id_type=MESH,
        )

    def send(unit, line, kind, first, second, part, towards):
        one = moved(unit, line, kind, first, second, part, index(unit % 2, *towards))
        one.start()
        where = (first, second) if unit % 2 == 0 else (second, first)
        in_flight.setdefault((unit // 2,) + where, []).append(one)

    def arrived(unit, line, kind, first, second, part):
        moved(unit, line, kind, first, second, part, me).wait_recv()

    def send_line(unit, first):
        send(unit, LINES[first], 0, first, 0, None, (0, 1))
        send(unit, LINES[first], 1, first, 0, None, (0, -1))

    def pass_on(unit, first):
        arrived(unit, LINES[first], 0, first, -1, None)
        send(unit, LINES[first], 2, first, -1, 0, (0, 1))
        arrived(unit, LINES[first], 1, first, 1, None)
        send(unit, LINES[first], 3, first, 1, 1, (0, -1))

    def last_of(unit, first):
        arrived(unit, LINES[first], 2, first, 2, 0)
        arrived(unit, LINES[first], 3, first, 2, 1)

    def open_unit(unit):
        for number in (2 * unit, 2 * unit + 1):
            if number != OWN:
                dispatch(number, own_expert).wait_recv()
        send(unit, RING, 0, 0, 0, None, (1, 0))
        send(unit, RING, 1, 0, 0, None, (-1, 0))
        send_line(unit, 0)

    def ring_one(unit):
        arrived(unit, RING, 0, -1, 0, None)
        send(unit, RING, 2, -1, 0, 0, (1, 0))
        arrived(unit, RING, 1, 1, 0, None)
        send(unit, RING, 3, 1, 0, 1, (-1, 0))
        send_line(unit, -1)
        send_line(unit, 1)
        pass_on(unit, 0)

    def ring_two(unit):
        arrived(unit, RING, 2, 2, 0, 0)
        arrived(unit, RING, 3, 2, 0, 1)
        send_line(unit, 2)
        last_of(unit, 0)

    def lines_one(unit):
        pass_on(unit, -1)
        pass_on(unit, 1)

    def lines_two(unit):
        pass_on(unit, 2)
        last_of(unit, -1)
        last_of(unit, 1)

    row_tile = slots // 2

    def over_blocks(group, where, number, body):
        rows = pl.ds(group * row_tile, row_tile)

        def one(block, carry):
            body(index(0, *where(block)), rows)
            return carry

        lax.fori_loop(0, number, one, 0)

    def grow(owner, rows):
        part = wide[pl.ds(pl.multiple_of(owner * width, 16), width), :]
        total[rows, :] += jnp.dot(blocks[owner, rows, :], part, preferred_element_type=jnp.float32)

    open_unit(2)
    open_unit(3)
    total[...] = jnp.zeros_like(total)
    open_unit(0)
    ring_one(2)
    ring_one(3)
    open_unit(1)
    for one in weights:
        one.wait()
    over_blocks(1, single(0, 0), 1, grow)
    over_blocks(1, beside, 4, grow)
    for unit in (2, 3):
        ring_two(unit)
    ring_one(0)
    ring_one(1)
    over_blocks(0, single(0, 0), 1, grow)
    over_blocks(1, across_ring, 2, grow)
    for unit in (2, 3):
        lines_one(unit)
    over_blocks(0, beside, 4, grow)
    for unit in (0, 1):
        ring_two(unit)
    for unit in (2, 3):
        lines_two(unit)
    over_blocks(1, corner, 4, grow)
    over_blocks(0, across_ring, 2, grow)
    for unit in (0, 1):
        lines_one(unit)
    over_blocks(1, knight, 4, grow)
    for unit in (2, 3):
        last_of(unit, 2)
    over_blocks(1, single(2, 2), 1, grow)
    over_blocks(0, corner, 4, grow)
    for unit in (0, 1):
        lines_two(unit)
    over_blocks(0, knight, 4, grow)
    for unit in (0, 1):
        last_of(unit, 2)
    over_blocks(0, single(2, 2), 1, grow)

    def activate(group):
        def one(step, carry):
            rows = pl.ds(pl.multiple_of(group * row_tile + step * capacity, 16), capacity)
            gate = total[rows, 0:units]
            hidden[rows, :] = (
                gate / (1.0 + jnp.exp(-gate)) * total[rows, units : 2 * units]
            ).astype(hidden.dtype)
            return carry

        lax.fori_loop(0, row_tile // capacity, one, 0)

    def project(owner, rows):
        part = down[:, pl.ds(pl.multiple_of(owner * width, LANES), width)]
        blocks[owner, rows, :] = jnp.dot(
            hidden[rows, :], part, preferred_element_type=jnp.float32
        ).astype(blocks.dtype)

    def fill(group, where, number):
        for block in range(number):
            for one in in_flight.pop((group,) + where(block), ()):
                one.wait_send()
        over_blocks(group, where, number, project)

    summing = []

    def part_rows(unit, part):
        start, size = span(slots, unit, part)
        return pl.ds(start, size)

    def landing(unit, line, kind):
        if kind < 2:
            return landed.at[unit, line, kind]
        size = span(slots, unit, 0)[1]
        return landed.at[unit, line, 2, pl.ds((kind - 2) * size, size), :]

    def sum_copy(unit, line, kind, first, second, part, target):
        return pltpu.make_async_remote_copy(
            src_ref=blocks.at[index(unit % 2, first, second), part_rows(unit, part), :],
            dst_ref=landing(unit, line, kind),
            send_sem=sum_sems.at[0, unit, line, kind],
            recv_sem=sum_sems.at[1, unit, line, kind],
            device_id={"ctx": target},
            device_id_type=MESH,
        )

    def give(unit, line, kind, first, second, part):
        step = 1 if kind % 2 == 0 else -1
        half = unit % 2
        target = index(half, step, 0) if line == RING else index(half, 0, step)
        one = sum_copy(unit, line, kind, first, second, part, target)
        one.start()
        summing.append(one)

    def taken(unit, line, kind):
        part = None if kind < 2 else kind - 2
        sum_copy(unit, line, kind, 0, 0, part, me).wait_recv()

    def add(unit, first, second, part, line, kinds):
        for kind in kinds:
            taken(unit, line, kind)
        owner = index(unit % 2, first, second)
        start, size = span(slots, unit, part)

        def one(step, carry):
            offset = pl.multiple_of(step * capacity, 16)
            rows = pl.ds(pl.multiple_of(start + offset, 16), capacity)
            value = blocks[owner, rows, :].astype(jnp.float32)
            for kind in kinds:
                value = value + landing(unit, line, kind)[pl.ds(offset, capacity), :].astype(
                    jnp.float32
                )
            blocks[owner, rows, :] = value.astype(blocks.dtype)
            return carry

        lax.fori_loop(0, size // capacity, one, 0)

    def at(line, offset):
        return (offset, 0) if line == RING else ({v: k for k, v in LINES.items()}[line], offset)

    def begin(unit, line):
        give(unit, line, 2, *at(line, 2), 0)
        give(unit, line, 3, *at(line, 2), 1)

    def middle(unit, line):
        add(unit, *at(line, 1), 0, line, (2,))
        give(unit, line, 0, *at(line, 1), None)
        add(unit, *at(line, -1), 1, line, (3,))
        give(unit, line, 1, *at(line, -1), None)

    def finish(unit, line):
        add(unit, *at(line, 0), None, line, (0, 1))

    def back(number, target):
        return pltpu.make_async_remote_copy(
            src_ref=answer.at[rows_of(number), :],
            dst_ref=returned.at[rows_of(number), :],
            send_sem=return_sems.at[0, number],
            recv_sem=return_sems.at[1, number],
            device_id={"exp": target},
            device_id_type=MESH,
        )

    def hand_back(unit):
        for kind in (0, 1):
            taken(unit, RING, kind)
        owner = index(0, 0, 0)
        for step in (0, 1):
            number = 2 * unit + step
            rows = rows_of(number)
            there = pl.ds(step * capacity, capacity)
            value = blocks[owner, rows, :].astype(jnp.float32)
            for kind in (0, 1):
                value = value + landed[unit, RING, kind, there, :].astype(jnp.float32)
            if number == OWN:
                returned[rows, :] = value.astype(returned.dtype)
            else:
                answer[rows, :] = value.astype(answer.dtype)
                one = back(number, at_peer(number, -1))
                one.start()
                summing.append(one)

    def start_lines(group):
        units = (2 * group, 2 * group + 1)
        fill(group, single(2, 2), 1)
        for unit in units:
            begin(unit, LINES[2])
        fill(group, knight, 4)
        for first in (1, -1):
            for unit in units:
                begin(unit, LINES[first])
        fill(group, across_ring, 2)
        for unit in units:
            begin(unit, LINES[0])

    def middle_lines(group):
        units = (2 * group, 2 * group + 1)
        for unit in units:
            middle(unit, LINES[2])
        fill(group, corner, 4)
        for first in (1, -1):
            for unit in units:
                middle(unit, LINES[first])
        fill(group, beside, 4)
        for unit in units:
            middle(unit, LINES[0])

    def finish_lines(group):
        units = (2 * group, 2 * group + 1)
        fill(group, single(0, 0), 1)
        for unit in units:
            finish(unit, LINES[2])
            begin(unit, RING)
        for first in (1, -1):
            for unit in units:
                finish(unit, LINES[first])
        for unit in units:
            middle(unit, RING)
        for unit in units:
            finish(unit, LINES[0])

    activate(0)
    start_lines(0)
    activate(1)
    middle_lines(0)
    for one in crossing:
        one.wait_send()
    start_lines(1)
    finish_lines(0)
    middle_lines(1)
    for unit in (1, 0):
        hand_back(unit)
    finish_lines(1)
    for unit in (3, 2):
        hand_back(unit)

    lane = lax.broadcasted_iota(jnp.int32, (tokens, LANES), 1)

    def mixed(number):
        rows = rows_of(number)
        gate = jnp.sum(jnp.where(lane == at_peer(number, 1), gates, 0.0), axis=1, keepdims=True)
        return gate * lax.dot_general(
            pick_all[rows, :],
            returned[rows, :],
            (((0,), (0,)), ((), ())),
            preferred_element_type=jnp.float32,
        )

    value = mixer_ref[...].astype(jnp.float32) + mixed(OWN)
    for number in (2, 3, 0, 1, 5, 6, 7):
        back(number, own_expert).wait_recv()
        value = value + mixed(number)
    out_ref[...] = value.astype(out_ref.dtype)
    for one in summing + square_copies:
        one.wait_send()


def expert_layer(
    mixer_out, squares, ids, route_gates, gain, expert_gate, expert_up, expert_down, capacity
):
    rows, width = mixer_out.shape
    features, units = expert_gate.shape[1:]
    slots = EXPERTS * capacity
    count = SIDE * SIDE
    here = pl.BlockSpec(memory_space=pltpu.VMEM)
    away = pl.BlockSpec(memory_space=pl.ANY)
    bf16, f32 = jnp.bfloat16, jnp.float32
    return pl.pallas_call(
        functools.partial(expert_kernel, capacity, features),
        out_shape=jax.ShapeDtypeStruct((rows, width), bf16),
        in_specs=[here] * 5 + [away] * 3,
        out_specs=here,
        scratch_shapes=[
            pltpu.VMEM((count, slots, width), bf16),
            pltpu.VMEM((len(UNITS), 5, 3, slots // len(UNITS), width), bf16),
            pltpu.VMEM((features, 2 * units), bf16),
            pltpu.VMEM((units, features), bf16),
            pltpu.VMEM((slots, 2 * units), f32),
            pltpu.VMEM((slots, units), bf16),
            pltpu.VMEM((slots, width), bf16),
            pltpu.VMEM((slots, width), bf16),
            pltpu.VMEM((slots, width), bf16),
            pltpu.VMEM((count,) + squares.shape, f32),
            pltpu.VMEM((slots, rows), bf16),
            pltpu.VMEM((2, EXPERTS, rows), f32),
            pltpu.SemaphoreType.DMA((2, count - 1)),
            pltpu.SemaphoreType.DMA((2, EXPERTS)),
            pltpu.SemaphoreType.DMA((2, EXPERTS)),
            pltpu.SemaphoreType.DMA((2, len(UNITS), 5, 4)),
            pltpu.SemaphoreType.DMA((2, len(UNITS), 5, 4)),
            pltpu.SemaphoreType.DMA((3,)),
        ],
        compiler_params=pltpu.CompilerParams(
            collective_id=3, has_side_effects=True, vmem_limit_bytes=56 * 1024 * 1024
        ),
        name="expert_layer",
    )(mixer_out, squares, ids, route_gates, gain, expert_gate, expert_up, expert_down)


def shards(
    mixer_in,
    gate_in,
    delta_in,
    b_proj,
    c_proj,
    conv_kernel,
    conv_bias,
    delta_bias,
    decay_log,
    skip_gain,
    prefix_state,
    prefix_tail,
    out_proj,
    residual,
    norm_gain,
    expert_gate,
    expert_up,
    expert_down,
    expert_ids,
    route_gates,
):
    mixer_out, squares = mixer(
        mixer_in, gate_in, delta_in, b_proj, c_proj, conv_kernel, conv_bias, delta_bias, decay_log,
        skip_gain, prefix_state, prefix_tail, out_proj, residual,
    )
    block_rows = residual.shape[0]
    experts = expert_gate.shape[0] * lax.axis_size("exp")
    top_count = expert_ids.shape[1]
    capacity = 3 * block_rows * top_count // (2 * experts)
    block_out = expert_layer(
        mixer_out, squares, expert_ids.T, route_gates.T, norm_gain[None],
        expert_gate, expert_up, expert_down, capacity,
    )
    return (mixer_out, block_out)


def solution(mesh):
    placed = (
        P("ctx", "exp"),
        P("ctx", "exp"),
        P("ctx", "exp"),
        P(None, "ctx"),
        P(None, "ctx"),
        P(None, "exp"),
        P("exp"),
        P("exp"),
        P(None, "exp"),
        P("exp"),
        P(None, "exp"),
        P(None, "exp"),
        P("exp", "ctx"),
        P("exp", "ctx"),
        P("ctx"),
        P("exp", None, "ctx"),
        P("exp", None, "ctx"),
        P("exp", "ctx", None),
        P("exp", None),
        P("exp", None),
    )
    return jax.shard_map(
        shards,
        mesh=mesh,
        in_specs=placed,
        out_specs=(P("exp", "ctx"), P("exp", "ctx")),
        check_vma=False,
    )
```

```python
import functools
import math

import jax
import jax.numpy as jnp
from jax import lax
from jax.experimental import pallas as pl
from jax.experimental.pallas import tpu as pltpu
from jax.sharding import PartitionSpec as P

SIDE = 4
STATES = 16
LANES = 128
STRIP = 512
LOG2E = math.log2(math.e)
MESH = pl.DeviceIdType.MESH


EXPERTS = 8
LINES = {0: 0, -1: 1, 1: 2, 2: 3}
RING = 4


class Torus:
    def __init__(self):
        me = lax.axis_index("ctx")
        self.me = me
        self.place = (me // SIDE, me % SIDE)

    def index(self, half, first, second):
        a = lax.rem(self.place[half] + first + 2 * SIDE, SIDE)
        b = lax.rem(self.place[1 - half] + second + 2 * SIDE, SIDE)
        return a * SIDE + b if half == 0 else b * SIDE + a


PEERS = ((0, 0), (0, 1), (2, 0), (2, 1), (1, 0), (1, 1), (-1, 0), (-1, 1))
OWN = 0
UNITS = (0, 1, 2, 3)


def span(rows, unit, part=None):
    size = rows // len(UNITS)
    return (unit * size, size) if part is None else (unit * size + part * (size // 2), size // 2)


SLOTS = (
    (0, 0),
    (1, 0), (-1, 0), (0, 1), (0, -1),
    (2, 0), (0, 2),
    (1, 1), (-1, 1), (1, -1), (-1, -1),
    (1, 2), (-1, 2), (2, 1), (2, -1),
    (2, 2),
)


def lane_parts(value):
    return tuple(value[:, k * LANES : (k + 1) * LANES] for k in range(value.shape[1] // LANES))


def sign(i):
    return 1 - 2 * (i % 2)


def beside(i):
    return sign(i) * (1 - i // 2), sign(i) * (i // 2)


def across_ring(i):
    return 2 * (1 - i), 2 * i


def corner(i):
    return sign(i), 1 - 2 * (i // 2)


def knight(i):
    along = i // 2
    return sign(i) * (1 - along) + 2 * along, 2 * (1 - along) + sign(i) * along


def single(dx, dy):
    return lambda i: (dx, dy)


def mixer_kernel(
    mixer_ref, gate_ref, delta_ref, b_ref, c_ref, taps_ref, bias_ref, delta_bias_ref, decay_ref,
    gain_ref, prefix_ref, tail_ref, weight_ref, residual_ref,
    out_ref, squares_ref,
    rim, padded, act, step, drive, summed, b_wide, c_wide, ends, spans, line_ends, line_spans,
    rows_all, weight, parts, got, landed, home,
    rim_sems, end_sems, gather_sems, pair_sems, sum_send_sems, sum_sems, weight_sem,
):
    torus = Torus()
    me, index = torus.me, torus.index
    x, y = torus.place
    own = lax.axis_index("exp")
    z, core = own // 2, own % 2
    count = SIDE * SIDE
    tokens, channels = mixer_ref.shape
    strips = channels // STRIP
    f32 = jnp.float32

    def strip_lanes(strip):
        return pl.ds(pl.multiple_of(strip * STRIP, STRIP), STRIP)

    load = pltpu.make_async_copy(weight_ref, weight, weight_sem)
    load.start()
    barrier = pltpu.get_barrier_semaphore()
    for k in range(1, count):
        pl.semaphore_signal(
            barrier, inc=1, device_id={"ctx": lax.rem(me + k, count)}, device_id_type=MESH
        )
    for k in range(1, EXPERTS):
        pl.semaphore_signal(
            barrier, inc=1, device_id={"exp": lax.rem(own + k, EXPERTS)}, device_id_type=MESH
        )
    for t in range(tokens):
        b_wide[t] = jnp.broadcast_to(b_ref[:, t : t + 1], (STATES, LANES))
        c_wide[t] = jnp.broadcast_to(c_ref[:, t : t + 1], (STATES, LANES))

    pl.semaphore_wait(barrier, count - 1 + EXPERTS - 1)

    def rim_copy(target):
        return pltpu.make_async_remote_copy(
            src_ref=mixer_ref.at[pl.ds(tokens - 16, 16), :],
            dst_ref=rim,
            send_sem=rim_sems.at[0],
            recv_sem=rim_sems.at[1],
            device_id={"ctx": target},
            device_id_type=MESH,
        )

    @pl.when(me < count - 1)
    def _():
        rim_copy(me + 1).start()

    def find_step(strip, carry):
        lanes = strip_lanes(strip)
        value = jnp.log(1.0 + jnp.exp(delta_ref[:, lanes].astype(f32) + delta_bias_ref[:, lanes]))
        step[:, lanes] = value
        spans[0, :, lanes] = jnp.sum(value, axis=0, keepdims=True)
        return carry

    lax.fori_loop(0, strips, find_step, 0)

    @pl.when(me > 0)
    def _():
        rim_copy(me).wait_recv()

    @pl.when(me == 0)
    def _():
        rim[...] = jnp.zeros_like(rim)

    def rates(lanes):
        return -jnp.exp(decay_ref[:, lanes]) * LOG2E

    def advance(rate, state, steps, drives, i, b_column):
        return tuple(
            jnp.exp2(r * s) * h + b_column * d
            for r, s, h, d in zip(
                rate, lane_parts(steps[i : i + 1]), state, lane_parts(drives[i : i + 1])
            )
        )

    def prepare(strip, carry):
        lanes = strip_lanes(strip)
        padded[0:8] = rim[:, lanes].astype(f32)[8:16]
        padded[8 : 8 + tokens] = mixer_ref[:, lanes].astype(f32)

        @pl.when(me == 0)
        def _():
            padded[5:8] = tail_ref[:, lanes].astype(f32)

        convolved = bias_ref[:, lanes]
        for k in range(4):
            convolved = convolved + taps_ref[k : k + 1, lanes] * padded[5 + k : 5 + k + tokens]
        value = convolved / (1.0 + jnp.exp(-convolved))
        act[:, lanes] = value
        drive[:, lanes] = value * step[:, lanes]
        rate = lane_parts(rates(lanes))

        def group(number, state):
            base = pl.multiple_of(number * 8, 8)
            steps, drives = step[pl.ds(base, 8), lanes], drive[pl.ds(base, 8), lanes]
            for i in range(8):
                state = advance(rate, state, steps, drives, i, b_wide[base + i])
            return state

        zero = jnp.zeros((STATES, LANES), f32)
        state = lax.fori_loop(0, tokens // 8, group, (zero,) * (STRIP // LANES))
        ends[0, :, lanes] = jnp.concatenate(state, axis=1).astype(ends.dtype)
        return carry

    half_channels = channels // 2
    per_half = strips // 2

    def end_copies(stage, half, k, place, target):
        lanes = pl.ds(half * half_channels, half_channels)
        pairs = ((ends, line_ends), (spans, line_spans))
        return [
            pltpu.make_async_remote_copy(
                src_ref=mine.at[stage, :, lanes],
                dst_ref=whole.at[stage, place, :, lanes],
                send_sem=end_sems.at[0, stage, half, k - 1, part],
                recv_sem=end_sems.at[1, stage, half, k - 1, part],
                device_id={"ctx": target},
                device_id_type=MESH,
            )
            for part, (mine, whole) in enumerate(pairs)
        ]

    def follow(stage, strip):
        lanes = strip_lanes(strip)

        def one(source, state):
            return (
                jnp.exp2(rates(lanes) * line_spans[stage, source, :, lanes]) * state
                + line_ends[stage, source, :, lanes].astype(f32)
            )

        return one

    def line_end(half, number, carry):
        strip = half * per_half + number
        lanes = strip_lanes(strip)
        state = lax.fori_loop(0, SIDE, follow(0, strip), jnp.zeros((STATES, STRIP), f32))
        ends[1, :, lanes] = state.astype(ends.dtype)
        spans[1, :, lanes] = sum(line_spans[0, source, :, lanes] for source in range(SIDE))
        return carry

    leaving = []
    for half in (0, 1):
        lax.fori_loop(half * per_half, (half + 1) * per_half, prepare, 0)
        lanes = pl.ds(half * half_channels, half_channels)
        for k in range(1, SIDE):
            leaving += end_copies(0, half, k, y, index(0, 0, k))
            for one in leaving[-2:]:
                one.start()
        line_ends[0, y, :, lanes] = ends[0, :, lanes]
        line_spans[0, y, :, lanes] = spans[0, :, lanes]
    for half in (0, 1):
        for k in range(1, SIDE):
            for one in end_copies(0, half, k, lax.rem(y + SIDE - k, SIDE), me):
                one.wait_recv()
        lax.fori_loop(0, per_half, functools.partial(line_end, half), 0)
        for k in range(1, SIDE):

            @pl.when(x + k < SIDE)
            def _():
                for one in end_copies(1, half, k, x, (x + k) * SIDE + y):
                    one.start()

    in_flight = []

    def moved(half, line, kind, first, second, part, towards, target):
        def rows(a, b):
            where = (a, b) if half == 0 else (b, a)
            where = tuple((v + 1) % SIDE - 1 for v in where)
            start, size = (0, tokens) if part is None else (part * (tokens // 2), tokens // 2)
            return rows_all.at[half, pl.ds(SLOTS.index(where) * tokens + start, size), :]

        return pltpu.make_async_remote_copy(
            src_ref=rows(first, second),
            dst_ref=rows(first - towards[0], second - towards[1]),
            send_sem=gather_sems.at[0, half, line, kind],
            recv_sem=gather_sems.at[1, half, line, kind],
            device_id={"ctx": target},
            device_id_type=MESH,
        )

    def send(half, line, kind, first, second, part, towards):
        one = moved(half, line, kind, first, second, part, towards, index(half, *towards))
        one.start()
        in_flight.append(one)

    def arrived(half, line, kind, first, second, part):
        moved(half, line, kind, first, second, part, (0, 0), me).wait_recv()

    def send_line(half, first):
        send(half, LINES[first], 0, first, 0, None, (0, 1))
        send(half, LINES[first], 1, first, 0, None, (0, -1))

    def pass_on(half, first):
        arrived(half, LINES[first], 0, first, -1, None)
        send(half, LINES[first], 2, first, -1, 0, (0, 1))
        arrived(half, LINES[first], 1, first, 1, None)
        send(half, LINES[first], 3, first, 1, 1, (0, -1))

    def last_of(half, first):
        arrived(half, LINES[first], 2, first, 2, 0)
        arrived(half, LINES[first], 3, first, 2, 1)

    def scan(half, strip, carry):
        lanes = strip_lanes(half * per_half + strip)
        rate = lane_parts(rates(lanes))
        state = prefix_ref[:, lanes]
        state = lax.fori_loop(0, x, follow(1, half * per_half + strip), state)
        state = lax.fori_loop(0, y, follow(0, half * per_half + strip), state)

        def group(number, state):
            base = pl.multiple_of(number * 8, 8)
            steps, drives = step[pl.ds(base, 8), lanes], drive[pl.ds(base, 8), lanes]
            found = []
            for i in range(8):
                state = advance(rate, state, steps, drives, i, b_wide[base + i])
                c_column = c_wide[base + i]
                found.append(
                    jnp.concatenate(
                        [jnp.sum(c_column * h, axis=0, keepdims=True) for h in state], axis=1
                    )
                )
            summed[pl.ds(base, 8), :] = jnp.concatenate(found, axis=0)
            return state

        lax.fori_loop(0, tokens // 8, group, lane_parts(state))
        gate = gate_ref[:, lanes].astype(f32)
        mixed = summed[...] + gain_ref[:, lanes] * act[:, lanes]
        rows_all[half, 0:tokens, strip_lanes(strip)] = (
            mixed * (gate / (1.0 + jnp.exp(-gate)))
        ).astype(rows_all.dtype)
        return carry

    for half in (0, 1):
        for k in range(1, SIDE):

            @pl.when(x >= k)
            def _():
                for one in end_copies(1, half, k, x - k, me):
                    one.wait_recv()

        lax.fori_loop(0, per_half, functools.partial(scan, half), 0)
        send(half, RING, 0, 0, 0, None, (1, 0))
        send(half, RING, 1, 0, 0, None, (-1, 0))
        send_line(half, 0)

    width = weight.shape[1]
    sibling = own + 1 - 2 * core

    def of_slot(where, number):
        dx, dy = where(number)
        line = lax.rem(y + dy + SIDE, SIDE)
        return lax.rem(x + dx + SIDE, SIDE), line // 2, line % 2

    def pair_copy(slot, target):
        return pltpu.make_async_remote_copy(
            src_ref=parts.at[slot],
            dst_ref=got.at[slot],
            send_sem=pair_sems.at[0, slot],
            recv_sem=pair_sems.at[1, slot],
            device_id={"exp": target},
            device_id_type=MESH,
        )

    def part_rows(part):
        return pl.ds(pl.multiple_of(part * tokens, tokens), tokens)

    def sum_copy(slot, column, part):
        behind = lax.rem(column - z + SIDE, SIDE) - 1
        return pltpu.make_async_remote_copy(
            src_ref=parts.at[slot],
            dst_ref=landed.at[behind, part_rows(part), :],
            send_sem=sum_send_sems.at[slot],
            recv_sem=sum_sems.at[behind, part],
            device_id={"exp": column * 2 + core},
            device_id_type=MESH,
        )

    def project(where, number, first_slot):
        together = min(number, 2)

        def one(pair, carry):
            first = first_slot + pair * together
            rows = pl.ds(pl.multiple_of(first * tokens, tokens), together * tokens)
            value = jnp.dot(
                rows_all[0, rows, :], weight[0:half_channels], preferred_element_type=f32
            ) + jnp.dot(
                rows_all[1, rows, :], weight[half_channels:], preferred_element_type=f32
            )
            for k in range(together):
                column, owner, part = of_slot(where, pair * together + k)
                parts[first + k] = value[k * tokens : (k + 1) * tokens].astype(parts.dtype)

                @pl.when(owner != core)
                def _():
                    pair_copy(first + k, sibling).start()

            return carry

        lax.fori_loop(0, number // together, one, 0)

    def settle(where, number, first_slot):
        def one(k, carry):
            slot = first_slot + k
            column, owner, part = of_slot(where, k)

            @pl.when(owner == core)
            def _():
                pair_copy(slot, own).wait_recv()
                value = parts[slot].astype(f32) + got[slot].astype(f32)

                @pl.when(column == z)
                def _():
                    home[part_rows(part), :] = value

                @pl.when(column != z)
                def _():
                    parts[slot] = value.astype(parts.dtype)
                    sum_copy(slot, column, part).start()

            return carry

        lax.fori_loop(0, number, one, 0)

    def clear(where, number, first_slot):
        def one(k, carry):
            slot = first_slot + k
            column, owner, part = of_slot(where, k)

            @pl.when(owner != core)
            def _():
                pair_copy(slot, sibling).wait_send()

            @pl.when((owner == core) & (column != z))
            def _():
                sum_copy(slot, column, part).wait_send()

            return carry

        lax.fori_loop(0, number, one, 0)

    load.wait()
    project(single(0, 0), 1, 0)
    for half in (0, 1):
        arrived(half, RING, 0, -1, 0, None)
        send(half, RING, 2, -1, 0, 0, (1, 0))
        arrived(half, RING, 1, 1, 0, None)
        send(half, RING, 3, 1, 0, 1, (-1, 0))
        send_line(half, -1)
        send_line(half, 1)
    for half in (0, 1):
        pass_on(half, 0)
    project(beside, 4, 1)
    settle(single(0, 0), 1, 0)
    for half in (0, 1):
        arrived(half, RING, 2, 2, 0, 0)
        arrived(half, RING, 3, 2, 0, 1)
        send_line(half, 2)
    for half in (0, 1):
        last_of(half, 0)
    project(across_ring, 2, 5)
    settle(beside, 4, 1)
    for first in (-1, 1):
        for half in (0, 1):
            pass_on(half, first)
    project(corner, 4, 7)
    settle(across_ring, 2, 5)
    for half in (0, 1):
        pass_on(half, 2)
    for first in (-1, 1):
        for half in (0, 1):
            last_of(half, first)
    project(knight, 4, 11)
    settle(corner, 4, 7)
    for half in (0, 1):
        last_of(half, 2)
    project(single(2, 2), 1, 15)
    settle(knight, 4, 11)

    settle(single(2, 2), 1, 15)
    value = home[...] + residual_ref[...].astype(f32)
    for behind in range(SIDE - 1):
        for part in (0, 1):
            rows = pl.ds(part * tokens, tokens)
            pltpu.make_async_remote_copy(
                src_ref=landed.at[behind, rows, :],
                dst_ref=landed.at[behind, rows, :],
                send_sem=sum_send_sems.at[0],
                recv_sem=sum_sems.at[behind, part],
                device_id={"exp": own},
                device_id_type=MESH,
            ).wait_recv()
        value = value + landed[behind].astype(f32)
    value = value.astype(out_ref.dtype)
    out_ref[...] = value
    value = value.astype(f32)
    value = value * value
    ones = jnp.ones((16, width), jnp.bfloat16)
    found = jnp.zeros((16, value.shape[0]), f32)
    for _ in range(3):
        term = value.astype(jnp.bfloat16)
        value = value - term.astype(f32)
        found = found + lax.dot_general(
            ones, term, (((1,), (1,)), ((), ())), preferred_element_type=f32
        )
    squares_ref[...] = found[0:8]

    @pl.when(me < count - 1)
    def _():
        rim_copy(me + 1).wait_send()

    for half in (0, 1):
        for k in range(1, SIDE):

            @pl.when(x + k < SIDE)
            def _():
                for one in end_copies(1, half, k, x, (x + k) * SIDE + y):
                    one.wait_send()

    clear(single(0, 0), 1, 0)
    clear(beside, 4, 1)
    clear(across_ring, 2, 5)
    clear(corner, 4, 7)
    clear(knight, 4, 11)
    clear(single(2, 2), 1, 15)
    for one in in_flight + leaving:
        one.wait_send()


def mixer(
    mixer_in, gate_in, delta_in, b_proj, c_proj, conv_kernel, conv_bias, delta_bias, decay_log,
    skip_gain, prefix_state, prefix_tail, out_proj, residual,
):
    tokens, channels = mixer_in.shape
    rows, width = residual.shape
    count = SIDE * SIDE
    here = pl.BlockSpec(memory_space=pltpu.VMEM)
    away = pl.BlockSpec(memory_space=pl.ANY)
    bf16, f32 = jnp.bfloat16, jnp.float32
    return pl.pallas_call(
        mixer_kernel,
        out_shape=(
            jax.ShapeDtypeStruct((rows, width), bf16),
            jax.ShapeDtypeStruct((8, rows), f32),
        ),
        in_specs=[here] * 12 + [away, here],
        out_specs=(here, here),
        scratch_shapes=[
            pltpu.VMEM((16, channels), bf16),
            pltpu.VMEM((8 + tokens, STRIP), f32),
            pltpu.VMEM((tokens, channels), f32),
            pltpu.VMEM((tokens, channels), f32),
            pltpu.VMEM((tokens, channels), f32),
            pltpu.VMEM((tokens, STRIP), f32),
            pltpu.VMEM((tokens, STATES, LANES), f32),
            pltpu.VMEM((tokens, STATES, LANES), f32),
            pltpu.VMEM((2, STATES, channels), bf16),
            pltpu.VMEM((2, 1, channels), f32),
            pltpu.VMEM((2, SIDE, STATES, channels), bf16),
            pltpu.VMEM((2, SIDE, 1, channels), f32),
            pltpu.VMEM((2, count * tokens, channels // 2), bf16),
            pltpu.VMEM((channels, width), bf16),
            pltpu.VMEM((count, tokens, width), bf16),
            pltpu.VMEM((count, tokens, width), bf16),
            pltpu.VMEM((SIDE - 1, rows, width), bf16),
            pltpu.VMEM((rows, width), f32),
            pltpu.SemaphoreType.DMA((2,)),
            pltpu.SemaphoreType.DMA((2, 2, 2, SIDE - 1, 2)),
            pltpu.SemaphoreType.DMA((2, 2, 5, 4)),
            pltpu.SemaphoreType.DMA((2, count)),
            pltpu.SemaphoreType.DMA((count,)),
            pltpu.SemaphoreType.DMA((SIDE - 1, 2)),
            pltpu.SemaphoreType.DMA,
        ],
        compiler_params=pltpu.CompilerParams(
            collective_id=1, has_side_effects=True, vmem_limit_bytes=56 * 1024 * 1024
        ),
        name="mixer",
    )(
        mixer_in, gate_in, delta_in, b_proj, c_proj, conv_kernel, conv_bias[None], delta_bias[None],
        decay_log, skip_gain[None], prefix_state, prefix_tail, out_proj, residual,
    )


def expert_kernel(
    capacity, features,
    mixer_ref, squares_ref, ids_ref, route_ref, gain_ref, gate_ref, up_ref, down_ref,
    out_ref,
    blocks, landed, wide, down, total, hidden, outgoing, answer, returned, all_squares, pick_all, routing, scales_out, scales,
    square_sems, scale_sems, dispatch_sems, return_sems, gather_sems, sum_sems, weight_sems,
):
    torus = Torus()
    me, index = torus.me, torus.index
    own_expert = lax.axis_index("exp")
    slots, width = answer.shape
    units = down.shape[0]
    count = SIDE * SIDE

    weights = [
        pltpu.make_async_copy(gate_ref.at[0], wide.at[:, pl.ds(0, units)], weight_sems.at[0]),
        pltpu.make_async_copy(up_ref.at[0], wide.at[:, pl.ds(units, units)], weight_sems.at[1]),
        pltpu.make_async_copy(down_ref.at[0], down, weight_sems.at[2]),
    ]
    for one in weights:
        one.start()

    barrier = pltpu.get_barrier_semaphore()
    for k in range(1, count):
        pl.semaphore_signal(
            barrier, inc=1, device_id={"ctx": lax.rem(me + k, count)}, device_id_type=MESH
        )
    for k in range(1, EXPERTS):
        pl.semaphore_signal(
            barrier, inc=1, device_id={"exp": lax.rem(own_expert + k, EXPERTS)}, device_id_type=MESH
        )

    tokens = mixer_ref.shape[0]
    z, core = own_expert // 2, own_expert % 2

    def at_peer(number, way):
        dz, dc = PEERS[number]
        other = core + dc - 2 * core * dc
        return lax.rem(z + way * dz + 2 * SIDE, SIDE) * 2 + other

    experts_wide = lax.broadcasted_iota(jnp.int32, (16, tokens), 0)
    named, gates_wide = jnp.zeros((16, tokens), jnp.float32), jnp.zeros((16, tokens), jnp.float32)
    for k in range(ids_ref.shape[0]):
        here = ids_ref[k : k + 1, :] == experts_wide
        named = jnp.where(here, 1.0, named)
        gates_wide = jnp.where(here, route_ref[k : k + 1, :], gates_wide)
    before = lax.broadcasted_iota(jnp.int32, (tokens, tokens), 0)
    after = lax.broadcasted_iota(jnp.int32, (tokens, tokens), 1)
    routing[0] = named[0:EXPERTS]
    routing[1] = jnp.dot(
        named.astype(jnp.bfloat16),
        (before < after).astype(jnp.float32).astype(jnp.bfloat16),
        preferred_element_type=jnp.float32,
    )[0:EXPERTS]
    first = lax.broadcasted_iota(jnp.int32, (16, LANES), 0)
    second = lax.broadcasted_iota(jnp.int32, (16, LANES), 1)
    turn = (first == second).astype(jnp.float32).astype(jnp.bfloat16)
    gates = jnp.zeros((tokens, LANES), jnp.float32)
    for _ in range(3):
        term = gates_wide.astype(jnp.bfloat16)
        gates_wide = gates_wide - term.astype(jnp.float32)
        gates = gates + lax.dot_general(
            term, turn, (((0,), (0,)), ((), ())), preferred_element_type=jnp.float32
        )

    for number in range(len(PEERS)):
        expert = pl.ds(at_peer(number, 1), 1)
        slot = lax.broadcasted_iota(jnp.int32, (capacity, tokens), 0).astype(jnp.float32)
        chosen = (routing[1, expert, :] == slot) & (routing[0, expert, :] > 0.5)
        rows = pl.ds(number * capacity, capacity)
        pick_all[rows, :] = chosen.astype(jnp.float32).astype(jnp.bfloat16)
        picked = jnp.dot(pick_all[rows, :], mixer_ref[...], preferred_element_type=jnp.float32)
        outgoing[rows, :] = (picked * gain_ref[...]).astype(outgoing.dtype)
    pl.semaphore_wait(barrier, count - 1 + EXPERTS - 1)

    square_copies = []
    for k in range(1, count):
        square_copies.append(
            pltpu.make_async_remote_copy(
                src_ref=squares_ref,
                dst_ref=all_squares.at[me],
                send_sem=square_sems.at[0, k - 1],
                recv_sem=square_sems.at[1, k - 1],
                device_id={"ctx": lax.rem(me + k, count)},
                device_id_type=MESH,
            )
        )
        square_copies[-1].start()

    def rows_of(number):
        return pl.ds(number * capacity, capacity)

    def dispatch(number, target):
        return pltpu.make_async_remote_copy(
            src_ref=outgoing.at[rows_of(number), :],
            dst_ref=blocks.at[me, rows_of(number), :],
            send_sem=dispatch_sems.at[0, number],
            recv_sem=dispatch_sems.at[1, number],
            device_id={"exp": target},
            device_id_type=MESH,
        )

    crossing = [dispatch(n, at_peer(n, 1)) for n in range(1, len(PEERS))]
    for one in crossing:
        one.start()
    blocks[me, rows_of(OWN), :] = outgoing[rows_of(OWN), :]

    def scale_copy(number, target):
        return pltpu.make_async_remote_copy(
            src_ref=scales_out.at[number],
            dst_ref=scales.at[number],
            send_sem=scale_sems.at[0, number],
            recv_sem=scale_sems.at[1, number],
            device_id={"exp": target},
            device_id_type=MESH,
        )

    def send_scales():
        all_squares[me] = squares_ref[...]
        for k in range(1, count):
            source = lax.rem(me + count - k, count)
            pltpu.make_async_remote_copy(
                src_ref=squares_ref,
                dst_ref=all_squares.at[source],
                send_sem=square_sems.at[0, k - 1],
                recv_sem=square_sems.at[1, k - 1],
                device_id={"ctx": me},
                device_id_type=MESH,
            ).wait_recv()
        scale = lax.rsqrt(jnp.sum(all_squares[...], axis=0)[0:1] / features + 1e-05)
        for number in range(len(PEERS)):
            chosen = pick_all[rows_of(number), :].astype(jnp.float32)
            row_scale = jnp.sum(chosen * scale, axis=1, keepdims=True)
            row_scale = jnp.broadcast_to(row_scale, (capacity, LANES))
            if number == OWN:
                scales[number] = row_scale
            else:
                scales_out[number] = row_scale
                one = scale_copy(number, at_peer(number, 1))
                one.start()
                crossing.append(one)

    in_flight = {}

    def moved(unit, line, kind, first, second, part, target):
        half = unit % 2
        start, size = span(slots, unit, part)
        ref = blocks.at[index(half, first, second), pl.ds(start, size), :]
        return pltpu.make_async_remote_copy(
            src_ref=ref,
            dst_ref=ref,
            send_sem=gather_sems.at[0, unit, line, kind],
            recv_sem=gather_sems.at[1, unit, line, kind],
            device_id={"ctx": target},
            device_id_type=MESH,
        )

    def send(unit, line, kind, first, second, part, towards):
        one = moved(unit, line, kind, first, second, part, index(unit % 2, *towards))
        one.start()
        where = (first, second) if unit % 2 == 0 else (second, first)
        in_flight.setdefault((unit // 2,) + where, []).append(one)

    def arrived(unit, line, kind, first, second, part):
        moved(unit, line, kind, first, second, part, me).wait_recv()

    def send_line(unit, first):
        send(unit, LINES[first], 0, first, 0, None, (0, 1))
        send(unit, LINES[first], 1, first, 0, None, (0, -1))

    def pass_on(unit, first):
        arrived(unit, LINES[first], 0, first, -1, None)
        send(unit, LINES[first], 2, first, -1, 0, (0, 1))
        arrived(unit, LINES[first], 1, first, 1, None)
        send(unit, LINES[first], 3, first, 1, 1, (0, -1))

    def last_of(unit, first):
        arrived(unit, LINES[first], 2, first, 2, 0)
        arrived(unit, LINES[first], 3, first, 2, 1)

    def open_unit(unit):
        for number in (2 * unit, 2 * unit + 1):
            if number != OWN:
                dispatch(number, own_expert).wait_recv()
        send(unit, RING, 0, 0, 0, None, (1, 0))
        send(unit, RING, 1, 0, 0, None, (-1, 0))
        send_line(unit, 0)

    def ring_one(unit):
        arrived(unit, RING, 0, -1, 0, None)
        send(unit, RING, 2, -1, 0, 0, (1, 0))
        arrived(unit, RING, 1, 1, 0, None)
        send(unit, RING, 3, 1, 0, 1, (-1, 0))
        send_line(unit, -1)
        send_line(unit, 1)
        pass_on(unit, 0)

    def ring_two(unit):
        arrived(unit, RING, 2, 2, 0, 0)
        arrived(unit, RING, 3, 2, 0, 1)
        send_line(unit, 2)
        last_of(unit, 0)

    def lines_one(unit):
        pass_on(unit, -1)
        pass_on(unit, 1)

    def lines_two(unit):
        pass_on(unit, 2)
        last_of(unit, -1)
        last_of(unit, 1)

    row_tile = slots // 2

    def over_blocks(group, where, number, body):
        rows = pl.ds(group * row_tile, row_tile)

        def one(block, carry):
            body(index(0, *where(block)), rows)
            return carry

        lax.fori_loop(0, number, one, 0)

    def grow(owner, rows):
        part = wide[pl.ds(pl.multiple_of(owner * width, 16), width), :]
        total[rows, :] += jnp.dot(blocks[owner, rows, :], part, preferred_element_type=jnp.float32)

    def activate(group):
        together = len(PEERS) // 2
        for number in range(group * together, (group + 1) * together):
            if number != OWN:
                scale_copy(number, own_expert).wait_recv()

        def one(step, carry):
            number = group * together + step
            rows = pl.ds(pl.multiple_of(number * capacity, 16), capacity)
            scale = jnp.concatenate([scales[number]] * (units // LANES), axis=1)
            gate = total[rows, 0:units] * scale
            up = total[rows, units : 2 * units] * scale
            hidden[rows, :] = (gate / (1.0 + jnp.exp(-gate)) * up).astype(hidden.dtype)
            return carry

        lax.fori_loop(0, together, one, 0)

    def project(owner, rows):
        part = down[:, pl.ds(pl.multiple_of(owner * width, LANES), width)]
        blocks[owner, rows, :] = jnp.dot(
            hidden[rows, :], part, preferred_element_type=jnp.float32
        ).astype(blocks.dtype)

    def fill(group, where, number):
        for block in range(number):
            for one in in_flight.pop((group,) + where(block), ()):
                one.wait_send()
        over_blocks(group, where, number, project)

    summing = []

    def part_rows(unit, part):
        start, size = span(slots, unit, part)
        return pl.ds(start, size)

    def landing(unit, line, kind):
        if kind < 2:
            return landed.at[unit, line, kind]
        size = span(slots, unit, 0)[1]
        return landed.at[unit, line, 2, pl.ds((kind - 2) * size, size), :]

    def sum_copy(unit, line, kind, first, second, part, target):
        return pltpu.make_async_remote_copy(
            src_ref=blocks.at[index(unit % 2, first, second), part_rows(unit, part), :],
            dst_ref=landing(unit, line, kind),
            send_sem=sum_sems.at[0, unit, line, kind],
            recv_sem=sum_sems.at[1, unit, line, kind],
            device_id={"ctx": target},
            device_id_type=MESH,
        )

    def give(unit, line, kind, first, second, part):
        step = 1 if kind % 2 == 0 else -1
        half = unit % 2
        target = index(half, step, 0) if line == RING else index(half, 0, step)
        one = sum_copy(unit, line, kind, first, second, part, target)
        one.start()
        summing.append(one)

    def taken(unit, line, kind):
        part = None if kind < 2 else kind - 2
        sum_copy(unit, line, kind, 0, 0, part, me).wait_recv()

    def add(unit, first, second, part, line, kinds):
        for kind in kinds:
            taken(unit, line, kind)
        owner = index(unit % 2, first, second)
        start, size = span(slots, unit, part)

        def one(step, carry):
            offset = pl.multiple_of(step * capacity, 16)
            rows = pl.ds(pl.multiple_of(start + offset, 16), capacity)
            value = blocks[owner, rows, :].astype(jnp.float32)
            for kind in kinds:
                value = value + landing(unit, line, kind)[pl.ds(offset, capacity), :].astype(
                    jnp.float32
                )
            blocks[owner, rows, :] = value.astype(blocks.dtype)
            return carry

        lax.fori_loop(0, size // capacity, one, 0)

    def at(line, offset):
        return (offset, 0) if line == RING else ({v: k for k, v in LINES.items()}[line], offset)

    def begin(unit, line):
        give(unit, line, 2, *at(line, 2), 0)
        give(unit, line, 3, *at(line, 2), 1)

    def middle(unit, line):
        add(unit, *at(line, 1), 0, line, (2,))
        give(unit, line, 0, *at(line, 1), None)
        add(unit, *at(line, -1), 1, line, (3,))
        give(unit, line, 1, *at(line, -1), None)

    def finish(unit, line):
        add(unit, *at(line, 0), None, line, (0, 1))

    def back(number, target):
        return pltpu.make_async_remote_copy(
            src_ref=answer.at[rows_of(number), :],
            dst_ref=returned.at[rows_of(number), :],
            send_sem=return_sems.at[0, number],
            recv_sem=return_sems.at[1, number],
            device_id={"exp": target},
            device_id_type=MESH,
        )

    def hand_back(unit):
        for kind in (0, 1):
            taken(unit, RING, kind)
        owner = index(0, 0, 0)
        for step in (0, 1):
            number = 2 * unit + step
            rows = rows_of(number)
            there = pl.ds(step * capacity, capacity)
            value = blocks[owner, rows, :].astype(jnp.float32)
            for kind in (0, 1):
                value = value + landed[unit, RING, kind, there, :].astype(jnp.float32)
            if number == OWN:
                returned[rows, :] = value.astype(returned.dtype)
            else:
                answer[rows, :] = value.astype(answer.dtype)
                one = back(number, at_peer(number, -1))
                one.start()
                summing.append(one)

    def both(group, step, *where):
        for unit in (2 * group, 2 * group + 1):
            step(unit, *where)

    def finish_lines(group):
        fill(group, single(0, 0), 1)
        for unit in (2 * group, 2 * group + 1):
            finish(unit, LINES[2])
            begin(unit, RING)
        for first in (1, -1):
            both(group, finish, LINES[first])
        both(group, middle, RING)
        both(group, finish, LINES[0])

    open_unit(0)
    send_scales()
    open_unit(1)
    ring_one(0)
    open_unit(2)
    open_unit(3)
    ring_one(1)
    total[...] = jnp.zeros_like(total)
    for one in weights:
        one.wait()
    over_blocks(0, single(0, 0), 1, grow)
    over_blocks(0, beside, 4, grow)
    both(0, ring_two)
    both(1, ring_one)
    both(0, lines_one)
    over_blocks(0, across_ring, 2, grow)
    over_blocks(1, single(0, 0), 1, grow)
    both(0, lines_two)
    both(1, ring_two)
    over_blocks(0, corner, 4, grow)
    over_blocks(1, beside, 4, grow)
    both(0, last_of, 2)
    both(1, lines_one)
    over_blocks(0, knight, 4, grow)
    over_blocks(0, single(2, 2), 1, grow)
    activate(0)
    fill(0, single(2, 2), 1)
    both(0, begin, LINES[2])
    both(1, lines_two)
    fill(0, knight, 4)
    both(0, begin, LINES[1])
    both(0, begin, LINES[-1])
    fill(0, across_ring, 2)
    both(0, begin, LINES[0])
    over_blocks(1, across_ring, 2, grow)
    over_blocks(1, corner, 4, grow)
    both(0, middle, LINES[2])
    both(1, last_of, 2)
    fill(0, corner, 4)
    both(0, middle, LINES[1])
    both(0, middle, LINES[-1])
    over_blocks(1, knight, 4, grow)
    over_blocks(1, single(2, 2), 1, grow)
    activate(1)
    fill(0, beside, 4)
    both(0, middle, LINES[0])
    for one in crossing:
        one.wait_send()
    fill(1, single(2, 2), 1)
    both(1, begin, LINES[2])
    fill(1, knight, 4)
    both(1, begin, LINES[1])
    both(1, begin, LINES[-1])
    fill(1, across_ring, 2)
    both(1, begin, LINES[0])
    finish_lines(0)
    both(1, middle, LINES[2])
    fill(1, corner, 4)
    both(1, middle, LINES[1])
    both(1, middle, LINES[-1])
    fill(1, beside, 4)
    both(1, middle, LINES[0])
    both(0, hand_back)
    finish_lines(1)
    both(1, hand_back)

    lane = lax.broadcasted_iota(jnp.int32, (tokens, LANES), 1)

    def mixed(number):
        rows = rows_of(number)
        gate = jnp.sum(jnp.where(lane == at_peer(number, 1), gates, 0.0), axis=1, keepdims=True)
        return gate * lax.dot_general(
            pick_all[rows, :],
            returned[rows, :],
            (((0,), (0,)), ((), ())),
            preferred_element_type=jnp.float32,
        )

    value = mixer_ref[...].astype(jnp.float32) + mixed(OWN)
    for number in range(1, len(PEERS)):
        back(number, own_expert).wait_recv()
        value = value + mixed(number)
    out_ref[...] = value.astype(out_ref.dtype)
    for one in summing + square_copies:
        one.wait_send()


def expert_layer(
    mixer_out, squares, ids, route_gates, gain, expert_gate, expert_up, expert_down, capacity
):
    rows, width = mixer_out.shape
    features, units = expert_gate.shape[1:]
    slots = EXPERTS * capacity
    count = SIDE * SIDE
    here = pl.BlockSpec(memory_space=pltpu.VMEM)
    away = pl.BlockSpec(memory_space=pl.ANY)
    bf16, f32 = jnp.bfloat16, jnp.float32
    return pl.pallas_call(
        functools.partial(expert_kernel, capacity, features),
        out_shape=jax.ShapeDtypeStruct((rows, width), bf16),
        in_specs=[here] * 5 + [away] * 3,
        out_specs=here,
        scratch_shapes=[
            pltpu.VMEM((count, slots, width), bf16),
            pltpu.VMEM((len(UNITS), 5, 3, slots // len(UNITS), width), bf16),
            pltpu.VMEM((features, 2 * units), bf16),
            pltpu.VMEM((units, features), bf16),
            pltpu.VMEM((slots, 2 * units), f32),
            pltpu.VMEM((slots, units), bf16),
            pltpu.VMEM((slots, width), bf16),
            pltpu.VMEM((slots, width), bf16),
            pltpu.VMEM((slots, width), bf16),
            pltpu.VMEM((count,) + squares.shape, f32),
            pltpu.VMEM((slots, rows), bf16),
            pltpu.VMEM((2, EXPERTS, rows), f32),
            pltpu.VMEM((EXPERTS, capacity, LANES), f32),
            pltpu.VMEM((EXPERTS, capacity, LANES), f32),
            pltpu.SemaphoreType.DMA((2, count - 1)),
            pltpu.SemaphoreType.DMA((2, EXPERTS)),
            pltpu.SemaphoreType.DMA((2, EXPERTS)),
            pltpu.SemaphoreType.DMA((2, EXPERTS)),
            pltpu.SemaphoreType.DMA((2, len(UNITS), 5, 4)),
            pltpu.SemaphoreType.DMA((2, len(UNITS), 5, 4)),
            pltpu.SemaphoreType.DMA((3,)),
        ],
        compiler_params=pltpu.CompilerParams(
            collective_id=3, has_side_effects=True, vmem_limit_bytes=56 * 1024 * 1024
        ),
        name="expert_layer",
    )(mixer_out, squares, ids, route_gates, gain, expert_gate, expert_up, expert_down)


def shards(
    mixer_in,
    gate_in,
    delta_in,
    b_proj,
    c_proj,
    conv_kernel,
    conv_bias,
    delta_bias,
    decay_log,
    skip_gain,
    prefix_state,
    prefix_tail,
    out_proj,
    residual,
    norm_gain,
    expert_gate,
    expert_up,
    expert_down,
    expert_ids,
    route_gates,
):
    mixer_out, squares = mixer(
        mixer_in, gate_in, delta_in, b_proj, c_proj, conv_kernel, conv_bias, delta_bias, decay_log,
        skip_gain, prefix_state, prefix_tail, out_proj, residual,
    )
    block_rows = residual.shape[0]
    experts = expert_gate.shape[0] * lax.axis_size("exp")
    top_count = expert_ids.shape[1]
    capacity = 3 * block_rows * top_count // (2 * experts)
    block_out = expert_layer(
        mixer_out, squares, expert_ids.T, route_gates.T, norm_gain[None],
        expert_gate, expert_up, expert_down, capacity,
    )
    return (mixer_out, block_out)


def solution(mesh):
    placed = (
        P("ctx", "exp"),
        P("ctx", "exp"),
        P("ctx", "exp"),
        P(None, "ctx"),
        P(None, "ctx"),
        P(None, "exp"),
        P("exp"),
        P("exp"),
        P(None, "exp"),
        P("exp"),
        P(None, "exp"),
        P(None, "exp"),
        P("exp", "ctx"),
        P("exp", "ctx"),
        P("ctx"),
        P("exp", None, "ctx"),
        P("exp", None, "ctx"),
        P("exp", "ctx", None),
        P("exp", None),
        P("exp", None),
    )
    return jax.shard_map(
        shards,
        mesh=mesh,
        in_specs=placed,
        out_specs=(P("exp", "ctx"), P("exp", "ctx")),
        check_vma=False,
    )
```

```python
import functools
import math

import jax
import jax.numpy as jnp
from jax import lax
from jax.experimental import pallas as pl
from jax.experimental.pallas import tpu as pltpu
from jax.sharding import PartitionSpec as P

SIDE = 4
STATES = 16
LANES = 128
STRIP = 512
LOG2E = math.log2(math.e)
MESH = pl.DeviceIdType.MESH


EXPERTS = 8
LINES = {0: 0, -1: 1, 1: 2, 2: 3}
RING = 4


class Torus:
    def __init__(self):
        me = lax.axis_index("ctx")
        self.me = me
        self.place = (me // SIDE, me % SIDE)

    def index(self, half, first, second):
        a = lax.rem(self.place[half] + first + 2 * SIDE, SIDE)
        b = lax.rem(self.place[1 - half] + second + 2 * SIDE, SIDE)
        return a * SIDE + b if half == 0 else b * SIDE + a


PEERS = ((0, 0), (0, 1), (2, 0), (2, 1), (1, 0), (1, 1), (-1, 0), (-1, 1))
OWN = 0
UNITS = (0, 1, 2, 3)


def span(rows, unit, part=None):
    size = rows // len(UNITS)
    return (unit * size, size) if part is None else (unit * size + part * (size // 2), size // 2)


SLOTS = (
    (0, 0),
    (1, 0), (-1, 0), (0, 1), (0, -1),
    (2, 0), (0, 2),
    (1, 1), (-1, 1), (1, -1), (-1, -1),
    (1, 2), (-1, 2), (2, 1), (2, -1),
    (2, 2),
)


def lane_parts(value):
    return tuple(value[:, k * LANES : (k + 1) * LANES] for k in range(value.shape[1] // LANES))


def sign(i):
    return 1 - 2 * (i % 2)


def beside(i):
    return sign(i) * (1 - i // 2), sign(i) * (i // 2)


def across_ring(i):
    return 2 * (1 - i), 2 * i


def corner(i):
    return sign(i), 1 - 2 * (i // 2)


def knight(i):
    along = i // 2
    return sign(i) * (1 - along) + 2 * along, 2 * (1 - along) + sign(i) * along


def single(dx, dy):
    return lambda i: (dx, dy)


def mixer_kernel(
    mixer_ref, gate_ref, delta_ref, b_ref, c_ref, taps_ref, bias_ref, delta_bias_ref, decay_ref,
    gain_ref, prefix_ref, tail_ref, weight_ref, residual_ref,
    out_ref, squares_ref,
    rim, padded, act, step, drive, summed, b_wide, c_wide, ends, spans, line_ends, line_spans,
    rows_all, weight, parts, got, landed, home,
    rim_sems, end_sems, gather_sems, pair_sems, sum_send_sems, sum_sems, weight_sem,
):
    torus = Torus()
    me, index = torus.me, torus.index
    x, y = torus.place
    own = lax.axis_index("exp")
    z, core = own // 2, own % 2
    count = SIDE * SIDE
    tokens, channels = mixer_ref.shape
    strips = channels // STRIP
    f32 = jnp.float32

    def strip_lanes(strip):
        return pl.ds(strip * STRIP if isinstance(strip, int) else pl.multiple_of(strip * STRIP, STRIP), STRIP)

    load = pltpu.make_async_copy(weight_ref, weight, weight_sem)
    load.start()
    barrier = pltpu.get_barrier_semaphore()
    for k in range(1, count):
        pl.semaphore_signal(
            barrier, inc=1, device_id={"ctx": lax.rem(me + k, count)}, device_id_type=MESH
        )
    for k in range(1, EXPERTS):
        pl.semaphore_signal(
            barrier, inc=1, device_id={"exp": lax.rem(own + k, EXPERTS)}, device_id_type=MESH
        )
    for t in range(tokens):
        b_wide[t] = jnp.broadcast_to(b_ref[:, t : t + 1], (STATES, LANES))
        c_wide[t] = jnp.broadcast_to(c_ref[:, t : t + 1], (STATES, LANES))

    pl.semaphore_wait(barrier, count - 1 + EXPERTS - 1)

    def rim_copy(target):
        return pltpu.make_async_remote_copy(
            src_ref=mixer_ref.at[pl.ds(tokens - 16, 16), :],
            dst_ref=rim,
            send_sem=rim_sems.at[0],
            recv_sem=rim_sems.at[1],
            device_id={"ctx": target},
            device_id_type=MESH,
        )

    @pl.when(me < count - 1)
    def _():
        rim_copy(me + 1).start()

    def find_step(strip, carry):
        lanes = strip_lanes(strip)
        value = jnp.log(1.0 + jnp.exp(delta_ref[:, lanes].astype(f32) + delta_bias_ref[:, lanes]))
        step[:, lanes] = value
        spans[0, :, lanes] = jnp.sum(value, axis=0, keepdims=True)
        return carry

    lax.fori_loop(0, strips, find_step, 0)

    @pl.when(me > 0)
    def _():
        rim_copy(me).wait_recv()

    @pl.when(me == 0)
    def _():
        rim[...] = jnp.zeros_like(rim)

    def rates(lanes):
        return -jnp.exp(decay_ref[:, lanes]) * LOG2E

    def advance(rate, state, steps, drives, i, b_column):
        return tuple(
            jnp.exp2(r * s) * h + b_column * d
            for r, s, h, d in zip(
                rate, lane_parts(steps[i : i + 1]), state, lane_parts(drives[i : i + 1])
            )
        )

    def prepare(strip):
        lanes = strip_lanes(strip)
        padded[0:8] = rim[:, lanes].astype(f32)[8:16]
        padded[8 : 8 + tokens] = mixer_ref[:, lanes].astype(f32)

        @pl.when(me == 0)
        def _():
            padded[5:8] = tail_ref[:, lanes].astype(f32)

        convolved = bias_ref[:, lanes]
        for k in range(4):
            convolved = convolved + taps_ref[k : k + 1, lanes] * padded[5 + k : 5 + k + tokens]
        value = convolved / (1.0 + jnp.exp(-convolved))
        act[:, lanes] = value
        drive[:, lanes] = value * step[:, lanes]
        rate = lane_parts(rates(lanes))

        def group(number, state):
            base = pl.multiple_of(number * 8, 8)
            steps, drives = step[pl.ds(base, 8), lanes], drive[pl.ds(base, 8), lanes]
            for i in range(8):
                state = advance(rate, state, steps, drives, i, b_wide[base + i])
            return state

        zero = jnp.zeros((STATES, LANES), f32)
        state = lax.fori_loop(0, tokens // 8, group, (zero,) * (STRIP // LANES))
        ends[0, :, lanes] = jnp.concatenate(state, axis=1).astype(ends.dtype)

    def end_copies(stage, strip, k, place, target):
        lanes = strip_lanes(strip)
        pairs = ((ends, line_ends), (spans, line_spans))
        return [
            pltpu.make_async_remote_copy(
                src_ref=mine.at[stage, :, lanes],
                dst_ref=whole.at[stage, place, :, lanes],
                send_sem=end_sems.at[0, stage, strip, k - 1, part],
                recv_sem=end_sems.at[1, stage, strip, k - 1, part],
                device_id={"ctx": target},
                device_id_type=MESH,
            )
            for part, (mine, whole) in enumerate(pairs)
        ]

    def follow(stage, strip):
        lanes = strip_lanes(strip)

        def one(source, state):
            return (
                jnp.exp2(rates(lanes) * line_spans[stage, source, :, lanes]) * state
                + line_ends[stage, source, :, lanes].astype(f32)
            )

        return one

    leaving = []

    def open_strip(strip):
        prepare(strip)
        for k in range(1, SIDE):
            for one in end_copies(0, strip, k, y, index(0, 0, k)):
                one.start()
                leaving.append(one)
        lanes = strip_lanes(strip)
        line_ends[0, y, :, lanes] = ends[0, :, lanes]
        line_spans[0, y, :, lanes] = spans[0, :, lanes]

    def close_line(strip):
        for k in range(1, SIDE):
            for one in end_copies(0, strip, k, lax.rem(y + SIDE - k, SIDE), me):
                one.wait_recv()
        lanes = strip_lanes(strip)
        state = lax.fori_loop(0, SIDE, follow(0, strip), jnp.zeros((STATES, STRIP), f32))
        ends[1, :, lanes] = state.astype(ends.dtype)
        spans[1, :, lanes] = sum(line_spans[0, source, :, lanes] for source in range(SIDE))
        for k in range(1, SIDE):

            @pl.when(x + k < SIDE)
            def _():
                for one in end_copies(1, strip, k, x, (x + k) * SIDE + y):
                    one.start()

    in_flight = []

    def moved(strip, line, kind, first, second, part, towards, target):
        half = strip % 2

        def rows(a, b):
            where = (a, b) if half == 0 else (b, a)
            where = tuple((v + 1) % SIDE - 1 for v in where)
            start, size = (0, tokens) if part is None else (part * (tokens // 2), tokens // 2)
            return rows_all.at[strip, pl.ds(SLOTS.index(where) * tokens + start, size), :]

        return pltpu.make_async_remote_copy(
            src_ref=rows(first, second),
            dst_ref=rows(first - towards[0], second - towards[1]),
            send_sem=gather_sems.at[0, strip, line, kind],
            recv_sem=gather_sems.at[1, strip, line, kind],
            device_id={"ctx": target},
            device_id_type=MESH,
        )

    def send(strip, line, kind, first, second, part, towards):
        target = index(strip % 2, *towards)
        one = moved(strip, line, kind, first, second, part, towards, target)
        one.start()
        in_flight.append(one)

    def arrived(strip, line, kind, first, second, part):
        moved(strip, line, kind, first, second, part, (0, 0), me).wait_recv()

    def send_line(strip, first):
        send(strip, LINES[first], 0, first, 0, None, (0, 1))
        send(strip, LINES[first], 1, first, 0, None, (0, -1))

    def pass_on(strip, first):
        arrived(strip, LINES[first], 0, first, -1, None)
        send(strip, LINES[first], 2, first, -1, 0, (0, 1))
        arrived(strip, LINES[first], 1, first, 1, None)
        send(strip, LINES[first], 3, first, 1, 1, (0, -1))

    def last_of(strip, first):
        arrived(strip, LINES[first], 2, first, 2, 0)
        arrived(strip, LINES[first], 3, first, 2, 1)

    def ring_one(strip):
        arrived(strip, RING, 0, -1, 0, None)
        send(strip, RING, 2, -1, 0, 0, (1, 0))
        arrived(strip, RING, 1, 1, 0, None)
        send(strip, RING, 3, 1, 0, 1, (-1, 0))
        send_line(strip, -1)
        send_line(strip, 1)
        pass_on(strip, 0)

    def ring_two(strip):
        arrived(strip, RING, 2, 2, 0, 0)
        arrived(strip, RING, 3, 2, 0, 1)
        send_line(strip, 2)
        last_of(strip, 0)

    def lines_one(strip):
        pass_on(strip, -1)
        pass_on(strip, 1)

    def lines_two(strip):
        pass_on(strip, 2)
        last_of(strip, -1)
        last_of(strip, 1)

    def scan(strip):
        for k in range(1, SIDE):

            @pl.when(x >= k)
            def _():
                for one in end_copies(1, strip, k, x - k, me):
                    one.wait_recv()

        lanes = strip_lanes(strip)
        rate = lane_parts(rates(lanes))
        state = prefix_ref[:, lanes]
        state = lax.fori_loop(0, x, follow(1, strip), state)
        state = lax.fori_loop(0, y, follow(0, strip), state)

        def group(number, state):
            base = pl.multiple_of(number * 8, 8)
            steps, drives = step[pl.ds(base, 8), lanes], drive[pl.ds(base, 8), lanes]
            found = []
            for i in range(8):
                state = advance(rate, state, steps, drives, i, b_wide[base + i])
                c_column = c_wide[base + i]
                found.append(
                    jnp.concatenate(
                        [jnp.sum(c_column * h, axis=0, keepdims=True) for h in state], axis=1
                    )
                )
            summed[pl.ds(base, 8), :] = jnp.concatenate(found, axis=0)
            return state

        lax.fori_loop(0, tokens // 8, group, lane_parts(state))
        gate = gate_ref[:, lanes].astype(f32)
        mixed = summed[...] + gain_ref[:, lanes] * act[:, lanes]
        rows_all[strip, 0:tokens, :] = (mixed * (gate / (1.0 + jnp.exp(-gate)))).astype(
            rows_all.dtype
        )
        send(strip, RING, 0, 0, 0, None, (1, 0))
        send(strip, RING, 1, 0, 0, None, (-1, 0))
        send_line(strip, 0)

    open_strip(0)
    for strip in range(1, strips):
        open_strip(strip)
        close_line(strip - 1)
    scan(0)
    close_line(strips - 1)
    for strip in range(1, strips - 1):
        scan(strip)
    ring_one(0)
    scan(strips - 1)
    for strip in range(1, strips):
        ring_one(strip)

    width = weight.shape[1]
    sibling = own + 1 - 2 * core

    def of_slot(where, number):
        dx, dy = where(number)
        line = lax.rem(y + dy + SIDE, SIDE)
        return lax.rem(x + dx + SIDE, SIDE), line // 2, line % 2

    def pair_copy(slot, target):
        return pltpu.make_async_remote_copy(
            src_ref=parts.at[slot],
            dst_ref=got.at[slot],
            send_sem=pair_sems.at[0, slot],
            recv_sem=pair_sems.at[1, slot],
            device_id={"exp": target},
            device_id_type=MESH,
        )

    def part_rows(part):
        return pl.ds(pl.multiple_of(part * tokens, tokens), tokens)

    def sum_copy(slot, column, part):
        behind = lax.rem(column - z + SIDE, SIDE) - 1
        return pltpu.make_async_remote_copy(
            src_ref=parts.at[slot],
            dst_ref=landed.at[behind, part_rows(part), :],
            send_sem=sum_send_sems.at[slot],
            recv_sem=sum_sems.at[behind, part],
            device_id={"exp": column * 2 + core},
            device_id_type=MESH,
        )

    def project(where, number, first_slot):
        together = min(number, 2)

        def one(pair, carry):
            first = first_slot + pair * together
            rows = pl.ds(pl.multiple_of(first * tokens, tokens), together * tokens)
            value = sum(
                jnp.dot(
                    rows_all[strip, rows, :],
                    weight[strip * STRIP : (strip + 1) * STRIP],
                    preferred_element_type=f32,
                )
                for strip in range(strips)
            )
            for k in range(together):
                column, owner, part = of_slot(where, pair * together + k)
                parts[first + k] = value[k * tokens : (k + 1) * tokens].astype(parts.dtype)

                @pl.when(owner != core)
                def _():
                    pair_copy(first + k, sibling).start()

            return carry

        lax.fori_loop(0, number // together, one, 0)

    def settle(where, number, first_slot):
        def one(k, carry):
            slot = first_slot + k
            column, owner, part = of_slot(where, k)

            @pl.when(owner == core)
            def _():
                pair_copy(slot, own).wait_recv()
                value = parts[slot].astype(f32) + got[slot].astype(f32)

                @pl.when(column == z)
                def _():
                    home[part_rows(part), :] = value

                @pl.when(column != z)
                def _():
                    parts[slot] = value.astype(parts.dtype)
                    sum_copy(slot, column, part).start()

            return carry

        lax.fori_loop(0, number, one, 0)

    def clear(where, number, first_slot):
        def one(k, carry):
            slot = first_slot + k
            column, owner, part = of_slot(where, k)

            @pl.when(owner != core)
            def _():
                pair_copy(slot, sibling).wait_send()

            @pl.when((owner == core) & (column != z))
            def _():
                sum_copy(slot, column, part).wait_send()

            return carry

        lax.fori_loop(0, number, one, 0)

    load.wait()
    project(single(0, 0), 1, 0)
    project(beside, 4, 1)
    settle(single(0, 0), 1, 0)
    for strip in range(strips):
        ring_two(strip)
    project(across_ring, 2, 5)
    settle(beside, 4, 1)
    for strip in range(strips):
        lines_one(strip)
    project(corner, 4, 7)
    settle(across_ring, 2, 5)
    for strip in range(strips):
        lines_two(strip)
    project(knight, 4, 11)
    settle(corner, 4, 7)
    for strip in range(strips):
        last_of(strip, 2)
    project(single(2, 2), 1, 15)
    settle(knight, 4, 11)
    settle(single(2, 2), 1, 15)
    value = home[...] + residual_ref[...].astype(f32)
    for behind in range(SIDE - 1):
        for part in (0, 1):
            rows = pl.ds(part * tokens, tokens)
            pltpu.make_async_remote_copy(
                src_ref=landed.at[behind, rows, :],
                dst_ref=landed.at[behind, rows, :],
                send_sem=sum_send_sems.at[0],
                recv_sem=sum_sems.at[behind, part],
                device_id={"exp": own},
                device_id_type=MESH,
            ).wait_recv()
        value = value + landed[behind].astype(f32)
    value = value.astype(out_ref.dtype)
    out_ref[...] = value
    value = value.astype(f32)
    value = value * value
    ones = jnp.ones((16, width), jnp.bfloat16)
    found = jnp.zeros((16, value.shape[0]), f32)
    for _ in range(3):
        term = value.astype(jnp.bfloat16)
        value = value - term.astype(f32)
        found = found + lax.dot_general(
            ones, term, (((1,), (1,)), ((), ())), preferred_element_type=f32
        )
    squares_ref[...] = found[0:8]

    @pl.when(me < count - 1)
    def _():
        rim_copy(me + 1).wait_send()

    for strip in range(strips):
        for k in range(1, SIDE):

            @pl.when(x + k < SIDE)
            def _():
                for one in end_copies(1, strip, k, x, (x + k) * SIDE + y):
                    one.wait_send()

    clear(single(0, 0), 1, 0)
    clear(beside, 4, 1)
    clear(across_ring, 2, 5)
    clear(corner, 4, 7)
    clear(knight, 4, 11)
    clear(single(2, 2), 1, 15)
    for one in in_flight + leaving:
        one.wait_send()


def mixer(
    mixer_in, gate_in, delta_in, b_proj, c_proj, conv_kernel, conv_bias, delta_bias, decay_log,
    skip_gain, prefix_state, prefix_tail, out_proj, residual,
):
    tokens, channels = mixer_in.shape
    rows, width = residual.shape
    count = SIDE * SIDE
    here = pl.BlockSpec(memory_space=pltpu.VMEM)
    away = pl.BlockSpec(memory_space=pl.ANY)
    bf16, f32 = jnp.bfloat16, jnp.float32
    return pl.pallas_call(
        mixer_kernel,
        out_shape=(
            jax.ShapeDtypeStruct((rows, width), bf16),
            jax.ShapeDtypeStruct((8, rows), f32),
        ),
        in_specs=[here] * 12 + [away, here],
        out_specs=(here, here),
        scratch_shapes=[
            pltpu.VMEM((16, channels), bf16),
            pltpu.VMEM((8 + tokens, STRIP), f32),
            pltpu.VMEM((tokens, channels), f32),
            pltpu.VMEM((tokens, channels), f32),
            pltpu.VMEM((tokens, channels), f32),
            pltpu.VMEM((tokens, STRIP), f32),
            pltpu.VMEM((tokens, STATES, LANES), f32),
            pltpu.VMEM((tokens, STATES, LANES), f32),
            pltpu.VMEM((2, STATES, channels), bf16),
            pltpu.VMEM((2, 1, channels), f32),
            pltpu.VMEM((2, SIDE, STATES, channels), bf16),
            pltpu.VMEM((2, SIDE, 1, channels), f32),
            pltpu.VMEM((channels // STRIP, count * tokens, STRIP), bf16),
            pltpu.VMEM((channels, width), bf16),
            pltpu.VMEM((count, tokens, width), bf16),
            pltpu.VMEM((count, tokens, width), bf16),
            pltpu.VMEM((SIDE - 1, rows, width), bf16),
            pltpu.VMEM((rows, width), f32),
            pltpu.SemaphoreType.DMA((2,)),
            pltpu.SemaphoreType.DMA((2, 2, channels // STRIP, SIDE - 1, 2)),
            pltpu.SemaphoreType.DMA((2, channels // STRIP, 5, 4)),
            pltpu.SemaphoreType.DMA((2, count)),
            pltpu.SemaphoreType.DMA((count,)),
            pltpu.SemaphoreType.DMA((SIDE - 1, 2)),
            pltpu.SemaphoreType.DMA,
        ],
        compiler_params=pltpu.CompilerParams(
            collective_id=1, has_side_effects=True, vmem_limit_bytes=56 * 1024 * 1024
        ),
        name="mixer",
    )(
        mixer_in, gate_in, delta_in, b_proj, c_proj, conv_kernel, conv_bias[None], delta_bias[None],
        decay_log, skip_gain[None], prefix_state, prefix_tail, out_proj, residual,
    )


def expert_kernel(
    capacity, features,
    mixer_ref, squares_ref, ids_ref, route_ref, gain_ref, gate_ref, up_ref, down_ref,
    out_ref,
    blocks, landed, wide, down, total, hidden, outgoing, answer, returned, all_squares, pick_all, routing, scales_out, scales,
    square_sems, scale_sems, dispatch_sems, return_sems, gather_sems, sum_sems, weight_sems,
):
    torus = Torus()
    me, index = torus.me, torus.index
    own_expert = lax.axis_index("exp")
    slots, width = answer.shape
    units = down.shape[0]
    count = SIDE * SIDE

    weights = [
        pltpu.make_async_copy(gate_ref.at[0], wide.at[:, pl.ds(0, units)], weight_sems.at[0]),
        pltpu.make_async_copy(up_ref.at[0], wide.at[:, pl.ds(units, units)], weight_sems.at[1]),
        pltpu.make_async_copy(down_ref.at[0], down, weight_sems.at[2]),
    ]
    for one in weights:
        one.start()

    barrier = pltpu.get_barrier_semaphore()
    for k in range(1, count):
        pl.semaphore_signal(
            barrier, inc=1, device_id={"ctx": lax.rem(me + k, count)}, device_id_type=MESH
        )
    for k in range(1, EXPERTS):
        pl.semaphore_signal(
            barrier, inc=1, device_id={"exp": lax.rem(own_expert + k, EXPERTS)}, device_id_type=MESH
        )

    tokens = mixer_ref.shape[0]
    z, core = own_expert // 2, own_expert % 2

    def at_peer(number, way):
        dz, dc = PEERS[number]
        other = core + dc - 2 * core * dc
        return lax.rem(z + way * dz + 2 * SIDE, SIDE) * 2 + other

    experts_wide = lax.broadcasted_iota(jnp.int32, (16, tokens), 0)
    named, gates_wide = jnp.zeros((16, tokens), jnp.float32), jnp.zeros((16, tokens), jnp.float32)
    for k in range(ids_ref.shape[0]):
        here = ids_ref[k : k + 1, :] == experts_wide
        named = jnp.where(here, 1.0, named)
        gates_wide = jnp.where(here, route_ref[k : k + 1, :], gates_wide)
    before = lax.broadcasted_iota(jnp.int32, (tokens, tokens), 0)
    after = lax.broadcasted_iota(jnp.int32, (tokens, tokens), 1)
    routing[0] = named[0:EXPERTS]
    routing[1] = jnp.dot(
        named.astype(jnp.bfloat16),
        (before < after).astype(jnp.float32).astype(jnp.bfloat16),
        preferred_element_type=jnp.float32,
    )[0:EXPERTS]
    first = lax.broadcasted_iota(jnp.int32, (16, LANES), 0)
    second = lax.broadcasted_iota(jnp.int32, (16, LANES), 1)
    turn = (first == second).astype(jnp.float32).astype(jnp.bfloat16)
    gates = jnp.zeros((tokens, LANES), jnp.float32)
    for _ in range(3):
        term = gates_wide.astype(jnp.bfloat16)
        gates_wide = gates_wide - term.astype(jnp.float32)
        gates = gates + lax.dot_general(
            term, turn, (((0,), (0,)), ((), ())), preferred_element_type=jnp.float32
        )

    for number in range(len(PEERS)):
        expert = pl.ds(at_peer(number, 1), 1)
        slot = lax.broadcasted_iota(jnp.int32, (capacity, tokens), 0).astype(jnp.float32)
        chosen = (routing[1, expert, :] == slot) & (routing[0, expert, :] > 0.5)
        rows = pl.ds(number * capacity, capacity)
        pick_all[rows, :] = chosen.astype(jnp.float32).astype(jnp.bfloat16)
        picked = jnp.dot(pick_all[rows, :], mixer_ref[...], preferred_element_type=jnp.float32)
        outgoing[rows, :] = (picked * gain_ref[...]).astype(outgoing.dtype)
    pl.semaphore_wait(barrier, count - 1 + EXPERTS - 1)

    square_copies = []
    for k in range(1, count):
        square_copies.append(
            pltpu.make_async_remote_copy(
                src_ref=squares_ref,
                dst_ref=all_squares.at[me],
                send_sem=square_sems.at[0, k - 1],
                recv_sem=square_sems.at[1, k - 1],
                device_id={"ctx": lax.rem(me + k, count)},
                device_id_type=MESH,
            )
        )
        square_copies[-1].start()

    def rows_of(number):
        return pl.ds(number * capacity, capacity)

    def dispatch(number, target):
        return pltpu.make_async_remote_copy(
            src_ref=outgoing.at[rows_of(number), :],
            dst_ref=blocks.at[me, rows_of(number), :],
            send_sem=dispatch_sems.at[0, number],
            recv_sem=dispatch_sems.at[1, number],
            device_id={"exp": target},
            device_id_type=MESH,
        )

    crossing = [dispatch(n, at_peer(n, 1)) for n in range(1, len(PEERS))]
    for one in crossing:
        one.start()
    blocks[me, rows_of(OWN), :] = outgoing[rows_of(OWN), :]

    def scale_copy(number, target):
        return pltpu.make_async_remote_copy(
            src_ref=scales_out.at[number],
            dst_ref=scales.at[number],
            send_sem=scale_sems.at[0, number],
            recv_sem=scale_sems.at[1, number],
            device_id={"exp": target},
            device_id_type=MESH,
        )

    def send_scales():
        all_squares[me] = squares_ref[...]
        for k in range(1, count):
            source = lax.rem(me + count - k, count)
            pltpu.make_async_remote_copy(
                src_ref=squares_ref,
                dst_ref=all_squares.at[source],
                send_sem=square_sems.at[0, k - 1],
                recv_sem=square_sems.at[1, k - 1],
                device_id={"ctx": me},
                device_id_type=MESH,
            ).wait_recv()
        scale = lax.rsqrt(jnp.sum(all_squares[...], axis=0)[0:1] / features + 1e-05)
        for number in range(len(PEERS)):
            chosen = pick_all[rows_of(number), :].astype(jnp.float32)
            row_scale = jnp.sum(chosen * scale, axis=1, keepdims=True)
            row_scale = jnp.broadcast_to(row_scale, (capacity, LANES))
            if number == OWN:
                scales[number] = row_scale
            else:
                scales_out[number] = row_scale
                one = scale_copy(number, at_peer(number, 1))
                one.start()
                crossing.append(one)

    in_flight = {}

    def moved(unit, line, kind, first, second, part, target):
        half = unit % 2
        start, size = span(slots, unit, part)
        ref = blocks.at[index(half, first, second), pl.ds(start, size), :]
        return pltpu.make_async_remote_copy(
            src_ref=ref,
            dst_ref=ref,
            send_sem=gather_sems.at[0, unit, line, kind],
            recv_sem=gather_sems.at[1, unit, line, kind],
            device_id={"ctx": target},
            device_id_type=MESH,
        )

    def send(unit, line, kind, first, second, part, towards):
        one = moved(unit, line, kind, first, second, part, index(unit % 2, *towards))
        one.start()
        where = (first, second) if unit % 2 == 0 else (second, first)
        in_flight.setdefault((unit // 2,) + where, []).append(one)

    def arrived(unit, line, kind, first, second, part):
        moved(unit, line, kind, first, second, part, me).wait_recv()

    def send_line(unit, first):
        send(unit, LINES[first], 0, first, 0, None, (0, 1))
        send(unit, LINES[first], 1, first, 0, None, (0, -1))

    def pass_on(unit, first):
        arrived(unit, LINES[first], 0, first, -1, None)
        send(unit, LINES[first], 2, first, -1, 0, (0, 1))
        arrived(unit, LINES[first], 1, first, 1, None)
        send(unit, LINES[first], 3, first, 1, 1, (0, -1))

    def last_of(unit, first):
        arrived(unit, LINES[first], 2, first, 2, 0)
        arrived(unit, LINES[first], 3, first, 2, 1)

    def open_unit(unit):
        for number in (2 * unit, 2 * unit + 1):
            if number != OWN:
                dispatch(number, own_expert).wait_recv()
        send(unit, RING, 0, 0, 0, None, (1, 0))
        send(unit, RING, 1, 0, 0, None, (-1, 0))
        send_line(unit, 0)

    def ring_one(unit):
        arrived(unit, RING, 0, -1, 0, None)
        send(unit, RING, 2, -1, 0, 0, (1, 0))
        arrived(unit, RING, 1, 1, 0, None)
        send(unit, RING, 3, 1, 0, 1, (-1, 0))
        send_line(unit, -1)
        send_line(unit, 1)
        pass_on(unit, 0)

    def ring_two(unit):
        arrived(unit, RING, 2, 2, 0, 0)
        arrived(unit, RING, 3, 2, 0, 1)
        send_line(unit, 2)
        last_of(unit, 0)

    def lines_one(unit):
        pass_on(unit, -1)
        pass_on(unit, 1)

    def lines_two(unit):
        pass_on(unit, 2)
        last_of(unit, -1)
        last_of(unit, 1)

    row_tile = slots // 2

    def over_blocks(group, where, number, body):
        rows = pl.ds(group * row_tile, row_tile)

        def one(block, carry):
            body(index(0, *where(block)), rows)
            return carry

        lax.fori_loop(0, number, one, 0)

    def grow(owner, rows):
        part = wide[pl.ds(pl.multiple_of(owner * width, 16), width), :]
        total[rows, :] += jnp.dot(blocks[owner, rows, :], part, preferred_element_type=jnp.float32)

    def activate(group):
        together = len(PEERS) // 2
        for number in range(group * together, (group + 1) * together):
            if number != OWN:
                scale_copy(number, own_expert).wait_recv()

        def one(step, carry):
            number = group * together + step
            rows = pl.ds(pl.multiple_of(number * capacity, 16), capacity)
            scale = jnp.concatenate([scales[number]] * (units // LANES), axis=1)
            gate = total[rows, 0:units] * scale
            up = total[rows, units : 2 * units] * scale
            hidden[rows, :] = (gate / (1.0 + jnp.exp(-gate)) * up).astype(hidden.dtype)
            return carry

        lax.fori_loop(0, together, one, 0)

    def project(owner, rows):
        part = down[:, pl.ds(pl.multiple_of(owner * width, LANES), width)]
        blocks[owner, rows, :] = jnp.dot(
            hidden[rows, :], part, preferred_element_type=jnp.float32
        ).astype(blocks.dtype)

    def fill(group, where, number):
        for block in range(number):
            for one in in_flight.pop((group,) + where(block), ()):
                one.wait_send()
        over_blocks(group, where, number, project)

    summing = []

    def part_rows(unit, part):
        start, size = span(slots, unit, part)
        return pl.ds(start, size)

    def landing(unit, line, kind):
        if kind < 2:
            return landed.at[unit, line, kind]
        size = span(slots, unit, 0)[1]
        return landed.at[unit, line, 2, pl.ds((kind - 2) * size, size), :]

    def sum_copy(unit, line, kind, first, second, part, target):
        return pltpu.make_async_remote_copy(
            src_ref=blocks.at[index(unit % 2, first, second), part_rows(unit, part), :],
            dst_ref=landing(unit, line, kind),
            send_sem=sum_sems.at[0, unit, line, kind],
            recv_sem=sum_sems.at[1, unit, line, kind],
            device_id={"ctx": target},
            device_id_type=MESH,
        )

    def give(unit, line, kind, first, second, part):
        step = 1 if kind % 2 == 0 else -1
        half = unit % 2
        target = index(half, step, 0) if line == RING else index(half, 0, step)
        one = sum_copy(unit, line, kind, first, second, part, target)
        one.start()
        summing.append(one)

    def taken(unit, line, kind):
        part = None if kind < 2 else kind - 2
        sum_copy(unit, line, kind, 0, 0, part, me).wait_recv()

    def add(unit, first, second, part, line, kinds):
        for kind in kinds:
            taken(unit, line, kind)
        owner = index(unit % 2, first, second)
        start, size = span(slots, unit, part)

        def one(step, carry):
            offset = pl.multiple_of(step * capacity, 16)
            rows = pl.ds(pl.multiple_of(start + offset, 16), capacity)
            value = blocks[owner, rows, :].astype(jnp.float32)
            for kind in kinds:
                value = value + landing(unit, line, kind)[pl.ds(offset, capacity), :].astype(
                    jnp.float32
                )
            blocks[owner, rows, :] = value.astype(blocks.dtype)
            return carry

        lax.fori_loop(0, size // capacity, one, 0)

    def at(line, offset):
        return (offset, 0) if line == RING else ({v: k for k, v in LINES.items()}[line], offset)

    def begin(unit, line):
        give(unit, line, 2, *at(line, 2), 0)
        give(unit, line, 3, *at(line, 2), 1)

    def middle(unit, line):
        add(unit, *at(line, 1), 0, line, (2,))
        give(unit, line, 0, *at(line, 1), None)
        add(unit, *at(line, -1), 1, line, (3,))
        give(unit, line, 1, *at(line, -1), None)

    def finish(unit, line):
        add(unit, *at(line, 0), None, line, (0, 1))

    def back(number, target):
        return pltpu.make_async_remote_copy(
            src_ref=answer.at[rows_of(number), :],
            dst_ref=returned.at[rows_of(number), :],
            send_sem=return_sems.at[0, number],
            recv_sem=return_sems.at[1, number],
            device_id={"exp": target},
            device_id_type=MESH,
        )

    def hand_back(unit):
        for kind in (0, 1):
            taken(unit, RING, kind)
        owner = index(0, 0, 0)
        for step in (0, 1):
            number = 2 * unit + step
            rows = rows_of(number)
            there = pl.ds(step * capacity, capacity)
            value = blocks[owner, rows, :].astype(jnp.float32)
            for kind in (0, 1):
                value = value + landed[unit, RING, kind, there, :].astype(jnp.float32)
            if number == OWN:
                returned[rows, :] = value.astype(returned.dtype)
            else:
                answer[rows, :] = value.astype(answer.dtype)
                one = back(number, at_peer(number, -1))
                one.start()
                summing.append(one)

    def both(group, step, *where):
        for unit in (2 * group, 2 * group + 1):
            step(unit, *where)

    def finish_lines(group):
        fill(group, single(0, 0), 1)
        for unit in (2 * group, 2 * group + 1):
            finish(unit, LINES[2])
            begin(unit, RING)
        for first in (1, -1):
            both(group, finish, LINES[first])
        both(group, middle, RING)
        both(group, finish, LINES[0])

    for unit in UNITS:
        open_unit(unit)
    send_scales()
    both(0, ring_one)
    both(1, ring_one)
    total[...] = jnp.zeros_like(total)
    for one in weights:
        one.wait()
    over_blocks(0, single(0, 0), 1, grow)
    over_blocks(0, beside, 4, grow)
    both(0, ring_two)
    both(0, lines_one)
    both(1, ring_two)
    over_blocks(0, across_ring, 2, grow)
    over_blocks(1, single(0, 0), 1, grow)
    both(0, lines_two)
    both(1, lines_one)
    over_blocks(0, corner, 4, grow)
    over_blocks(1, beside, 4, grow)
    both(0, last_of, 2)
    over_blocks(0, knight, 4, grow)
    over_blocks(0, single(2, 2), 1, grow)
    activate(0)
    fill(0, single(2, 2), 1)
    both(0, begin, LINES[2])
    both(1, lines_two)
    fill(0, knight, 4)
    both(0, begin, LINES[1])
    both(0, begin, LINES[-1])
    fill(0, across_ring, 2)
    both(0, begin, LINES[0])
    over_blocks(1, across_ring, 2, grow)
    over_blocks(1, corner, 4, grow)
    both(0, middle, LINES[2])
    both(1, last_of, 2)
    fill(0, corner, 4)
    both(0, middle, LINES[1])
    both(0, middle, LINES[-1])
    over_blocks(1, knight, 4, grow)
    over_blocks(1, single(2, 2), 1, grow)
    activate(1)
    fill(0, beside, 4)
    both(0, middle, LINES[0])
    for one in crossing:
        one.wait_send()
    fill(1, single(2, 2), 1)
    both(1, begin, LINES[2])
    fill(1, knight, 4)
    both(1, begin, LINES[1])
    both(1, begin, LINES[-1])
    fill(1, across_ring, 2)
    both(1, begin, LINES[0])
    finish_lines(0)
    both(1, middle, LINES[2])
    fill(1, corner, 4)
    both(1, middle, LINES[1])
    both(1, middle, LINES[-1])
    fill(1, beside, 4)
    both(1, middle, LINES[0])
    both(0, hand_back)
    lane = lax.broadcasted_iota(jnp.int32, (tokens, LANES), 1)

    def mixed(number):
        rows = rows_of(number)
        gate = jnp.sum(jnp.where(lane == at_peer(number, 1), gates, 0.0), axis=1, keepdims=True)
        return gate * lax.dot_general(
            pick_all[rows, :],
            returned[rows, :],
            (((0,), (0,)), ((), ())),
            preferred_element_type=jnp.float32,
        )

    finish_lines(1)
    value = mixer_ref[...].astype(jnp.float32) + mixed(OWN)
    for number in range(1, len(PEERS)):
        if number == len(PEERS) // 2:
            both(1, hand_back)
        back(number, own_expert).wait_recv()
        value = value + mixed(number)
    out_ref[...] = value.astype(out_ref.dtype)
    for one in summing + square_copies:
        one.wait_send()


def expert_layer(
    mixer_out, squares, ids, route_gates, gain, expert_gate, expert_up, expert_down, capacity
):
    rows, width = mixer_out.shape
    features, units = expert_gate.shape[1:]
    slots = EXPERTS * capacity
    count = SIDE * SIDE
    here = pl.BlockSpec(memory_space=pltpu.VMEM)
    away = pl.BlockSpec(memory_space=pl.ANY)
    bf16, f32 = jnp.bfloat16, jnp.float32
    return pl.pallas_call(
        functools.partial(expert_kernel, capacity, features),
        out_shape=jax.ShapeDtypeStruct((rows, width), bf16),
        in_specs=[here] * 5 + [away] * 3,
        out_specs=here,
        scratch_shapes=[
            pltpu.VMEM((count, slots, width), bf16),
            pltpu.VMEM((len(UNITS), 5, 3, slots // len(UNITS), width), bf16),
            pltpu.VMEM((features, 2 * units), bf16),
            pltpu.VMEM((units, features), bf16),
            pltpu.VMEM((slots, 2 * units), f32),
            pltpu.VMEM((slots, units), bf16),
            pltpu.VMEM((slots, width), bf16),
            pltpu.VMEM((slots, width), bf16),
            pltpu.VMEM((slots, width), bf16),
            pltpu.VMEM((count,) + squares.shape, f32),
            pltpu.VMEM((slots, rows), bf16),
            pltpu.VMEM((2, EXPERTS, rows), f32),
            pltpu.VMEM((EXPERTS, capacity, LANES), f32),
            pltpu.VMEM((EXPERTS, capacity, LANES), f32),
            pltpu.SemaphoreType.DMA((2, count - 1)),
            pltpu.SemaphoreType.DMA((2, EXPERTS)),
            pltpu.SemaphoreType.DMA((2, EXPERTS)),
            pltpu.SemaphoreType.DMA((2, EXPERTS)),
            pltpu.SemaphoreType.DMA((2, len(UNITS), 5, 4)),
            pltpu.SemaphoreType.DMA((2, len(UNITS), 5, 4)),
            pltpu.SemaphoreType.DMA((3,)),
        ],
        compiler_params=pltpu.CompilerParams(
            collective_id=3, has_side_effects=True, vmem_limit_bytes=56 * 1024 * 1024
        ),
        name="expert_layer",
    )(mixer_out, squares, ids, route_gates, gain, expert_gate, expert_up, expert_down)


def shards(
    mixer_in,
    gate_in,
    delta_in,
    b_proj,
    c_proj,
    conv_kernel,
    conv_bias,
    delta_bias,
    decay_log,
    skip_gain,
    prefix_state,
    prefix_tail,
    out_proj,
    residual,
    norm_gain,
    expert_gate,
    expert_up,
    expert_down,
    expert_ids,
    route_gates,
):
    mixer_out, squares = mixer(
        mixer_in, gate_in, delta_in, b_proj, c_proj, conv_kernel, conv_bias, delta_bias, decay_log,
        skip_gain, prefix_state, prefix_tail, out_proj, residual,
    )
    block_rows = residual.shape[0]
    experts = expert_gate.shape[0] * lax.axis_size("exp")
    top_count = expert_ids.shape[1]
    capacity = 3 * block_rows * top_count // (2 * experts)
    block_out = expert_layer(
        mixer_out, squares, expert_ids.T, route_gates.T, norm_gain[None],
        expert_gate, expert_up, expert_down, capacity,
    )
    return (mixer_out, block_out)


def solution(mesh):
    placed = (
        P("ctx", "exp"),
        P("ctx", "exp"),
        P("ctx", "exp"),
        P(None, "ctx"),
        P(None, "ctx"),
        P(None, "exp"),
        P("exp"),
        P("exp"),
        P(None, "exp"),
        P("exp"),
        P(None, "exp"),
        P(None, "exp"),
        P("exp", "ctx"),
        P("exp", "ctx"),
        P("ctx"),
        P("exp", None, "ctx"),
        P("exp", None, "ctx"),
        P("exp", "ctx", None),
        P("exp", None),
        P("exp", None),
    )
    return jax.shard_map(
        shards,
        mesh=mesh,
        in_specs=placed,
        out_specs=(P("exp", "ctx"), P("exp", "ctx")),
        check_vma=False,
    )
```
